32 devices in a mesh: ap: 16 (over z, y, x), sc: 2 (over core).
Axes of the slice: x: 2, y: 2, z: 4, core: 2. Of those that a mesh axis runs over, the one named last changes fastest.
Arguments:
- covariances: float32 [512, 512], P('ap'), as said below
- clusters: int32 [512, 16], P('ap'), may hold values from 0 to 255, as said below
- cluster_valid: int32 [512, 16], P('ap'), may hold values 0 or 1
- pilots: int32 [512], P('ap'), may hold values from 0 to 15
- received_pilot: float32 [256, 16, 128], P('ap', 'sc'), may hold values from -9 to 9
- received_data: float32 [256, 16, 128], P('ap', 'sc'), may hold values from -18 to 18
Outputs:
- symbols_out: float32 [512, 16, 32], P('ap', 'sc')
- gain_out: float32 [512, 16], P('ap', 'sc')
The draws below stay inside these ranges and needn't reach their ends.
Inputs may be any that keep to these rules, and one draw needn't show every extreme that they name: `clusters`: the 16 ids in one user's row differ and lie on 16 different indices of ap (ids l with l // 16 = index); within the 32 users of one aligned block (the users of one device), the slots whose ids lie on one index of ap number exactly 32 for every index. `covariances`: each row-major 4 x 4 complex matrix is Hermitian positive definite.
All inputs are finite; a program needn't handle non-finite values. No bound on the sum of `cluster_valid` on one device may be relied on, other than what follows from the above.
Results may differ from the reference program's by a relative error of at most 0.00011.
Values sent between devices are 32-bit elements; how exact they have to be, the bound alone decides.
A program may use at most 64 MiB of HBM per device.

```python
import jax
import jax.numpy as jnp
from jax import lax

CLUSTER = 16
PILOT_SEQUENCES = 16
DATA_SYMBOLS = 16
AP_DEV = 16
USER_DEV = 32
APS = 256
USERS = 512
SUBC = 16


def draw_covariances(key, part):
    first = jax.random.fold_in(key, 11)
    second = jax.random.fold_in(key, 12)
    third = jax.random.fold_in(key, 13)
    array_shape = (USERS, CLUSTER, 4, 4)
    real_fac = jax.random.normal(first, array_shape, jnp.float32)
    imag_fac = jax.random.normal(second, array_shape, jnp.float32)
    scale_log = jax.random.uniform(third, (USERS, CLUSTER, 1, 1), jnp.float32, jnp.log(0.1), jnp.log(3.0))
    fading = jnp.exp(scale_log)
    real_cov = (jnp.einsum('ucij,uckj->ucik', real_fac, real_fac) + jnp.einsum('ucij,uckj->ucik', imag_fac, imag_fac)) / 4.0
    imag_cov = (jnp.einsum('ucij,uckj->ucik', imag_fac, real_fac) - jnp.einsum('ucij,uckj->ucik', real_fac, imag_fac)) / 4.0
    real_cov = fading * (real_cov + 0.3 * jnp.eye(4, dtype=jnp.float32))
    imag_cov = fading * imag_cov
    joined = jnp.concatenate([real_cov.reshape(USERS, CLUSTER, 16), imag_cov.reshape(USERS, CLUSTER, 16)], -1)
    return joined.reshape(USERS, CLUSTER * 32).astype(jnp.float32)


def draw_clusters(key, part):
    blocks = USERS // USER_DEV
    owners = APS // AP_DEV
    block_keys = jax.random.split(jax.random.fold_in(key, 21), blocks)
    orders = jax.vmap(lambda one_key: jax.random.permutation(one_key, owners))(block_keys)
    offsets = jax.random.randint(jax.random.fold_in(key, 22), (blocks, 1), 0, owners)
    places = jnp.arange(USER_DEV * CLUSTER, dtype=jnp.int32)[None, :]
    column = (places + offsets) % owners
    target = jnp.take_along_axis(orders, column, 1)
    within = jax.random.randint(jax.random.fold_in(key, 23), (blocks, USER_DEV * CLUSTER), 0, AP_DEV)
    chosen = target * AP_DEV + within
    return chosen.reshape(USERS, CLUSTER).astype(jnp.int32)


def with_ends(drawn, own_key, smallest, high):
    dims = drawn.shape
    index_at = [jax.random.randint(jax.random.fold_in(own_key, axis), (), 0, dims[axis]) for axis in range(len(dims))]
    drawn = drawn.at[tuple(index_at)].set(smallest)
    longest = dims.index(max(dims))
    index_at[longest] = (index_at[longest] + 1) % dims[longest]
    return drawn.at[tuple(index_at)].set(high)


def block_levels(rng, extent, pieces, smallest, high):
    def one(axis_at, blocks):
        steps = jax.random.uniform(jax.random.fold_in(jax.random.fold_in(rng, 6), axis_at), (blocks,), jnp.float32, smallest / len(pieces), high / len(pieces))
        return jnp.repeat(jnp.exp(steps), extent[axis_at] // blocks).reshape((-1,) + (1,) * (len(extent) - axis_at - 1))

    gain = one(*pieces[0])
    for cut in pieces[1:]:
        gain = gain * one(*cut)
    return gain


def normal_values(rng, extent, deviation, bound, shards=(), held_as=jnp.bfloat16):
    array = jax.random.normal(rng, extent, jnp.float32) * deviation
    if len(shards) > 0:
        array = block_levels(rng, extent, shards, -0.22, 0.18) * array
    return jnp.clip(array, min=-bound, max=bound).astype(held_as)


def setup_inputs(seed: int = 0) -> dict:
    key_list = jax.random.split(jax.random.key(seed), 7)
    return {
        "covariances": draw_covariances(jax.random.fold_in(key_list[6], 71), 0),
        "clusters": draw_clusters(jax.random.fold_in(key_list[6], 71), 0),
        "cluster_valid": with_ends((jax.random.randint(key_list[2], (USERS, CLUSTER), 0, 4) < 3).astype(jnp.int32), jax.random.fold_in(key_list[2], 1), 0, 1),
        "pilots": with_ends(jax.random.randint(key_list[3], (USERS,), 0, PILOT_SEQUENCES), jax.random.fold_in(key_list[3], 1), 0, PILOT_SEQUENCES - 1).astype(jnp.int32),
        "received_pilot": normal_values(key_list[4], (APS, SUBC, PILOT_SEQUENCES * 8), 1.5, 9.0, ((0, 16), (1, 2)), jnp.float32),
        "received_data": normal_values(key_list[5], (APS, SUBC, DATA_SYMBOLS * 8), 3.0, 18.0, ((0, 16), (1, 2)), jnp.float32),
    }


def embed_real(flat):
    real_block = flat[..., :16].reshape(flat.shape[:-1] + (4, 4))
    imag_block = flat[..., 16:].reshape(flat.shape[:-1] + (4, 4))
    upper = jnp.concatenate([real_block, -imag_block], -1)
    lower = jnp.concatenate([imag_block, real_block], -1)
    return jnp.concatenate([upper, lower], -2)

def reference(covariances, clusters, cluster_valid, pilots, received_pilot, received_data):
    highest_precision = lax.Precision.HIGHEST
    user_count, cluster = clusters.shape
    access_point_count = received_pilot.shape[0]
    subcarrier_list = received_pilot.shape[1]
    flat_access_points = clusters.reshape(-1)
    presence = cluster_valid.reshape(-1).astype(jnp.float32)
    pilot_assignment = jnp.repeat(pilots, cluster)
    cov_mat = embed_real(covariances.reshape(-1, 32)) * presence[:, None, None]
    bin_ids = flat_access_points * PILOT_SEQUENCES + pilot_assignment
    identity = jnp.eye(8, dtype=jnp.float32)
    psi_mat = jax.ops.segment_sum(cov_mat, bin_ids, num_segments=access_point_count * PILOT_SEQUENCES) + identity
    psi_inv = jnp.linalg.inv(psi_mat)
    filt_mat = jnp.einsum('sij,sjk->sik', cov_mat, psi_inv[bin_ids], precision=highest_precision)
    err_mat = cov_mat - jnp.einsum('sij,sjk->sik', filt_mat, cov_mat, precision=highest_precision)
    err_ap = jax.ops.segment_sum(err_mat, flat_access_points, num_segments=access_point_count)
    pilot_observation = received_pilot.reshape(access_point_count, subcarrier_list, PILOT_SEQUENCES, 8)
    data_observation = received_data.reshape(access_point_count, subcarrier_list, DATA_SYMBOLS, 8)

    def each_subcarrier(subcarrier_index):
        slot_observation = pilot_observation[flat_access_points, subcarrier_index, pilot_assignment]
        estimate = jnp.einsum('sij,sj->si', filt_mat, slot_observation, precision=highest_precision)
        rotated = jnp.concatenate([-estimate[:, 4:], estimate[:, :4]], 1)
        outer = estimate[:, :, None] * estimate[:, None, :] + rotated[:, :, None] * rotated[:, None, :]
        interf = identity + err_ap + jax.ops.segment_sum(outer, flat_access_points, num_segments=access_point_count)
        combining_weight = jnp.linalg.inv(interf)
        weighted_symbols = jnp.einsum('qlw,qfw->qfl', combining_weight, data_observation[:, subcarrier_index], precision=highest_precision)
        slot_weighted = weighted_symbols[flat_access_points]
        real_part = jnp.einsum('si,sdi->sd', estimate, slot_weighted, precision=highest_precision)
        imag_part = jnp.einsum('si,sdi->sd', rotated, slot_weighted, precision=highest_precision)
        power = jnp.einsum('si,sij,sj->s', estimate, combining_weight[flat_access_points], estimate, precision=highest_precision)
        amplitude = jnp.stack([real_part, imag_part], -1).reshape(user_count, cluster, DATA_SYMBOLS * 2)
        return (jnp.sum(amplitude, 1), jnp.sum(power.reshape(user_count, cluster), 1))
    symbol_estimates, gain_total = lax.map(each_subcarrier, jnp.arange(subcarrier_list))
    return (jnp.transpose(symbol_estimates, (1, 0, 2)), jnp.transpose(gain_total, (1, 0)))
```

```python
import functools

import jax
import jax.numpy as jnp
from jax import lax
from jax.experimental import pallas as pl
from jax.experimental.pallas import tpu as pltpu
from jax.sharding import PartitionSpec as P

F32 = jnp.float32
BF16 = jnp.bfloat16
MESH = pl.DeviceIdType.MESH
PAIRS = [(0, 1), (0, 2), (0, 3), (1, 2), (1, 3), (2, 3)]
ENTRIES = [(i, i) for i in range(4)] + PAIRS
DIAGONAL = [8, 11, 9, 12]
REAL = dict(zip(PAIRS, [0, 1, 2, 3, 4, 10]))
IMAG = dict(zip(PAIRS, [16, 17, 18, 19, 20, 26]))
CODE = 24


def split(x, parts):
    out = []
    for _ in range(parts - 1):
        head = x.astype(BF16)
        out.append(head)
        x = x - head.astype(F32)
    out.append(x.astype(BF16))
    return out


def dot(a, b, rhs_transposed=False):
    dims = (((1,), (1,)), ((), ())) if rhs_transposed else (((1,), (0,)), ((), ()))
    return lax.dot_general(a, b, dims, preferred_element_type=F32)


def dot_split(a, b, parts, rhs_transposed=False):
    rows = a.shape[0]
    full = dot(jnp.concatenate(split(a, parts), 0), b, rhs_transposed)
    total = full[:rows]
    for p in range(1, parts):
        total = total + full[p * rows : (p + 1) * rows]
    return total


def get(h, i, j):
    if i == j:
        return h[i, i]
    if i < j:
        return h[i, j]
    re, im = h[j, i]
    return re, -im


def hermitian_inverse(h):
    h = dict(h)
    for k in range(4):
        inv = 1.0 / h[k, k][0]
        col = {i: get(h, i, k) for i in range(4) if i != k}
        scaled = {i: (c[0] * inv, c[1] * inv) for i, c in col.items()}
        new = {}
        for i, j in ENTRIES:
            if i == k and j == k:
                new[i, j] = (-inv, None)
            elif i == k:
                re, im = scaled[j]
                new[i, j] = (re, -im)
            elif j == k:
                new[i, j] = scaled[i]
            elif i == j:
                a, s = col[i], scaled[i]
                new[i, j] = (h[i, i][0] - (a[0] * s[0] + a[1] * s[1]), None)
            else:
                a, s = scaled[i], col[j]
                re = h[i, j][0] - (a[0] * s[0] + a[1] * s[1])
                im = h[i, j][1] - (a[1] * s[0] - a[0] * s[1])
                new[i, j] = (re, im)
        h = new
    return {k: (-v[0], None if v[1] is None else -v[1]) for k, v in h.items()}


def parts_of(h):
    out = [h[i, i][0] for i in range(4)]
    for p in PAIRS:
        out += list(h[p])
    return out


def from_parts(x):
    h = {(i, i): (x[i], None) for i in range(4)}
    for q, p in enumerate(PAIRS):
        h[p] = (x[4 + 2 * q], x[5 + 2 * q])
    return h


def add_products(acc, a, b):
    re, im = a[0] * b[0], None
    if a[1] is not None and b[1] is not None:
        re = re - a[1] * b[1]
    if b[1] is not None:
        im = a[0] * b[1]
    if a[1] is not None:
        im = a[1] * b[0] if im is None else im + a[1] * b[0]
    if acc is None:
        return re, im
    if im is None:
        im = acc[1]
    elif acc[1] is not None:
        im = acc[1] + im
    return acc[0] + re, im


def block_transpose(x):
    lane_block = lax.broadcasted_iota(jnp.int32, x[0].shape, 1) // 16
    x = list(x)
    for m in (1, 2, 4):
        upper = (lane_block & m) != 0
        new = list(x)
        for p in range(8):
            if p & m:
                continue
            q = p + m
            new[p] = jnp.where(upper, pltpu.roll(x[q], 16 * m, 1), x[p])
            new[q] = jnp.where(upper, x[q], pltpu.roll(x[p], 128 - 16 * m, 1))
        x = new
    return x


def lane_groups(x):
    lane_block = lax.broadcasted_iota(jnp.int32, x[0].shape, 1) // 32
    x = list(x)
    for m in (1, 2):
        upper = (lane_block & m) != 0
        new = list(x)
        for p in range(4):
            if p & m:
                continue
            q = p + m
            new[p] = jnp.where(upper, pltpu.roll(x[q], 32 * m, 1), x[p])
            new[q] = jnp.where(upper, x[q], pltpu.roll(x[p], 128 - 32 * m, 1))
        x = new
    return x


def kernel(
    n, cov_hbm, cl_hbm, valid_hbm, pilot_hbm, rp_hbm, rd_hbm, home,
    cov_ref, cl_ref, valid_ref, pilot_ref, rp_ref, rd_ref,
    send, recv, trans, pinv, obs, data, data_in, ones, gathered, held, out_p, in_p, out_w, in_w, back,
    load_sem, send_sem, recv_sem, data_send_sem, data_recv_sem,
    p_send_sem, p_recv_sem, w_send_sem, w_recv_sem, back_send_sem, back_recv_sem,
):
    me = lax.axis_index("ap")
    core = lax.axis_index("sc")
    rows = n // 4
    sets = n // 16
    groups = 4 * sets
    q, z = lax.div(me, rows), lax.rem(me, rows)

    pairs = [
        (cl_hbm, cl_ref), (valid_hbm, valid_ref), (pilot_hbm, pilot_ref),
        (cov_hbm, cov_ref), (rp_hbm, rp_ref), (rd_hbm, rd_ref),
    ]
    loads = [pltpu.make_async_copy(a, b, load_sem.at[i]) for i, (a, b) in enumerate(pairs)]
    for load in loads:
        load.start()

    barrier = pltpu.get_barrier_semaphore()

    @pl.loop(1, n)
    def _(d):
        pl.semaphore_signal(barrier, inc=1, device_id=(lax.rem(me + d, n), core), device_id_type=MESH)

    trans[...] = jnp.zeros_like(trans)
    ones[...] = jnp.zeros_like(ones)
    for load in loads[:4]:
        load.wait()
    wide = lambda x: jnp.concatenate([x] * 4, 1)
    cl = wide(cl_ref[...])
    code = jnp.where(
        wide(valid_ref[...]) > 0, (wide(pilot_ref[...]) * 16 + (cl & 15)).astype(F32) + 1.0, 0.0
    )
    owner = (cl >> 4) - lax.broadcasted_iota(jnp.int32, (16, 128), 1) // 32
    slots = []
    for a in range(4):
        part = cov_ref[:, 128 * a : 128 * a + 128]
        turned = jnp.concatenate([part] * 4, 0).T
        slots += [turned[32 * j : 32 * j + 32] for j in range(4)]
    row8 = lax.broadcasted_iota(jnp.int32, (8, 128), 0)
    for t in range(n // 4):
        tiles = [jnp.zeros((8, 128), F32)] * 4
        mark = jnp.zeros((8, 128), F32)
        for c in range(16):
            mine = jnp.broadcast_to(owner[c : c + 1], (8, 128)) == 4 * t
            tiles = [jnp.where(mine, slots[c][8 * v : 8 * v + 8], tiles[v]) for v in range(4)]
            mark = jnp.where(mine, jnp.broadcast_to(code[c : c + 1], (8, 128)), mark)
        first = jnp.broadcast_to(tiles[0][0:1], (8, 128))
        second = jnp.broadcast_to(tiles[0][5:6], (8, 128))
        tiles[1] = jnp.where(row8 == 1, first, jnp.where(row8 == 6, second, tiles[1]))
        tiles[3] = jnp.where(row8 == 1, mark, tiles[3])
        tiles = [jnp.where(row8 < 3, pltpu.roll(x, 7, 0), pltpu.roll(x, 5, 0)) for x in tiles]
        for j, tile in enumerate(lane_groups(tiles)):
            send[4 * t + j] = tile

    pl.semaphore_wait(barrier, n - 1)

    def slot_copy(p, slot):
        return pltpu.make_async_remote_copy(
            src_ref=send.at[p, 0:5], dst_ref=recv.at[slot, 0:5],
            send_sem=send_sem.at[p], recv_sem=recv_sem.at[slot],
            device_id=(p, core), device_id_type=MESH,
        )

    def data_copy(p, slot):
        return pltpu.make_async_remote_copy(
            src_ref=data, dst_ref=data_in.at[slot],
            send_sem=data_send_sem.at[p], recv_sem=data_recv_sem.at[slot],
            device_id=(q * rows + p, core), device_id_type=MESH,
        )

    def p_copy(p, slot):
        return pltpu.make_async_remote_copy(
            src_ref=out_p.at[p], dst_ref=in_p.at[slot],
            send_sem=p_send_sem.at[p], recv_sem=p_recv_sem.at[slot],
            device_id=(q * rows + p, core), device_id_type=MESH,
        )

    def w_copy(p, slot):
        return pltpu.make_async_remote_copy(
            src_ref=out_w.at[p], dst_ref=in_w.at[slot],
            send_sem=w_send_sem.at[p], recv_sem=w_recv_sem.at[slot],
            device_id=(q * rows + p, core), device_id_type=MESH,
        )

    def back_copy(p, slot):
        return pltpu.make_async_remote_copy(
            src_ref=back.at[p], dst_ref=home.at[slot],
            send_sem=back_send_sem.at[p], recv_sem=back_recv_sem.at[slot],
            device_id=(p * rows + z, core), device_id_type=MESH,
        )

    @pl.loop(1, n)
    def _(d):
        p = lax.rem(me + d, n)
        slot_copy(p, me).start()

    recv[me] = send[me]

    for load in loads[4:]:
        load.wait()
    turned = jnp.concatenate([rd_ref[:, f, :] for f in range(8)], 0).T.reshape(16, 8, 128)
    for f, tile in enumerate(block_transpose([turned[:, i, :] for i in range(8)])):
        data[:, f, :] = tile

    @pl.loop(1, rows)
    def _(d):
        data_copy(lax.rem(z + d, rows), z).start()

    turned = jnp.concatenate([rp_ref[:, f, :] for f in range(8)], 0).T
    for half in range(2):
        tiles = [turned[8 * (8 * half + t) : 8 * (8 * half + t) + 8] for t in range(8)]
        for f, tile in enumerate(block_transpose(tiles)):
            obs[f, :, 128 * half : 128 * half + 128] = tile
    observed = jnp.concatenate([obs[:, i, :] for i in range(8)], 0)
    observed = jnp.concatenate(split(observed, 3), 0)

    @pl.loop(1, n)
    def _(d):
        p = lax.rem(me + n - d, n)
        slot_copy(p, p).wait_recv()

    row32 = lax.broadcasted_iota(jnp.int32, (32, 128), 0)
    codes, matrices = [], []
    for e in range(sets):
        for j in range(4):
            tiles = lane_groups([recv[h * rows + 4 * e + j] for h in range(4)])
            for v, tile in enumerate(tiles):
                trans[e, j, 8 * v : 8 * v + 5] = tile[0:5]
            codes.append(tiles[3][0:1])
            matrices.append(jnp.where(row32 == CODE, 0.0, trans[e, j]))
    codes = jnp.concatenate(codes, 1) - 1.0
    matrices = jnp.concatenate(matrices, 1)
    width = 128 * groups
    bins = lax.broadcasted_iota(jnp.int32, (256, width), 0).astype(F32)
    choose = jnp.where(bins == codes, 1.0, 0.0).astype(BF16)
    places = jnp.where(codes >= 0.0, codes - 16.0 * jnp.floor(codes * 0.0625), -1.0)
    ap_rows = (lax.broadcasted_iota(jnp.int32, (128, width), 0) & 15).astype(F32)
    pick = jnp.where(ap_rows == places, 1.0, 0.0).astype(BF16)
    for g in range(groups):
        out_p[g] = jnp.broadcast_to(places[:, 128 * g : 128 * g + 128], (8, 128))

        @pl.when(z != g)
        def _():
            p_copy(g, z).start()

    psi = dot_split(matrices, choose, 3, True)
    hermitian = {(i, i): (psi[r : r + 1] + 1.0, None) for i, r in enumerate(DIAGONAL)}
    hermitian.update({p: (psi[REAL[p] : REAL[p] + 1], psi[IMAG[p] : IMAG[p] + 1]) for p in PAIRS})
    inverse = jnp.concatenate(parts_of(hermitian_inverse(hermitian)), 0)
    slot_inverse = dot_split(inverse, choose, 3)
    slot_obs = dot(observed, choose)
    slot_obs = slot_obs[0:64] + slot_obs[64:128] + slot_obs[128:192]

    estimates, outers = [], []
    for e in range(sets):
        for j in range(4):
            g = 4 * e + j
            pinv[j] = slot_inverse[:, 128 * g : 128 * g + 128]
        pi = from_parts([pinv[:, x, :] for x in range(16)])
        r = {(i, i): (trans[e, :, DIAGONAL[i], :], None) for i in range(4)}
        for p in PAIRS:
            r[p] = (trans[e, :, REAL[p], :], trans[e, :, IMAG[p], :])
        w = {}
        for i in range(4):
            for k in range(4):
                acc = None
                for l in range(4):
                    acc = add_products(acc, get(r, i, l), get(pi, l, k))
                w[i, k] = acc
        err = {}
        for i, k in ENTRIES:
            acc = None
            for l in range(4):
                acc = add_products(acc, w[i, l], get(r, l, k))
            re = r[i, k][0] - acc[0]
            err[i, k] = (re, None) if i == k else (re, r[i, k][1] - acc[1])
        for j in range(4):
            g = 4 * e + j
            cols = slice(128 * g, 128 * g + 128)
            y = [(slot_obs[8 * i : 8 * i + 8, cols], slot_obs[32 + 8 * i : 40 + 8 * i, cols]) for i in range(4)]
            h = []
            for i in range(4):
                acc = None
                for k in range(4):
                    wr, wi = w[i, k]
                    acc = add_products(acc, (wr[j : j + 1], wi[j : j + 1]), y[k])
                h.append(acc)
            estimates.append(h)
            out = []
            for i in range(4):
                out.append(h[i][0] * h[i][0] + h[i][1] * h[i][1] + err[i, i][0][j : j + 1])
            for i, k in PAIRS:
                out.append(h[i][0] * h[k][0] + h[i][1] * h[k][1] + err[i, k][0][j : j + 1])
                out.append(h[i][1] * h[k][0] - h[i][0] * h[k][1] + err[i, k][1][j : j + 1])
            outers.append(jnp.concatenate(out, 0))
    summed = dot_split(jnp.concatenate(outers, 1), pick, 3, True)
    own_f = lax.broadcasted_iota(jnp.int32, (8, 128), 1) // 16 == lax.broadcasted_iota(jnp.int32, (8, 128), 0)
    comps = [
        jnp.sum(jnp.where(own_f, summed[8 * x : 8 * x + 8], 0.0), 0, keepdims=True) for x in range(16)
    ]
    weight = hermitian_inverse(from_parts([c + 1.0 if x < 4 else c for x, c in enumerate(comps)]))

    masked = jnp.concatenate([jnp.where(own_f, c, 0.0) for c in parts_of(weight)], 0)
    slot_weight = dot_split(masked, pick, 3)
    for g in range(groups):
        cols = slice(128 * g, 128 * g + 128)
        h = estimates[g]
        gs = from_parts([slot_weight[8 * x : 8 * x + 8, cols] for x in range(16)])
        for i in range(4):
            gs[i, i] = (gs[i, i][0], None)
        power = None
        for i in range(4):
            acc = None
            for k in range(4):
                acc = add_products(acc, get(gs, i, k), h[k])
            out_w[g, 8 * i : 8 * i + 8] = acc[0]
            out_w[g, 32 + 8 * i : 40 + 8 * i] = acc[1]
            term = h[i][0] * acc[0] + h[i][1] * acc[1]
            power = term if power is None else power + term
        out_w[g, 64:72] = power

        @pl.when(z != g)
        def _():
            w_copy(g, z).start()

    row16 = lax.broadcasted_iota(jnp.int32, (16, 128), 0).astype(F32)
    in_p[z] = out_p[z]
    in_w[z] = out_w[z]
    for k in range(rows):
        p = z ^ k
        if k > 0:
            data_copy(p, p).wait_recv()
            p_copy(p, p).wait_recv()
        place = in_p[p]
        hot = jnp.where(row16 == jnp.concatenate([place, place], 0), 1.0, 0.0).astype(BF16)
        for i in range(8):
            for half in range(2):
                at = 128 * half + 16 * i
                ones[k % 2, at : at + 16, 128 * i : 128 * i + 128] = hot
        source = (data[...] if k == 0 else data_in[p]).reshape(128, 128)
        left = jnp.concatenate(split(source, 2), 1)
        for i in range(4):
            cols = slice(256 * i, 256 * i + 256)
            wide_out = dot(left, ones[k % 2, :, cols])
            gathered[k, 2 * i] = wide_out[:, :128].reshape(16, 8, 128)
            gathered[k, 2 * i + 1] = wide_out[:, 128:].reshape(16, 8, 128)

    sums = [None] * 32
    power = None
    for k in range(rows):
        p = z ^ k
        if k > 0:
            w_copy(p, p).wait_recv()
        u = [in_w[p, 8 * i : 8 * i + 8] for i in range(8)]
        part = in_w[p, 64:72]
        power = part if power is None else power + part
        for s in range(16):
            d = [gathered[k, i, s] for i in range(8)]
            re = im = None
            for i in range(4):
                x = u[i] * d[i] + u[i + 4] * d[i + 4]
                y = u[i] * d[i + 4] - u[i + 4] * d[i]
                re = x if re is None else re + x
                im = y if im is None else im + y
            sums[2 * s] = re if k == 0 else sums[2 * s] + re
            sums[2 * s + 1] = im if k == 0 else sums[2 * s + 1] + im
    for s in range(32):
        held[s] = sums[s]
    for half in range(2):
        tile = jnp.concatenate([held[:, 4 * half + f, :] for f in range(4)], 0).T.reshape(4, 4, 8, 128)
        for j in range(4):
            back[:, 2 * j + half] = tile[:, j]
    turned = jnp.concatenate([power, jnp.zeros((120, 128), F32)], 0).T.reshape(4, 4, 8, 128)
    gains = turned[:, 0].reshape(32, 128)
    for j in range(1, 4):
        gains = gains + pltpu.roll(turned[:, j].reshape(32, 128), 8 * j, 1)
    back[:, 8] = gains.reshape(4, 8, 128)

    for k in range(1, 4):
        back_copy(lax.rem(q + k, 4), q).start()
    home[q] = back[q]
    for k in range(1, 4):
        p = lax.rem(q + 4 - k, 4)
        back_copy(p, p).wait_recv()

    @pl.loop(1, n)
    def _(k):
        p = lax.rem(me + k, n)
        slot_copy(p, p).wait_send()

    @pl.loop(1, rows)
    def _(k):
        p = lax.rem(z + k, rows)
        data_copy(p, p).wait_send()
        p_copy(p, p).wait_send()
        w_copy(p, p).wait_send()

    for k in range(1, 4):
        p = lax.rem(q + k, 4)
        back_copy(p, p).wait_send()


def finish(home, sym_ref, gain_ref):
    total = (home[0] + home[1]) + (home[2] + home[3])
    for j in range(4):
        for f in range(8):
            tile = total[2 * j + f // 4]
            sym_ref[8 * j : 8 * j + 8, f, :] = tile[:, 32 * (f % 4) : 32 * (f % 4) + 32]
    gains = jnp.concatenate([total[8], jnp.zeros((120, 128), F32)], 0).T
    gain_ref[...] = jnp.concatenate([gains[8 * j : 8 * j + 8, 0:8] for j in range(4)], 1)


def body(n, covariances, clusters, cluster_valid, pilots, received_pilot, received_data):
    vmem = pl.BlockSpec(memory_space=pltpu.VMEM)
    rows = n // 4
    home = pl.pallas_call(
        functools.partial(kernel, n),
        out_shape=pltpu.VMEM((4, 9, 8, 128), F32),
        in_specs=[pl.BlockSpec(memory_space=pltpu.HBM)] * 6,
        out_specs=vmem,
        scratch_shapes=[
            pltpu.VMEM((32, 512), F32),
            pltpu.VMEM((16, 32), jnp.int32),
            pltpu.VMEM((16, 32), jnp.int32),
            pltpu.VMEM((1, 32), jnp.int32),
            pltpu.VMEM((16, 8, 128), F32),
            pltpu.VMEM((16, 8, 128), F32),
            pltpu.VMEM((n, 8, 128), F32),
            pltpu.VMEM((n, 8, 128), F32),
            pltpu.VMEM((n // 16, 4, 32, 128), F32),
            pltpu.VMEM((4, 16, 128), F32),
            pltpu.VMEM((8, 8, 256), F32),
            pltpu.VMEM((16, 8, 128), F32),
            pltpu.VMEM((rows, 16, 8, 128), F32),
            pltpu.VMEM((2, 256, 1024), BF16),
            pltpu.VMEM((rows, 8, 16, 8, 128), F32),
            pltpu.VMEM((32, 8, 128), F32),
            pltpu.VMEM((rows, 8, 128), F32),
            pltpu.VMEM((rows, 8, 128), F32),
            pltpu.VMEM((rows, 72, 128), F32),
            pltpu.VMEM((rows, 72, 128), F32),
            pltpu.VMEM((4, 9, 8, 128), F32),
            pltpu.SemaphoreType.DMA((6,)),
            pltpu.SemaphoreType.DMA((n,)),
            pltpu.SemaphoreType.DMA((n,)),
            pltpu.SemaphoreType.DMA((rows,)),
            pltpu.SemaphoreType.DMA((rows,)),
            pltpu.SemaphoreType.DMA((rows,)),
            pltpu.SemaphoreType.DMA((rows,)),
            pltpu.SemaphoreType.DMA((rows,)),
            pltpu.SemaphoreType.DMA((rows,)),
            pltpu.SemaphoreType.DMA((4,)),
            pltpu.SemaphoreType.DMA((4,)),
        ],
        compiler_params=pltpu.CompilerParams(
            collective_id=0, has_side_effects=True, vmem_limit_bytes=65000 * 1024
        ),
    )(covariances, clusters.T, cluster_valid.T, pilots.reshape(1, -1), received_pilot, received_data)
    symbols, gain = pl.pallas_call(
        finish,
        out_shape=(jax.ShapeDtypeStruct((32, 8, 32), F32), jax.ShapeDtypeStruct((8, 32), F32)),
        in_specs=[vmem],
        out_specs=(vmem, vmem),
    )(pltpu.with_memory_space_constraint(home, pltpu.VMEM))
    return symbols, gain.T


def solution(mesh):
    placed = (
        P("ap", None),
        P("ap", None),
        P("ap", None),
        P("ap"),
        P("ap", "sc", None),
        P("ap", "sc", None),
    )
    return jax.shard_map(
        functools.partial(body, mesh.shape["ap"]),
        mesh=mesh,
        in_specs=placed,
        out_specs=(P("ap", "sc", None), P("ap", "sc")),
        check_vma=False,
    )
```

```python
import functools

import jax
import jax.numpy as jnp
from jax import lax
from jax.experimental import pallas as pl
from jax.experimental.pallas import tpu as pltpu
from jax.sharding import PartitionSpec as P

F32 = jnp.float32
BF16 = jnp.bfloat16
MESH = pl.DeviceIdType.MESH
PAIRS = [(0, 1), (0, 2), (0, 3), (1, 2), (1, 3), (2, 3)]
ENTRIES = [(i, i) for i in range(4)] + PAIRS
DIAGONAL = [8, 11, 9, 12]
REAL = dict(zip(PAIRS, [0, 1, 2, 3, 4, 10]))
IMAG = dict(zip(PAIRS, [16, 17, 18, 19, 20, 26]))
CODE = 24


def split(x, parts):
    out = []
    for _ in range(parts - 1):
        head = x.astype(BF16)
        out.append(head)
        x = x - head.astype(F32)
    out.append(x.astype(BF16))
    return out


def dot(a, b, rhs_transposed=False):
    dims = (((1,), (1,)), ((), ())) if rhs_transposed else (((1,), (0,)), ((), ()))
    return lax.dot_general(a, b, dims, preferred_element_type=F32)


def dot_split(a, b, parts, rhs_transposed=False):
    rows = a.shape[0]
    full = dot(jnp.concatenate(split(a, parts), 0), b, rhs_transposed)
    total = full[:rows]
    for p in range(1, parts):
        total = total + full[p * rows : (p + 1) * rows]
    return total


def get(h, i, j):
    if i == j:
        return h[i, i]
    if i < j:
        return h[i, j]
    re, im = h[j, i]
    return re, -im


def hermitian_inverse(h):
    h = dict(h)
    for k in range(4):
        inv = 1.0 / h[k, k][0]
        col = {i: get(h, i, k) for i in range(4) if i != k}
        scaled = {i: (c[0] * inv, c[1] * inv) for i, c in col.items()}
        new = {}
        for i, j in ENTRIES:
            if i == k and j == k:
                new[i, j] = (-inv, None)
            elif i == k:
                re, im = scaled[j]
                new[i, j] = (re, -im)
            elif j == k:
                new[i, j] = scaled[i]
            elif i == j:
                a, s = col[i], scaled[i]
                new[i, j] = (h[i, i][0] - (a[0] * s[0] + a[1] * s[1]), None)
            else:
                a, s = scaled[i], col[j]
                re = h[i, j][0] - (a[0] * s[0] + a[1] * s[1])
                im = h[i, j][1] - (a[1] * s[0] - a[0] * s[1])
                new[i, j] = (re, im)
        h = new
    return {k: (-v[0], None if v[1] is None else -v[1]) for k, v in h.items()}


def parts_of(h):
    out = [h[i, i][0] for i in range(4)]
    for p in PAIRS:
        out += list(h[p])
    return out


def from_parts(x):
    h = {(i, i): (x[i], None) for i in range(4)}
    for q, p in enumerate(PAIRS):
        h[p] = (x[4 + 2 * q], x[5 + 2 * q])
    return h


def add_products(acc, a, b):
    re, im = a[0] * b[0], None
    if a[1] is not None and b[1] is not None:
        re = re - a[1] * b[1]
    if b[1] is not None:
        im = a[0] * b[1]
    if a[1] is not None:
        im = a[1] * b[0] if im is None else im + a[1] * b[0]
    if acc is None:
        return re, im
    if im is None:
        im = acc[1]
    elif acc[1] is not None:
        im = acc[1] + im
    return acc[0] + re, im


def block_transpose(x):
    lane_block = lax.broadcasted_iota(jnp.int32, x[0].shape, 1) // 16
    x = list(x)
    for m in (1, 2, 4):
        upper = (lane_block & m) != 0
        new = list(x)
        for p in range(8):
            if p & m:
                continue
            q = p + m
            new[p] = jnp.where(upper, pltpu.roll(x[q], 16 * m, 1), x[p])
            new[q] = jnp.where(upper, x[q], pltpu.roll(x[p], 128 - 16 * m, 1))
        x = new
    return x


def lane_groups(x):
    lane_block = lax.broadcasted_iota(jnp.int32, x[0].shape, 1) // 32
    x = list(x)
    for m in (1, 2):
        upper = (lane_block & m) != 0
        new = list(x)
        for p in range(4):
            if p & m:
                continue
            q = p + m
            new[p] = jnp.where(upper, pltpu.roll(x[q], 32 * m, 1), x[p])
            new[q] = jnp.where(upper, x[q], pltpu.roll(x[p], 128 - 32 * m, 1))
        x = new
    return x


def kernel(
    n, cov_hbm, cl_hbm, valid_hbm, pilot_hbm, rp_hbm, rd_hbm, home,
    cov_ref, cl_ref, valid_ref, pilot_ref, rp_ref, rd_ref,
    send, recv, trans, pinv, obs, data, data_in, ones, gathered, held, out_p, in_p, out_w, in_w, back,
    load_sem, send_sem, recv_sem, data_send_sem, data_recv_sem,
    p_send_sem, p_recv_sem, w_send_sem, w_recv_sem, back_send_sem, back_recv_sem,
):
    me = lax.axis_index("ap")
    core = lax.axis_index("sc")
    rows = n // 4
    sets = n // 16
    groups = 4 * sets
    q, z = lax.div(me, rows), lax.rem(me, rows)

    pairs = [
        (cl_hbm, cl_ref), (valid_hbm, valid_ref), (pilot_hbm, pilot_ref),
        (cov_hbm, cov_ref), (rp_hbm, rp_ref), (rd_hbm, rd_ref),
    ]
    loads = [pltpu.make_async_copy(a, b, load_sem.at[i]) for i, (a, b) in enumerate(pairs)]
    odd = lax.rem(core, 2) == 1
    pair = core ^ 1
    barrier = pltpu.get_barrier_semaphore()

    def greet(p, c):
        pl.semaphore_signal(barrier, inc=1, device_id=(p, c), device_id_type=MESH)

    @pl.when(odd)
    def _():
        for load in loads[:4]:
            load.start()

        @pl.loop(1, n)
        def _(d):
            greet(me ^ (n - d), core)

    @pl.when(jnp.logical_not(odd))
    def _():
        @pl.loop(0, n)
        def _(d):
            greet(me ^ (n - 1 - d), pair)

        @pl.loop(1, rows)
        def _(d):
            greet(q * rows + (z ^ d), core)

        for d in range(1, 4):
            greet((q ^ d) * rows + z, core)

    for load in loads[4:]:
        load.start()

    trans[...] = jnp.zeros_like(trans)
    ones[...] = jnp.zeros_like(ones)

    def slot_copy(p, slot, to):
        return pltpu.make_async_remote_copy(
            src_ref=send.at[p, 0:5], dst_ref=recv.at[slot, 0:5],
            send_sem=send_sem.at[lax.rem(to, 2), p], recv_sem=recv_sem.at[slot],
            device_id=(p, to), device_id_type=MESH,
        )

    def data_copy(p, slot):
        return pltpu.make_async_remote_copy(
            src_ref=data, dst_ref=data_in.at[slot],
            send_sem=data_send_sem.at[p], recv_sem=data_recv_sem.at[slot],
            device_id=(q * rows + p, core), device_id_type=MESH,
        )

    def p_copy(p, slot):
        return pltpu.make_async_remote_copy(
            src_ref=out_p.at[p], dst_ref=in_p.at[slot],
            send_sem=p_send_sem.at[p], recv_sem=p_recv_sem.at[slot],
            device_id=(q * rows + p, core), device_id_type=MESH,
        )

    def w_copy(p, slot):
        return pltpu.make_async_remote_copy(
            src_ref=out_w.at[p], dst_ref=in_w.at[slot],
            send_sem=w_send_sem.at[p], recv_sem=w_recv_sem.at[slot],
            device_id=(q * rows + p, core), device_id_type=MESH,
        )

    def back_copy(p, slot):
        return pltpu.make_async_remote_copy(
            src_ref=back.at[p], dst_ref=home.at[slot],
            send_sem=back_send_sem.at[p], recv_sem=back_recv_sem.at[slot],
            device_id=(p * rows + z, core), device_id_type=MESH,
        )

    @pl.when(odd)
    def _():
        for load in loads[:4]:
            load.wait()
        wide = lambda x: jnp.concatenate([x] * 4, 1)
        cl = wide(cl_ref[...])
        code = jnp.where(
            wide(valid_ref[...]) > 0, (wide(pilot_ref[...]) * 16 + (cl & 15)).astype(F32) + 1.0, 0.0
        )
        owner = (cl >> 4) - lax.broadcasted_iota(jnp.int32, (16, 128), 1) // 32
        slots = []
        for a in range(4):
            part = cov_ref[:, 128 * a : 128 * a + 128]
            turned = jnp.concatenate([part] * 4, 0).T
            slots += [turned[32 * j : 32 * j + 32] for j in range(4)]
        row8 = lax.broadcasted_iota(jnp.int32, (8, 128), 0)
        for t in range(n // 4):
            tiles = [jnp.zeros((8, 128), F32)] * 4
            mark = jnp.zeros((8, 128), F32)
            for c in range(16):
                mine = jnp.broadcast_to(owner[c : c + 1], (8, 128)) == 4 * t
                tiles = [jnp.where(mine, slots[c][8 * v : 8 * v + 8], tiles[v]) for v in range(4)]
                mark = jnp.where(mine, jnp.broadcast_to(code[c : c + 1], (8, 128)), mark)
            first = jnp.broadcast_to(tiles[0][0:1], (8, 128))
            second = jnp.broadcast_to(tiles[0][5:6], (8, 128))
            tiles[1] = jnp.where(row8 == 1, first, jnp.where(row8 == 6, second, tiles[1]))
            tiles[3] = jnp.where(row8 == 1, mark, tiles[3])
            tiles = [jnp.where(row8 < 3, pltpu.roll(x, 7, 0), pltpu.roll(x, 5, 0)) for x in tiles]
            for j, tile in enumerate(lane_groups(tiles)):
                send[4 * t + j] = tile
        pl.semaphore_wait(barrier, 2 * n - 1)

        @pl.loop(0, n)
        def _(d):
            slot_copy(me ^ (n - 1 - d), me, pair).start()

        @pl.loop(1, n)
        def _(d):
            slot_copy(me ^ (n - d), me, core).start()

        recv[me] = send[me]

    @pl.when(jnp.logical_not(odd))
    def _():
        pl.semaphore_wait(barrier, rows + 2)

    for load in loads[4:]:
        load.wait()
    turned = jnp.concatenate([rd_ref[:, f, :] for f in range(8)], 0).T.reshape(16, 8, 128)
    for f, tile in enumerate(block_transpose([turned[:, i, :] for i in range(8)])):
        data[:, f, :] = tile

    @pl.loop(1, rows)
    def _(d):
        data_copy(lax.rem(z + d, rows), z).start()

    turned = jnp.concatenate([rp_ref[:, f, :] for f in range(8)], 0).T
    for half in range(2):
        tiles = [turned[8 * (8 * half + t) : 8 * (8 * half + t) + 8] for t in range(8)]
        for f, tile in enumerate(block_transpose(tiles)):
            obs[f, :, 128 * half : 128 * half + 128] = tile
    observed = jnp.concatenate([obs[:, i, :] for i in range(8)], 0)
    observed = jnp.concatenate(split(observed, 3), 0)

    @pl.loop(1, n)
    def _(d):
        p = me ^ d
        slot_copy(p, p, pair).wait_recv()

    @pl.when(jnp.logical_not(odd))
    def _():
        slot_copy(me, me, pair).wait_recv()


    row32 = lax.broadcasted_iota(jnp.int32, (32, 128), 0)
    codes, matrices = [], []
    for e in range(sets):
        for j in range(4):
            tiles = lane_groups([recv[h * rows + 4 * e + j] for h in range(4)])
            for v, tile in enumerate(tiles):
                trans[e, j, 8 * v : 8 * v + 5] = tile[0:5]
            codes.append(tiles[3][0:1])
            matrices.append(jnp.where(row32 == CODE, 0.0, trans[e, j]))
    codes = jnp.concatenate(codes, 1) - 1.0
    matrices = jnp.concatenate(matrices, 1)
    width = 128 * groups
    bins = lax.broadcasted_iota(jnp.int32, (256, width), 0).astype(F32)
    choose = jnp.where(bins == codes, 1.0, 0.0).astype(BF16)
    places = jnp.where(codes >= 0.0, codes - 16.0 * jnp.floor(codes * 0.0625), -1.0)
    ap_rows = (lax.broadcasted_iota(jnp.int32, (128, width), 0) & 15).astype(F32)
    pick = jnp.where(ap_rows == places, 1.0, 0.0).astype(BF16)
    for g in range(groups):
        out_p[g] = jnp.broadcast_to(places[:, 128 * g : 128 * g + 128], (8, 128))

        @pl.when(z != g)
        def _():
            p_copy(g, z).start()

    psi = dot_split(matrices, choose, 3, True)
    hermitian = {(i, i): (psi[r : r + 1] + 1.0, None) for i, r in enumerate(DIAGONAL)}
    hermitian.update({p: (psi[REAL[p] : REAL[p] + 1], psi[IMAG[p] : IMAG[p] + 1]) for p in PAIRS})
    inverse = jnp.concatenate(parts_of(hermitian_inverse(hermitian)), 0)
    slot_inverse = dot_split(inverse, choose, 3)
    slot_obs = dot(observed, choose)
    slot_obs = slot_obs[0:64] + slot_obs[64:128] + slot_obs[128:192]

    estimates, outers = [], []
    for e in range(sets):
        for j in range(4):
            g = 4 * e + j
            pinv[j] = slot_inverse[:, 128 * g : 128 * g + 128]
        pi = from_parts([pinv[:, x, :] for x in range(16)])
        r = {(i, i): (trans[e, :, DIAGONAL[i], :], None) for i in range(4)}
        for p in PAIRS:
            r[p] = (trans[e, :, REAL[p], :], trans[e, :, IMAG[p], :])
        w = {}
        for i in range(4):
            for k in range(4):
                acc = None
                for l in range(4):
                    acc = add_products(acc, get(r, i, l), get(pi, l, k))
                w[i, k] = acc
        err = {}
        for i, k in ENTRIES:
            acc = None
            for l in range(4):
                acc = add_products(acc, w[i, l], get(r, l, k))
            re = r[i, k][0] - acc[0]
            err[i, k] = (re, None) if i == k else (re, r[i, k][1] - acc[1])
        for j in range(4):
            g = 4 * e + j
            cols = slice(128 * g, 128 * g + 128)
            y = [(slot_obs[8 * i : 8 * i + 8, cols], slot_obs[32 + 8 * i : 40 + 8 * i, cols]) for i in range(4)]
            h = []
            for i in range(4):
                acc = None
                for k in range(4):
                    wr, wi = w[i, k]
                    acc = add_products(acc, (wr[j : j + 1], wi[j : j + 1]), y[k])
                h.append(acc)
            estimates.append(h)
            out = []
            for i in range(4):
                out.append(h[i][0] * h[i][0] + h[i][1] * h[i][1] + err[i, i][0][j : j + 1])
            for i, k in PAIRS:
                out.append(h[i][0] * h[k][0] + h[i][1] * h[k][1] + err[i, k][0][j : j + 1])
                out.append(h[i][1] * h[k][0] - h[i][0] * h[k][1] + err[i, k][1][j : j + 1])
            outers.append(jnp.concatenate(out, 0))
    summed = dot_split(jnp.concatenate(outers, 1), pick, 3, True)
    own_f = lax.broadcasted_iota(jnp.int32, (8, 128), 1) // 16 == lax.broadcasted_iota(jnp.int32, (8, 128), 0)
    comps = [
        jnp.sum(jnp.where(own_f, summed[8 * x : 8 * x + 8], 0.0), 0, keepdims=True) for x in range(16)
    ]
    weight = hermitian_inverse(from_parts([c + 1.0 if x < 4 else c for x, c in enumerate(comps)]))

    masked = jnp.concatenate([jnp.where(own_f, c, 0.0) for c in parts_of(weight)], 0)
    slot_weight = dot_split(masked, pick, 3)
    for g in range(groups):
        cols = slice(128 * g, 128 * g + 128)
        h = estimates[g]
        gs = from_parts([slot_weight[8 * x : 8 * x + 8, cols] for x in range(16)])
        for i in range(4):
            gs[i, i] = (gs[i, i][0], None)
        power = None
        for i in range(4):
            acc = None
            for k in range(4):
                acc = add_products(acc, get(gs, i, k), h[k])
            out_w[g, 8 * i : 8 * i + 8] = acc[0]
            out_w[g, 32 + 8 * i : 40 + 8 * i] = acc[1]
            term = h[i][0] * acc[0] + h[i][1] * acc[1]
            power = term if power is None else power + term
        out_w[g, 64:72] = power

        @pl.when(z != g)
        def _():
            w_copy(g, z).start()

    row16 = lax.broadcasted_iota(jnp.int32, (16, 128), 0).astype(F32)
    in_p[z] = out_p[z]
    in_w[z] = out_w[z]
    for k in range(rows):
        p = z ^ k
        if k > 0:
            data_copy(p, p).wait_recv()
            p_copy(p, p).wait_recv()
        place = in_p[p]
        hot = jnp.where(row16 == jnp.concatenate([place, place], 0), 1.0, 0.0).astype(BF16)
        for i in range(8):
            for half in range(2):
                at = 128 * half + 16 * i
                ones[k % 2, at : at + 16, 128 * i : 128 * i + 128] = hot
        source = (data[...] if k == 0 else data_in[p]).reshape(128, 128)
        left = jnp.concatenate(split(source, 2), 1)
        for i in range(4):
            cols = slice(256 * i, 256 * i + 256)
            wide_out = dot(left, ones[k % 2, :, cols])
            gathered[k, 2 * i] = wide_out[:, :128].reshape(16, 8, 128)
            gathered[k, 2 * i + 1] = wide_out[:, 128:].reshape(16, 8, 128)

    sums = [None] * 32
    power = None
    for k in range(rows):
        p = z ^ k
        if k > 0:
            w_copy(p, p).wait_recv()
        u = [in_w[p, 8 * i : 8 * i + 8] for i in range(8)]
        part = in_w[p, 64:72]
        power = part if power is None else power + part
        for s in range(16):
            d = [gathered[k, i, s] for i in range(8)]
            re = im = None
            for i in range(4):
                x = u[i] * d[i] + u[i + 4] * d[i + 4]
                y = u[i] * d[i + 4] - u[i + 4] * d[i]
                re = x if re is None else re + x
                im = y if im is None else im + y
            sums[2 * s] = re if k == 0 else sums[2 * s] + re
            sums[2 * s + 1] = im if k == 0 else sums[2 * s + 1] + im
    for s in range(32):
        held[s] = sums[s]
    for half in range(2):
        tile = jnp.concatenate([held[:, 4 * half + f, :] for f in range(4)], 0).T.reshape(4, 4, 8, 128)
        for j in range(4):
            back[:, 2 * j + half] = tile[:, j]
    turned = jnp.concatenate([power, jnp.zeros((120, 128), F32)], 0).T.reshape(4, 4, 8, 128)
    gains = turned[:, 0].reshape(32, 128)
    for j in range(1, 4):
        gains = gains + pltpu.roll(turned[:, j].reshape(32, 128), 8 * j, 1)
    back[:, 8] = gains.reshape(4, 8, 128)

    for k in range(1, 4):
        back_copy(lax.rem(q + k, 4), q).start()
    home[q] = back[q]
    for k in range(1, 4):
        p = lax.rem(q + 4 - k, 4)
        back_copy(p, p).wait_recv()

    @pl.when(odd)
    def _():
        @pl.loop(1, n)
        def _(k):
            p = me ^ k
            slot_copy(p, p, pair).wait_send()
            slot_copy(p, p, core).wait_send()

        slot_copy(me, me, pair).wait_send()

    @pl.loop(1, rows)
    def _(k):
        p = lax.rem(z + k, rows)
        data_copy(p, p).wait_send()
        p_copy(p, p).wait_send()
        w_copy(p, p).wait_send()

    for k in range(1, 4):
        p = lax.rem(q + k, 4)
        back_copy(p, p).wait_send()


def finish(home, sym_ref, gain_ref):
    total = (home[0] + home[1]) + (home[2] + home[3])
    for j in range(4):
        for f in range(8):
            tile = total[2 * j + f // 4]
            sym_ref[8 * j : 8 * j + 8, f, :] = tile[:, 32 * (f % 4) : 32 * (f % 4) + 32]
    gains = jnp.concatenate([total[8], jnp.zeros((120, 128), F32)], 0).T
    gain_ref[...] = jnp.concatenate([gains[8 * j : 8 * j + 8, 0:8] for j in range(4)], 1)


def body(n, covariances, clusters, cluster_valid, pilots, received_pilot, received_data):
    vmem = pl.BlockSpec(memory_space=pltpu.VMEM)
    rows = n // 4
    home = pl.pallas_call(
        functools.partial(kernel, n),
        out_shape=pltpu.VMEM((4, 9, 8, 128), F32),
        in_specs=[pl.BlockSpec(memory_space=pltpu.HBM)] * 6,
        out_specs=vmem,
        scratch_shapes=[
            pltpu.VMEM((32, 512), F32),
            pltpu.VMEM((16, 32), jnp.int32),
            pltpu.VMEM((16, 32), jnp.int32),
            pltpu.VMEM((1, 32), jnp.int32),
            pltpu.VMEM((16, 8, 128), F32),
            pltpu.VMEM((16, 8, 128), F32),
            pltpu.VMEM((n, 8, 128), F32),
            pltpu.VMEM((n, 8, 128), F32),
            pltpu.VMEM((n // 16, 4, 32, 128), F32),
            pltpu.VMEM((4, 16, 128), F32),
            pltpu.VMEM((8, 8, 256), F32),
            pltpu.VMEM((16, 8, 128), F32),
            pltpu.VMEM((rows, 16, 8, 128), F32),
            pltpu.VMEM((2, 256, 1024), BF16),
            pltpu.VMEM((rows, 8, 16, 8, 128), F32),
            pltpu.VMEM((32, 8, 128), F32),
            pltpu.VMEM((rows, 8, 128), F32),
            pltpu.VMEM((rows, 8, 128), F32),
            pltpu.VMEM((rows, 72, 128), F32),
            pltpu.VMEM((rows, 72, 128), F32),
            pltpu.VMEM((4, 9, 8, 128), F32),
            pltpu.SemaphoreType.DMA((6,)),
            pltpu.SemaphoreType.DMA((2, n)),
            pltpu.SemaphoreType.DMA((n,)),
            pltpu.SemaphoreType.DMA((rows,)),
            pltpu.SemaphoreType.DMA((rows,)),
            pltpu.SemaphoreType.DMA((rows,)),
            pltpu.SemaphoreType.DMA((rows,)),
            pltpu.SemaphoreType.DMA((rows,)),
            pltpu.SemaphoreType.DMA((rows,)),
            pltpu.SemaphoreType.DMA((4,)),
            pltpu.SemaphoreType.DMA((4,)),
        ],
        compiler_params=pltpu.CompilerParams(
            collective_id=0, has_side_effects=True, vmem_limit_bytes=65000 * 1024
        ),
    )(covariances, clusters.T, cluster_valid.T, pilots.reshape(1, -1), received_pilot, received_data)
    symbols, gain = pl.pallas_call(
        finish,
        out_shape=(jax.ShapeDtypeStruct((32, 8, 32), F32), jax.ShapeDtypeStruct((8, 32), F32)),
        in_specs=[vmem],
        out_specs=(vmem, vmem),
    )(pltpu.with_memory_space_constraint(home, pltpu.VMEM))
    return symbols, gain.T


def solution(mesh):
    placed = (
        P("ap", None),
        P("ap", None),
        P("ap", None),
        P("ap"),
        P("ap", "sc", None),
        P("ap", "sc", None),
    )
    return jax.shard_map(
        functools.partial(body, mesh.shape["ap"]),
        mesh=mesh,
        in_specs=placed,
        out_specs=(P("ap", "sc", None), P("ap", "sc")),
        check_vma=False,
    )
```

```python
import functools

import jax
import jax.numpy as jnp
from jax import lax
from jax.experimental import pallas as pl
from jax.experimental.pallas import tpu as pltpu
from jax.sharding import PartitionSpec as P

F32 = jnp.float32
BF16 = jnp.bfloat16
MESH = pl.DeviceIdType.MESH
PAIRS = [(0, 1), (0, 2), (0, 3), (1, 2), (1, 3), (2, 3)]
ENTRIES = [(i, i) for i in range(4)] + PAIRS
DIAGONAL = [8, 11, 9, 12]
REAL = dict(zip(PAIRS, [0, 1, 2, 3, 4, 10]))
IMAG = dict(zip(PAIRS, [16, 17, 18, 19, 20, 26]))
CODE = 24


def split(x, parts):
    out = []
    for _ in range(parts - 1):
        head = x.astype(BF16)
        out.append(head)
        x = x - head.astype(F32)
    out.append(x.astype(BF16))
    return out


def dot(a, b, rhs_transposed=False):
    dims = (((1,), (1,)), ((), ())) if rhs_transposed else (((1,), (0,)), ((), ()))
    return lax.dot_general(a, b, dims, preferred_element_type=F32)


def dot_split(a, b, parts, rhs_transposed=False):
    rows = a.shape[0]
    full = dot(jnp.concatenate(split(a, parts), 0), b, rhs_transposed)
    total = full[:rows]
    for p in range(1, parts):
        total = total + full[p * rows : (p + 1) * rows]
    return total


def get(h, i, j):
    if i == j:
        return h[i, i]
    if i < j:
        return h[i, j]
    re, im = h[j, i]
    return re, -im


def hermitian_inverse(h):
    h = dict(h)
    for k in range(4):
        inv = 1.0 / h[k, k][0]
        col = {i: get(h, i, k) for i in range(4) if i != k}
        scaled = {i: (c[0] * inv, c[1] * inv) for i, c in col.items()}
        new = {}
        for i, j in ENTRIES:
            if i == k and j == k:
                new[i, j] = (-inv, None)
            elif i == k:
                re, im = scaled[j]
                new[i, j] = (re, -im)
            elif j == k:
                new[i, j] = scaled[i]
            elif i == j:
                a, s = col[i], scaled[i]
                new[i, j] = (h[i, i][0] - (a[0] * s[0] + a[1] * s[1]), None)
            else:
                a, s = scaled[i], col[j]
                re = h[i, j][0] - (a[0] * s[0] + a[1] * s[1])
                im = h[i, j][1] - (a[1] * s[0] - a[0] * s[1])
                new[i, j] = (re, im)
        h = new
    return {k: (-v[0], None if v[1] is None else -v[1]) for k, v in h.items()}


def parts_of(h):
    out = [h[i, i][0] for i in range(4)]
    for p in PAIRS:
        out += list(h[p])
    return out


def from_parts(x):
    h = {(i, i): (x[i], None) for i in range(4)}
    for q, p in enumerate(PAIRS):
        h[p] = (x[4 + 2 * q], x[5 + 2 * q])
    return h


def add_products(acc, a, b):
    re, im = a[0] * b[0], None
    if a[1] is not None and b[1] is not None:
        re = re - a[1] * b[1]
    if b[1] is not None:
        im = a[0] * b[1]
    if a[1] is not None:
        im = a[1] * b[0] if im is None else im + a[1] * b[0]
    if acc is None:
        return re, im
    if im is None:
        im = acc[1]
    elif acc[1] is not None:
        im = acc[1] + im
    return acc[0] + re, im


def block_transpose(x):
    lane_block = lax.broadcasted_iota(jnp.int32, x[0].shape, 1) // 16
    x = list(x)
    for m in (1, 2, 4):
        upper = (lane_block & m) != 0
        new = list(x)
        for p in range(8):
            if p & m:
                continue
            q = p + m
            new[p] = jnp.where(upper, pltpu.roll(x[q], 16 * m, 1), x[p])
            new[q] = jnp.where(upper, x[q], pltpu.roll(x[p], 128 - 16 * m, 1))
        x = new
    return x


def lane_groups(x):
    lane_block = lax.broadcasted_iota(jnp.int32, x[0].shape, 1) // 32
    x = list(x)
    for m in (1, 2):
        upper = (lane_block & m) != 0
        new = list(x)
        for p in range(4):
            if p & m:
                continue
            q = p + m
            new[p] = jnp.where(upper, pltpu.roll(x[q], 32 * m, 1), x[p])
            new[q] = jnp.where(upper, x[q], pltpu.roll(x[p], 128 - 32 * m, 1))
        x = new
    return x


def kernel(
    n, cov_hbm, cl_hbm, valid_hbm, pilot_hbm, rp_hbm, rd_hbm, home,
    cov_ref, cl_ref, valid_ref, pilot_ref, rp_ref, rd_ref,
    send, recv, trans, pinv, obs, data, data_in, ones, gathered, held, out_p, in_p, out_w, in_w, back,
    root_data, root_held, out_r, root_in,
    load_sem, send_sem, recv_sem, data_send_sem, data_recv_sem,
    p_send_sem, p_recv_sem, w_send_sem, w_recv_sem, back_send_sem, back_recv_sem,
    root_send_sem, root_data_sem, root_recv_sem,
):
    me = lax.axis_index("ap")
    core = lax.axis_index("sc")
    rows = n // 4
    sets = n // 16
    groups = 4 * sets
    q, z = lax.div(me, rows), lax.rem(me, rows)

    pairs = [
        (cl_hbm, cl_ref), (valid_hbm, valid_ref), (pilot_hbm, pilot_ref),
        (cov_hbm, cov_ref), (rp_hbm, rp_ref), (rd_hbm, rd_ref),
    ]
    loads = [pltpu.make_async_copy(a, b, load_sem.at[i]) for i, (a, b) in enumerate(pairs)]
    odd = lax.rem(core, 2) == 1
    pair = core ^ 1
    even = jnp.logical_not(odd)
    root = jnp.logical_and(me == 0, even)
    far = jnp.logical_and(q == 3, even)
    barrier = pltpu.get_barrier_semaphore()

    def greet(p, c):
        pl.semaphore_signal(barrier, inc=1, device_id=(p, c), device_id_type=MESH)

    @pl.when(odd)
    def _():
        for load in loads[:4]:
            load.start()

        @pl.loop(1, n)
        def _(d):
            greet(me ^ (n - d), core)

    @pl.when(jnp.logical_not(odd))
    def _():
        @pl.loop(0, n)
        def _(d):
            greet(me ^ (n - 1 - d), pair)

        @pl.loop(1, rows)
        def _(d):
            greet(q * rows + (z ^ d), core)

        for d in range(1, 4):
            greet((q ^ d) * rows + z, core)

    @pl.when(root)
    def _():
        for load in loads[:2]:
            load.start()

        @pl.loop(1, rows)
        def _(c):
            greet(3 * rows + c, core)

    for load in loads[4:]:
        load.start()

    trans[...] = jnp.zeros_like(trans)
    ones[...] = jnp.zeros_like(ones)

    def slot_copy(p, slot, to):
        return pltpu.make_async_remote_copy(
            src_ref=send.at[p, 0:5], dst_ref=recv.at[slot, 0:5],
            send_sem=send_sem.at[lax.rem(to, 2), p], recv_sem=recv_sem.at[slot],
            device_id=(p, to), device_id_type=MESH,
        )

    def data_copy(p, slot):
        return pltpu.make_async_remote_copy(
            src_ref=data, dst_ref=data_in.at[slot],
            send_sem=data_send_sem.at[p], recv_sem=data_recv_sem.at[slot],
            device_id=(q * rows + p, core), device_id_type=MESH,
        )

    def p_copy(p, slot):
        return pltpu.make_async_remote_copy(
            src_ref=out_p.at[p], dst_ref=in_p.at[slot],
            send_sem=p_send_sem.at[p], recv_sem=p_recv_sem.at[slot],
            device_id=(q * rows + p, core), device_id_type=MESH,
        )

    def w_copy(p, slot):
        return pltpu.make_async_remote_copy(
            src_ref=out_w.at[p], dst_ref=in_w.at[slot],
            send_sem=w_send_sem.at[p], recv_sem=w_recv_sem.at[slot],
            device_id=(q * rows + p, core), device_id_type=MESH,
        )

    def root_data_copy(slot):
        return pltpu.make_async_remote_copy(
            src_ref=data, dst_ref=root_data.at[slot],
            send_sem=root_send_sem.at[0], recv_sem=root_data_sem.at[slot],
            device_id=(0, core), device_id_type=MESH,
        )

    def root_copy(slot):
        return pltpu.make_async_remote_copy(
            src_ref=out_r, dst_ref=root_in.at[slot],
            send_sem=root_send_sem.at[1], recv_sem=root_recv_sem.at[slot],
            device_id=(0, core), device_id_type=MESH,
        )

    def back_copy(p, slot):
        return pltpu.make_async_remote_copy(
            src_ref=back.at[p], dst_ref=home.at[slot],
            send_sem=back_send_sem.at[p], recv_sem=back_recv_sem.at[slot],
            device_id=(p * rows + z, core), device_id_type=MESH,
        )

    @pl.when(odd)
    def _():
        for load in loads[:4]:
            load.wait()
        wide = lambda x: jnp.concatenate([x] * 4, 1)
        cl = wide(cl_ref[...])
        code = jnp.where(
            wide(valid_ref[...]) > 0, (wide(pilot_ref[...]) * 16 + (cl & 15)).astype(F32) + 1.0, 0.0
        )
        owner = (cl >> 4) - lax.broadcasted_iota(jnp.int32, (16, 128), 1) // 32
        slots = []
        for a in range(4):
            part = cov_ref[:, 128 * a : 128 * a + 128]
            turned = jnp.concatenate([part] * 4, 0).T
            slots += [turned[32 * j : 32 * j + 32] for j in range(4)]
        row8 = lax.broadcasted_iota(jnp.int32, (8, 128), 0)
        for t in range(n // 4):
            tiles = [jnp.zeros((8, 128), F32)] * 4
            mark = jnp.zeros((8, 128), F32)
            for c in range(16):
                mine = jnp.broadcast_to(owner[c : c + 1], (8, 128)) == 4 * t
                tiles = [jnp.where(mine, slots[c][8 * v : 8 * v + 8], tiles[v]) for v in range(4)]
                mark = jnp.where(mine, jnp.broadcast_to(code[c : c + 1], (8, 128)), mark)
            first = jnp.broadcast_to(tiles[0][0:1], (8, 128))
            second = jnp.broadcast_to(tiles[0][5:6], (8, 128))
            tiles[1] = jnp.where(row8 == 1, first, jnp.where(row8 == 6, second, tiles[1]))
            tiles[3] = jnp.where(row8 == 1, mark, tiles[3])
            tiles = [jnp.where(row8 < 3, pltpu.roll(x, 7, 0), pltpu.roll(x, 5, 0)) for x in tiles]
            for j, tile in enumerate(lane_groups(tiles)):
                send[4 * t + j] = tile
        pl.semaphore_wait(barrier, 2 * n - 1)

        @pl.loop(0, n)
        def _(d):
            slot_copy(me ^ (n - 1 - d), me, pair).start()

        @pl.loop(1, n)
        def _(d):
            slot_copy(me ^ (n - d), me, core).start()

        recv[me] = send[me]

    extra = jnp.logical_and(far, z > 0)

    @pl.when(jnp.logical_and(even, extra))
    def _():
        pl.semaphore_wait(barrier, rows + 3)

    @pl.when(jnp.logical_and(even, jnp.logical_not(extra)))
    def _():
        pl.semaphore_wait(barrier, rows + 2)

    for load in loads[4:]:
        load.wait()
    turned = jnp.concatenate([rd_ref[:, f, :] for f in range(8)], 0).T.reshape(16, 8, 128)
    for f, tile in enumerate(block_transpose([turned[:, i, :] for i in range(8)])):
        data[:, f, :] = tile

    @pl.loop(1, rows)
    def _(d):
        data_copy(lax.rem(z + d, rows), z).start()

    @pl.when(far)
    def _():
        root_data_copy(z).start()

    turned = jnp.concatenate([rp_ref[:, f, :] for f in range(8)], 0).T
    for half in range(2):
        tiles = [turned[8 * (8 * half + t) : 8 * (8 * half + t) + 8] for t in range(8)]
        for f, tile in enumerate(block_transpose(tiles)):
            obs[f, :, 128 * half : 128 * half + 128] = tile
    observed = jnp.concatenate([obs[:, i, :] for i in range(8)], 0)
    observed = jnp.concatenate(split(observed, 3), 0)

    @pl.loop(1, n)
    def _(d):
        p = me ^ d
        slot_copy(p, p, pair).wait_recv()

    @pl.when(jnp.logical_not(odd))
    def _():
        slot_copy(me, me, pair).wait_recv()


    row32 = lax.broadcasted_iota(jnp.int32, (32, 128), 0)
    codes, matrices = [], []
    for e in range(sets):
        for j in range(4):
            tiles = lane_groups([recv[h * rows + 4 * e + j] for h in range(4)])
            for v, tile in enumerate(tiles):
                trans[e, j, 8 * v : 8 * v + 5] = tile[0:5]
            codes.append(tiles[3][0:1])
            matrices.append(jnp.where(row32 == CODE, 0.0, trans[e, j]))
    codes = jnp.concatenate(codes, 1) - 1.0
    matrices = jnp.concatenate(matrices, 1)
    width = 128 * groups
    bins = lax.broadcasted_iota(jnp.int32, (256, width), 0).astype(F32)
    choose = jnp.where(bins == codes, 1.0, 0.0).astype(BF16)
    places = jnp.where(codes >= 0.0, codes - 16.0 * jnp.floor(codes * 0.0625), -1.0)
    ap_rows = (lax.broadcasted_iota(jnp.int32, (128, width), 0) & 15).astype(F32)
    pick = jnp.where(ap_rows == places, 1.0, 0.0).astype(BF16)
    for g in range(groups):
        out_p[g] = jnp.broadcast_to(places[:, 128 * g : 128 * g + 128], (8, 128))

        @pl.when(z != g)
        def _():
            p_copy(g, z).start()

    psi = dot_split(matrices, choose, 3, True)
    hermitian = {(i, i): (psi[r : r + 1] + 1.0, None) for i, r in enumerate(DIAGONAL)}
    hermitian.update({p: (psi[REAL[p] : REAL[p] + 1], psi[IMAG[p] : IMAG[p] + 1]) for p in PAIRS})
    inverse = jnp.concatenate(parts_of(hermitian_inverse(hermitian)), 0)
    slot_inverse = dot_split(inverse, choose, 3)
    slot_obs = dot(observed, choose)
    slot_obs = slot_obs[0:64] + slot_obs[64:128] + slot_obs[128:192]

    estimates, outers = [], []
    for e in range(sets):
        for j in range(4):
            g = 4 * e + j
            pinv[j] = slot_inverse[:, 128 * g : 128 * g + 128]
        pi = from_parts([pinv[:, x, :] for x in range(16)])
        r = {(i, i): (trans[e, :, DIAGONAL[i], :], None) for i in range(4)}
        for p in PAIRS:
            r[p] = (trans[e, :, REAL[p], :], trans[e, :, IMAG[p], :])
        w = {}
        for i in range(4):
            for k in range(4):
                acc = None
                for l in range(4):
                    acc = add_products(acc, get(r, i, l), get(pi, l, k))
                w[i, k] = acc
        err = {}
        for i, k in ENTRIES:
            acc = None
            for l in range(4):
                acc = add_products(acc, w[i, l], get(r, l, k))
            re = r[i, k][0] - acc[0]
            err[i, k] = (re, None) if i == k else (re, r[i, k][1] - acc[1])
        for j in range(4):
            g = 4 * e + j
            cols = slice(128 * g, 128 * g + 128)
            y = [(slot_obs[8 * i : 8 * i + 8, cols], slot_obs[32 + 8 * i : 40 + 8 * i, cols]) for i in range(4)]
            h = []
            for i in range(4):
                acc = None
                for k in range(4):
                    wr, wi = w[i, k]
                    acc = add_products(acc, (wr[j : j + 1], wi[j : j + 1]), y[k])
                h.append(acc)
            estimates.append(h)
            out = []
            for i in range(4):
                out.append(h[i][0] * h[i][0] + h[i][1] * h[i][1] + err[i, i][0][j : j + 1])
            for i, k in PAIRS:
                out.append(h[i][0] * h[k][0] + h[i][1] * h[k][1] + err[i, k][0][j : j + 1])
                out.append(h[i][1] * h[k][0] - h[i][0] * h[k][1] + err[i, k][1][j : j + 1])
            outers.append(jnp.concatenate(out, 0))
    summed = dot_split(jnp.concatenate(outers, 1), pick, 3, True)
    own_f = lax.broadcasted_iota(jnp.int32, (8, 128), 1) // 16 == lax.broadcasted_iota(jnp.int32, (8, 128), 0)
    comps = [
        jnp.sum(jnp.where(own_f, summed[8 * x : 8 * x + 8], 0.0), 0, keepdims=True) for x in range(16)
    ]
    weight = hermitian_inverse(from_parts([c + 1.0 if x < 4 else c for x, c in enumerate(comps)]))

    masked = jnp.concatenate([jnp.where(own_f, c, 0.0) for c in parts_of(weight)], 0)
    slot_weight = dot_split(masked, pick, 3)
    for g in range(groups):
        cols = slice(128 * g, 128 * g + 128)
        h = estimates[g]
        gs = from_parts([slot_weight[8 * x : 8 * x + 8, cols] for x in range(16)])
        for i in range(4):
            gs[i, i] = (gs[i, i][0], None)
        power = None
        for i in range(4):
            acc = None
            for k in range(4):
                acc = add_products(acc, get(gs, i, k), h[k])
            out_w[g, 8 * i : 8 * i + 8] = acc[0]
            out_w[g, 32 + 8 * i : 40 + 8 * i] = acc[1]
            term = h[i][0] * acc[0] + h[i][1] * acc[1]
            power = term if power is None else power + term
        out_w[g, 64:72] = power

        if g == 0:
            @pl.when(far)
            def _():
                quarter = lax.broadcasted_iota(jnp.int32, (8, 128), 1) // 32
                for m in range(2):
                    packed = out_w[0, 32 * m : 32 * m + 8]
                    for j in range(1, 4):
                        at = 32 * m + 8 * j
                        packed = jnp.where(quarter == j, pltpu.roll(out_w[0, at : at + 8], 32 * j, 1), packed)
                    out_r[8 * m : 8 * m + 8] = packed
                out_r[16:24] = out_w[0, 64:72]
                root_copy(z).start()

        @pl.when(z != g)
        def _():
            w_copy(g, z).start()

    row16 = lax.broadcasted_iota(jnp.int32, (16, 128), 0).astype(F32)
    in_p[z] = out_p[z]
    in_w[z] = out_w[z]
    for k in range(rows):
        p = z ^ k
        if k > 0:
            data_copy(p, p).wait_recv()
            p_copy(p, p).wait_recv()
        place = in_p[p]
        hot = jnp.where(row16 == jnp.concatenate([place, place], 0), 1.0, 0.0).astype(BF16)
        for i in range(8):
            for half in range(2):
                at = 128 * half + 16 * i
                ones[k % 2, at : at + 16, 128 * i : 128 * i + 128] = hot
        source = (data[...] if k == 0 else data_in[p]).reshape(128, 128)
        left = jnp.concatenate(split(source, 2), 1)
        for i in range(4):
            cols = slice(256 * i, 256 * i + 256)
            wide_out = dot(left, ones[k % 2, :, cols])
            gathered[k, 2 * i] = wide_out[:, :128].reshape(16, 8, 128)
            gathered[k, 2 * i + 1] = wide_out[:, 128:].reshape(16, 8, 128)

    sums = [None] * 32
    power = None
    for k in range(rows):
        p = z ^ k
        if k > 0:
            w_copy(p, p).wait_recv()
        u = [in_w[p, 8 * i : 8 * i + 8] for i in range(8)]
        part = in_w[p, 64:72]
        power = part if power is None else power + part
        for s in range(16):
            d = [gathered[k, i, s] for i in range(8)]
            re = im = None
            for i in range(4):
                x = u[i] * d[i] + u[i + 4] * d[i + 4]
                y = u[i] * d[i + 4] - u[i + 4] * d[i]
                re = x if re is None else re + x
                im = y if im is None else im + y
            sums[2 * s] = re if k == 0 else sums[2 * s] + re
            sums[2 * s + 1] = im if k == 0 else sums[2 * s + 1] + im
    for s in range(32):
        held[s] = sums[s]
    for half in range(2):
        tile = jnp.concatenate([held[:, 4 * half + f, :] for f in range(4)], 0).T.reshape(4, 4, 8, 128)
        for j in range(4):
            back[:, 2 * j + half] = tile[:, j]
    turned = jnp.concatenate([power, jnp.zeros((120, 128), F32)], 0).T.reshape(4, 4, 8, 128)
    gains = turned[:, 0].reshape(32, 128)
    for j in range(1, 4):
        gains = gains + pltpu.roll(turned[:, j].reshape(32, 128), 8 * j, 1)
    back[:, 8] = gains.reshape(4, 8, 128)

    to_root = lambda p: jnp.logical_and(p == 0, jnp.logical_and(z == 0, far))
    for k in range(1, 4):
        p = lax.rem(q + k, 4)

        @pl.when(jnp.logical_not(to_root(p)))
        def _():
            back_copy(p, q).start()

    @pl.when(root)
    def _():
        for load in loads[:2]:
            load.wait()
        cl = jnp.concatenate([cl_ref[...]] * 4, 1)
        valid = jnp.concatenate([valid_ref[...]] * 4, 1)
        mark = jnp.where(valid > 0, (cl & 15).astype(F32) + 1.0, 0.0)
        owner = cl >> 4
        row = lax.broadcasted_iota(jnp.int32, (128, 128), 0)
        quarter = lax.broadcasted_iota(jnp.int32, (128, 128), 1) // 32
        base = jnp.where(((row >> 4) & 3) == quarter, ((row & 15) + 1).astype(F32), -1.0)
        for p in range(rows):
            place = jnp.sum(jnp.where(owner == 3 * rows + p, mark, 0.0), 0, keepdims=True)
            hot = jnp.where(base == place, 1.0, 0.0)
            hot = jnp.concatenate(
                [jnp.where(row < 64, hot, 0.0), jnp.where(row < 64, 0.0, hot)], 1
            ).astype(BF16)
            root_data_copy(p).wait_recv()
            left = jnp.concatenate(split(root_data[p].reshape(128, 128), 2), 1)
            both = dot(left, jnp.concatenate([hot, hot], 0))
            for m in range(2):
                root_held[p, m] = both[:, 128 * m : 128 * m + 128].reshape(16, 8, 128)
        sums = [None] * 32
        power = None
        for p in range(rows):
            root_copy(p).wait_recv()
            u, v, part = (root_in[p, 8 * m : 8 * m + 8] for m in range(3))
            power = part if p == 0 else power + part
            for s in range(16):
                x, y = root_held[p, 0, s], root_held[p, 1, s]
                re, im = u * x + v * y, u * y - v * x
                sums[2 * s] = re if p == 0 else sums[2 * s] + re
                sums[2 * s + 1] = im if p == 0 else sums[2 * s + 1] + im
        for s in range(32):
            x = sums[s] + pltpu.roll(sums[s], 64, 1)
            held[s] = x + pltpu.roll(x, 32, 1)
        for half in range(2):
            tile = jnp.concatenate([held[:, 4 * half + f, :] for f in range(4)], 0).T
            for j in range(4):
                home[3, 2 * j + half] = tile[8 * j : 8 * j + 8]
        turned = jnp.concatenate([power, jnp.zeros((120, 128), F32)], 0).T
        gains = turned[0:8]
        for j in range(1, 4):
            gains = gains + pltpu.roll(turned[8 * j : 8 * j + 8], 8 * j, 1)
        home[3, 8] = gains

    home[q] = back[q]
    for k in range(1, 4):
        p = lax.rem(q + k, 4)

        @pl.when(jnp.logical_not(jnp.logical_and(root, p == 3)))
        def _():
            back_copy(p, p).wait_recv()

    @pl.when(odd)
    def _():
        @pl.loop(1, n)
        def _(k):
            p = me ^ k
            slot_copy(p, p, pair).wait_send()
            slot_copy(p, p, core).wait_send()

        slot_copy(me, me, pair).wait_send()

    @pl.loop(1, rows)
    def _(k):
        p = lax.rem(z + k, rows)
        data_copy(p, p).wait_send()
        p_copy(p, p).wait_send()
        w_copy(p, p).wait_send()

    for k in range(1, 4):
        p = lax.rem(q + k, 4)

        @pl.when(jnp.logical_not(to_root(p)))
        def _():
            back_copy(p, p).wait_send()

    @pl.when(far)
    def _():
        root_data_copy(z).wait_send()
        root_copy(z).wait_send()


def finish(home, sym_ref, gain_ref):
    total = (home[0] + home[1]) + (home[2] + home[3])
    for j in range(4):
        for f in range(8):
            tile = total[2 * j + f // 4]
            sym_ref[8 * j : 8 * j + 8, f, :] = tile[:, 32 * (f % 4) : 32 * (f % 4) + 32]
    gains = jnp.concatenate([total[8], jnp.zeros((120, 128), F32)], 0).T
    gain_ref[...] = jnp.concatenate([gains[8 * j : 8 * j + 8, 0:8] for j in range(4)], 1)


def body(n, covariances, clusters, cluster_valid, pilots, received_pilot, received_data):
    vmem = pl.BlockSpec(memory_space=pltpu.VMEM)
    rows = n // 4
    home = pl.pallas_call(
        functools.partial(kernel, n),
        out_shape=pltpu.VMEM((4, 9, 8, 128), F32),
        in_specs=[pl.BlockSpec(memory_space=pltpu.HBM)] * 6,
        out_specs=vmem,
        scratch_shapes=[
            pltpu.VMEM((32, 512), F32),
            pltpu.VMEM((16, 32), jnp.int32),
            pltpu.VMEM((16, 32), jnp.int32),
            pltpu.VMEM((1, 32), jnp.int32),
            pltpu.VMEM((16, 8, 128), F32),
            pltpu.VMEM((16, 8, 128), F32),
            pltpu.VMEM((n, 8, 128), F32),
            pltpu.VMEM((n, 8, 128), F32),
            pltpu.VMEM((n // 16, 4, 32, 128), F32),
            pltpu.VMEM((4, 16, 128), F32),
            pltpu.VMEM((8, 8, 256), F32),
            pltpu.VMEM((16, 8, 128), F32),
            pltpu.VMEM((rows, 16, 8, 128), F32),
            pltpu.VMEM((2, 256, 1024), BF16),
            pltpu.VMEM((rows, 8, 16, 8, 128), F32),
            pltpu.VMEM((32, 8, 128), F32),
            pltpu.VMEM((rows, 8, 128), F32),
            pltpu.VMEM((rows, 8, 128), F32),
            pltpu.VMEM((rows, 72, 128), F32),
            pltpu.VMEM((rows, 72, 128), F32),
            pltpu.VMEM((4, 9, 8, 128), F32),
            pltpu.VMEM((rows, 16, 8, 128), F32),
            pltpu.VMEM((rows, 2, 16, 8, 128), F32),
            pltpu.VMEM((24, 128), F32),
            pltpu.VMEM((rows, 24, 128), F32),
            pltpu.SemaphoreType.DMA((6,)),
            pltpu.SemaphoreType.DMA((2, n)),
            pltpu.SemaphoreType.DMA((n,)),
            pltpu.SemaphoreType.DMA((rows,)),
            pltpu.SemaphoreType.DMA((rows,)),
            pltpu.SemaphoreType.DMA((rows,)),
            pltpu.SemaphoreType.DMA((rows,)),
            pltpu.SemaphoreType.DMA((rows,)),
            pltpu.SemaphoreType.DMA((rows,)),
            pltpu.SemaphoreType.DMA((4,)),
            pltpu.SemaphoreType.DMA((4,)),
            pltpu.SemaphoreType.DMA((2,)),
            pltpu.SemaphoreType.DMA((rows,)),
            pltpu.SemaphoreType.DMA((rows,)),
        ],
        compiler_params=pltpu.CompilerParams(
            collective_id=0, has_side_effects=True, vmem_limit_bytes=65000 * 1024
        ),
    )(covariances, clusters.T, cluster_valid.T, pilots.reshape(1, -1), received_pilot, received_data)
    symbols, gain = pl.pallas_call(
        finish,
        out_shape=(jax.ShapeDtypeStruct((32, 8, 32), F32), jax.ShapeDtypeStruct((8, 32), F32)),
        in_specs=[vmem],
        out_specs=(vmem, vmem),
    )(pltpu.with_memory_space_constraint(home, pltpu.VMEM))
    return symbols, gain.T


def solution(mesh):
    placed = (
        P("ap", None),
        P("ap", None),
        P("ap", None),
        P("ap"),
        P("ap", "sc", None),
        P("ap", "sc", None),
    )
    return jax.shard_map(
        functools.partial(body, mesh.shape["ap"]),
        mesh=mesh,
        in_specs=placed,
        out_specs=(P("ap", "sc", None), P("ap", "sc")),
        check_vma=False,
    )
```

```python
import functools

import jax
import jax.numpy as jnp
from jax import lax
from jax.experimental import pallas as pl
from jax.experimental.pallas import tpu as pltpu
from jax.sharding import PartitionSpec as P

F32 = jnp.float32
BF16 = jnp.bfloat16
MESH = pl.DeviceIdType.MESH
PAIRS = [(0, 1), (0, 2), (0, 3), (1, 2), (1, 3), (2, 3)]
ENTRIES = [(i, i) for i in range(4)] + PAIRS
DIAGONAL = [8, 11, 9, 12]
REAL = dict(zip(PAIRS, [0, 1, 2, 3, 4, 10]))
IMAG = dict(zip(PAIRS, [16, 17, 18, 19, 20, 26]))
CODE = 24


def split(x, parts):
    out = []
    for _ in range(parts - 1):
        head = x.astype(BF16)
        out.append(head)
        x = x - head.astype(F32)
    out.append(x.astype(BF16))
    return out


def dot(a, b, rhs_transposed=False):
    dims = (((1,), (1,)), ((), ())) if rhs_transposed else (((1,), (0,)), ((), ()))
    return lax.dot_general(a, b, dims, preferred_element_type=F32)


def dot_split(a, b, parts, rhs_transposed=False):
    rows = a.shape[0]
    full = dot(jnp.concatenate(split(a, parts), 0), b, rhs_transposed)
    total = full[:rows]
    for p in range(1, parts):
        total = total + full[p * rows : (p + 1) * rows]
    return total


def get(h, i, j):
    if i == j:
        return h[i, i]
    if i < j:
        return h[i, j]
    re, im = h[j, i]
    return re, -im


def hermitian_inverse(h):
    h = dict(h)
    for k in range(4):
        inv = 1.0 / h[k, k][0]
        col = {i: get(h, i, k) for i in range(4) if i != k}
        scaled = {i: (c[0] * inv, c[1] * inv) for i, c in col.items()}
        new = {}
        for i, j in ENTRIES:
            if i == k and j == k:
                new[i, j] = (-inv, None)
            elif i == k:
                re, im = scaled[j]
                new[i, j] = (re, -im)
            elif j == k:
                new[i, j] = scaled[i]
            elif i == j:
                a, s = col[i], scaled[i]
                new[i, j] = (h[i, i][0] - (a[0] * s[0] + a[1] * s[1]), None)
            else:
                a, s = scaled[i], col[j]
                re = h[i, j][0] - (a[0] * s[0] + a[1] * s[1])
                im = h[i, j][1] - (a[1] * s[0] - a[0] * s[1])
                new[i, j] = (re, im)
        h = new
    return {k: (-v[0], None if v[1] is None else -v[1]) for k, v in h.items()}


def from_parts(x):
    h = {(i, i): (x[i], None) for i in range(4)}
    for q, p in enumerate(PAIRS):
        h[p] = (x[4 + 2 * q], x[5 + 2 * q])
    return h


def add_products(acc, a, b):
    re, im = a[0] * b[0], None
    if a[1] is not None and b[1] is not None:
        re = re - a[1] * b[1]
    if b[1] is not None:
        im = a[0] * b[1]
    if a[1] is not None:
        im = a[1] * b[0] if im is None else im + a[1] * b[0]
    if acc is None:
        return re, im
    if im is None:
        im = acc[1]
    elif acc[1] is not None:
        im = acc[1] + im
    return acc[0] + re, im


def block_transpose(x):
    lane_block = lax.broadcasted_iota(jnp.int32, x[0].shape, 1) // 16
    x = list(x)
    for m in (1, 2, 4):
        upper = (lane_block & m) != 0
        new = list(x)
        for p in range(8):
            if p & m:
                continue
            q = p + m
            new[p] = jnp.where(upper, pltpu.roll(x[q], 16 * m, 1), x[p])
            new[q] = jnp.where(upper, x[q], pltpu.roll(x[p], 128 - 16 * m, 1))
        x = new
    return x


def lane_groups(x):
    lane_block = lax.broadcasted_iota(jnp.int32, x[0].shape, 1) // 32
    x = list(x)
    for m in (1, 2):
        upper = (lane_block & m) != 0
        new = list(x)
        for p in range(4):
            if p & m:
                continue
            q = p + m
            new[p] = jnp.where(upper, pltpu.roll(x[q], 32 * m, 1), x[p])
            new[q] = jnp.where(upper, x[q], pltpu.roll(x[p], 128 - 32 * m, 1))
        x = new
    return x


def kernel(
    n, cov_hbm, cl_hbm, valid_hbm, pilot_hbm, rp_hbm, rd_hbm, home,
    cov_ref, cl_ref, valid_ref, pilot_ref, rp_ref, rd_ref,
    send, recv, trans, pinv, obs, data, data_in, ones, gathered, held, out_p, in_p, out_w, in_w, back,
    root_data, root_held, out_r, root_in,
    load_sem, send_sem, recv_sem, data_send_sem, data_recv_sem,
    p_send_sem, p_recv_sem, w_send_sem, w_recv_sem, back_send_sem, back_recv_sem,
    root_send_sem, root_data_sem, root_recv_sem,
):
    me = lax.axis_index("ap")
    core = lax.axis_index("sc")
    rows = n // 4
    sets = n // 16
    groups = 4 * sets
    q, z = lax.div(me, rows), lax.rem(me, rows)

    pairs = [
        (cl_hbm, cl_ref), (valid_hbm, valid_ref), (pilot_hbm, pilot_ref),
        (cov_hbm, cov_ref), (rp_hbm, rp_ref), (rd_hbm, rd_ref),
    ]
    loads = [pltpu.make_async_copy(a, b, load_sem.at[i]) for i, (a, b) in enumerate(pairs)]
    odd = lax.rem(core, 2) == 1
    pair = core ^ 1
    even = jnp.logical_not(odd)
    root = jnp.logical_and(me == 0, even)
    far = jnp.logical_and(q == 3, even)
    barrier = pltpu.get_barrier_semaphore()

    def greet(p, c):
        pl.semaphore_signal(barrier, inc=1, device_id=(p, c), device_id_type=MESH)

    @pl.when(odd)
    def _():
        for load in loads[:4]:
            load.start()

        @pl.loop(1, n)
        def _(d):
            greet(me ^ (n - d), core)

    @pl.when(jnp.logical_not(odd))
    def _():
        @pl.loop(0, n)
        def _(d):
            greet(me ^ (n - 1 - d), pair)

        @pl.loop(1, rows)
        def _(d):
            greet(q * rows + (z ^ d), core)

        for d in range(1, 4):
            greet((q ^ d) * rows + z, core)

    @pl.when(root)
    def _():
        for load in loads[:2]:
            load.start()

        @pl.loop(1, rows)
        def _(c):
            greet(3 * rows + c, core)

    for load in loads[4:]:
        load.start()

    trans[...] = jnp.zeros_like(trans)
    ones[...] = jnp.zeros_like(ones)

    def slot_copy(p, slot, to):
        return pltpu.make_async_remote_copy(
            src_ref=send.at[p, 0:5], dst_ref=recv.at[slot, 0:5],
            send_sem=send_sem.at[lax.rem(to, 2), p], recv_sem=recv_sem.at[slot],
            device_id=(p, to), device_id_type=MESH,
        )

    def data_copy(p, slot):
        return pltpu.make_async_remote_copy(
            src_ref=data, dst_ref=data_in.at[slot],
            send_sem=data_send_sem.at[p], recv_sem=data_recv_sem.at[slot],
            device_id=(q * rows + p, core), device_id_type=MESH,
        )

    def p_copy(p, slot):
        return pltpu.make_async_remote_copy(
            src_ref=out_p.at[p], dst_ref=in_p.at[slot],
            send_sem=p_send_sem.at[p], recv_sem=p_recv_sem.at[slot],
            device_id=(q * rows + p, core), device_id_type=MESH,
        )

    def w_copy(p, slot):
        return pltpu.make_async_remote_copy(
            src_ref=out_w.at[p], dst_ref=in_w.at[slot],
            send_sem=w_send_sem.at[p], recv_sem=w_recv_sem.at[slot],
            device_id=(q * rows + p, core), device_id_type=MESH,
        )

    def root_data_copy(slot):
        return pltpu.make_async_remote_copy(
            src_ref=data, dst_ref=root_data.at[slot],
            send_sem=root_send_sem.at[0], recv_sem=root_data_sem.at[slot],
            device_id=(0, core), device_id_type=MESH,
        )

    def root_copy(slot):
        return pltpu.make_async_remote_copy(
            src_ref=out_r, dst_ref=root_in.at[slot],
            send_sem=root_send_sem.at[1], recv_sem=root_recv_sem.at[slot],
            device_id=(0, core), device_id_type=MESH,
        )

    def back_copy(p, slot):
        return pltpu.make_async_remote_copy(
            src_ref=back.at[p], dst_ref=home.at[slot],
            send_sem=back_send_sem.at[p], recv_sem=back_recv_sem.at[slot],
            device_id=(p * rows + z, core), device_id_type=MESH,
        )

    @pl.when(odd)
    def _():
        for load in loads[:4]:
            load.wait()
        wide = lambda x: jnp.concatenate([x] * 4, 1)
        cl = wide(cl_ref[...])
        code = jnp.where(
            wide(valid_ref[...]) > 0, (wide(pilot_ref[...]) * 16 + (cl & 15)).astype(F32) + 1.0, 0.0
        )
        owner = (cl >> 4) - lax.broadcasted_iota(jnp.int32, (16, 128), 1) // 32
        slots = []
        for a in range(4):
            part = cov_ref[:, 128 * a : 128 * a + 128]
            turned = jnp.concatenate([part] * 4, 0).T
            slots += [turned[32 * j : 32 * j + 32] for j in range(4)]
        row8 = lax.broadcasted_iota(jnp.int32, (8, 128), 0)
        for t in range(n // 4):
            tiles = [jnp.zeros((8, 128), F32)] * 4
            mark = jnp.zeros((8, 128), F32)
            for c in range(16):
                mine = jnp.broadcast_to(owner[c : c + 1], (8, 128)) == 4 * t
                tiles = [jnp.where(mine, slots[c][8 * v : 8 * v + 8], tiles[v]) for v in range(4)]
                mark = jnp.where(mine, jnp.broadcast_to(code[c : c + 1], (8, 128)), mark)
            first = jnp.broadcast_to(tiles[0][0:1], (8, 128))
            second = jnp.broadcast_to(tiles[0][5:6], (8, 128))
            tiles[1] = jnp.where(row8 == 1, first, jnp.where(row8 == 6, second, tiles[1]))
            tiles[3] = jnp.where(row8 == 1, mark, tiles[3])
            tiles = [jnp.where(row8 < 3, pltpu.roll(x, 7, 0), pltpu.roll(x, 5, 0)) for x in tiles]
            for j, tile in enumerate(lane_groups(tiles)):
                send[4 * t + j] = tile
        pl.semaphore_wait(barrier, 2 * n - 1)

        @pl.loop(0, n)
        def _(d):
            slot_copy(me ^ (n - 1 - d), me, pair).start()

        @pl.loop(1, n)
        def _(d):
            slot_copy(me ^ (n - d), me, core).start()

        recv[me] = send[me]

    extra = jnp.logical_and(far, z > 0)

    @pl.when(jnp.logical_and(even, extra))
    def _():
        pl.semaphore_wait(barrier, rows + 3)

    @pl.when(jnp.logical_and(even, jnp.logical_not(extra)))
    def _():
        pl.semaphore_wait(barrier, rows + 2)

    for load in loads[4:]:
        load.wait()
    turned = jnp.concatenate([rd_ref[:, f, :] for f in range(8)], 0).T.reshape(16, 8, 128)
    for f, tile in enumerate(block_transpose([turned[:, i, :] for i in range(8)])):
        data[:, f, :] = tile

    @pl.loop(1, rows)
    def _(d):
        data_copy(lax.rem(z + d, rows), z).start()

    @pl.when(far)
    def _():
        root_data_copy(z).start()

    turned = jnp.concatenate([rp_ref[:, f, :] for f in range(8)], 0).T
    for half in range(2):
        tiles = [turned[8 * (8 * half + t) : 8 * (8 * half + t) + 8] for t in range(8)]
        for f, tile in enumerate(block_transpose(tiles)):
            obs[f, :, 128 * half : 128 * half + 128] = tile
    observed = jnp.concatenate([obs[:, i, :] for i in range(8)], 0)
    observed = jnp.concatenate(split(observed, 3), 0)

    @pl.loop(1, n)
    def _(d):
        p = me ^ d
        slot_copy(p, p, pair).wait_recv()

    @pl.when(jnp.logical_not(odd))
    def _():
        slot_copy(me, me, pair).wait_recv()


    row32 = lax.broadcasted_iota(jnp.int32, (32, 128), 0)
    codes, matrices = [], []
    for e in range(sets):
        for j in range(4):
            tiles = lane_groups([recv[h * rows + 4 * e + j] for h in range(4)])
            for v, tile in enumerate(tiles):
                trans[e, j, 8 * v : 8 * v + 5] = tile[0:5]
            codes.append(tiles[3][0:1])
            matrices.append(jnp.where(row32 == CODE, 0.0, trans[e, j]))
    codes = jnp.concatenate(codes, 1) - 1.0
    matrices = jnp.concatenate(matrices, 1)
    width = 128 * groups
    bins = lax.broadcasted_iota(jnp.int32, (256, width), 0).astype(F32)
    choose = jnp.where(bins == codes, 1.0, 0.0).astype(BF16)
    places = jnp.where(codes >= 0.0, codes - 16.0 * jnp.floor(codes * 0.0625), -1.0)
    ap_rows = (lax.broadcasted_iota(jnp.int32, (128, width), 0) & 15).astype(F32)
    pick = jnp.where(ap_rows == places, 1.0, 0.0).astype(BF16)
    for g in range(groups):
        out_p[g] = jnp.broadcast_to(places[:, 128 * g : 128 * g + 128], (8, 128))

        @pl.when(z != g)
        def _():
            p_copy(g, z).start()

    if sets == 1:
        rest = jnp.zeros((124, 128), F32)
        column = jnp.concatenate([codes[:, 128 * j : 128 * j + 128] for j in range(4)] + [rest], 0).T
        column_places = jnp.where(column >= 0.0, column - 16.0 * jnp.floor(column * 0.0625), -1.0)

        def alike(x, y):
            blocks = [jnp.where(x[:, j : j + 1] == y, 1.0, 0.0).astype(BF16) for j in range(4)]
            return jnp.concatenate(blocks, 0)

        slot_psi = dot_split(matrices, alike(column, codes), 3)
    else:
        slot_psi = dot_split(dot_split(matrices, choose, 3, True), choose, 3)
    slot_obs = dot(observed, choose)
    slot_obs = slot_obs[0:64] + slot_obs[64:128] + slot_obs[128:192]

    estimates, outers = [], []
    for e in range(sets):
        for j in range(4):
            g = 4 * e + j
            pinv[j] = slot_psi[:, 128 * g : 128 * g + 128]
        psi = {(i, i): (pinv[:, DIAGONAL[i], :] + 1.0, None) for i in range(4)}
        psi.update({p: (pinv[:, REAL[p], :], pinv[:, IMAG[p], :]) for p in PAIRS})
        pi = hermitian_inverse(psi)
        r = {(i, i): (trans[e, :, DIAGONAL[i], :], None) for i in range(4)}
        for p in PAIRS:
            r[p] = (trans[e, :, REAL[p], :], trans[e, :, IMAG[p], :])
        w = {}
        for i in range(4):
            for k in range(4):
                acc = None
                for l in range(4):
                    acc = add_products(acc, get(r, i, l), get(pi, l, k))
                w[i, k] = acc
        err = {}
        for i, k in ENTRIES:
            acc = None
            for l in range(4):
                acc = add_products(acc, w[i, l], get(r, l, k))
            re = r[i, k][0] - acc[0]
            err[i, k] = (re, None) if i == k else (re, r[i, k][1] - acc[1])
        for j in range(4):
            g = 4 * e + j
            cols = slice(128 * g, 128 * g + 128)
            y = [(slot_obs[8 * i : 8 * i + 8, cols], slot_obs[32 + 8 * i : 40 + 8 * i, cols]) for i in range(4)]
            h = []
            for i in range(4):
                acc = None
                for k in range(4):
                    wr, wi = w[i, k]
                    acc = add_products(acc, (wr[j : j + 1], wi[j : j + 1]), y[k])
                h.append(acc)
            estimates.append(h)
            out = []
            for i in range(4):
                out.append(h[i][0] * h[i][0] + h[i][1] * h[i][1] + err[i, i][0][j : j + 1])
            for i, k in PAIRS:
                out.append(h[i][0] * h[k][0] + h[i][1] * h[k][1] + err[i, k][0][j : j + 1])
                out.append(h[i][1] * h[k][0] - h[i][0] * h[k][1] + err[i, k][1][j : j + 1])
            outers.append(jnp.concatenate(out, 0))
    outers = jnp.concatenate(outers, 1)
    if sets == 1:
        slot_sum = dot_split(outers, alike(column_places, places), 3)
    else:
        summed = dot_split(outers, pick, 3, True)
        own_f = lax.broadcasted_iota(jnp.int32, (8, 128), 1) // 16 == lax.broadcasted_iota(jnp.int32, (8, 128), 0)
        comps = [
            jnp.sum(jnp.where(own_f, summed[8 * x : 8 * x + 8], 0.0), 0, keepdims=True) for x in range(16)
        ]
        masked = jnp.concatenate([jnp.where(own_f, c, 0.0) for c in comps], 0)
        slot_sum = dot_split(masked, pick, 3)
    for g in range(groups):
        cols = slice(128 * g, 128 * g + 128)
        h = estimates[g]
        parts = [slot_sum[8 * x : 8 * x + 8, cols] for x in range(16)]
        gs = hermitian_inverse(from_parts([c + 1.0 if x < 4 else c for x, c in enumerate(parts)]))
        power = None
        for i in range(4):
            acc = None
            for k in range(4):
                acc = add_products(acc, get(gs, i, k), h[k])
            out_w[g, 8 * i : 8 * i + 8] = acc[0]
            out_w[g, 32 + 8 * i : 40 + 8 * i] = acc[1]
            term = h[i][0] * acc[0] + h[i][1] * acc[1]
            power = term if power is None else power + term
        out_w[g, 64:72] = power

        if g == 0:
            @pl.when(far)
            def _():
                quarter = lax.broadcasted_iota(jnp.int32, (8, 128), 1) // 32
                for m in range(2):
                    packed = out_w[0, 32 * m : 32 * m + 8]
                    for j in range(1, 4):
                        at = 32 * m + 8 * j
                        packed = jnp.where(quarter == j, pltpu.roll(out_w[0, at : at + 8], 32 * j, 1), packed)
                    out_r[8 * m : 8 * m + 8] = packed
                out_r[16:24] = out_w[0, 64:72]
                root_copy(z).start()

        @pl.when(z != g)
        def _():
            w_copy(g, z).start()

    row16 = lax.broadcasted_iota(jnp.int32, (16, 128), 0).astype(F32)
    in_p[z] = out_p[z]
    in_w[z] = out_w[z]
    for k in range(rows):
        p = z ^ k
        if k > 0:
            data_copy(p, p).wait_recv()
            p_copy(p, p).wait_recv()
        place = in_p[p]
        hot = jnp.where(row16 == jnp.concatenate([place, place], 0), 1.0, 0.0).astype(BF16)
        for i in range(8):
            for half in range(2):
                at = 128 * half + 16 * i
                ones[k % 2, at : at + 16, 128 * i : 128 * i + 128] = hot
        source = (data[...] if k == 0 else data_in[p]).reshape(128, 128)
        left = jnp.concatenate(split(source, 2), 1)
        for i in range(4):
            cols = slice(256 * i, 256 * i + 256)
            wide_out = dot(left, ones[k % 2, :, cols])
            gathered[k, 2 * i] = wide_out[:, :128].reshape(16, 8, 128)
            gathered[k, 2 * i + 1] = wide_out[:, 128:].reshape(16, 8, 128)

    sums = [None] * 32
    power = None
    for k in range(rows):
        p = z ^ k
        if k > 0:
            w_copy(p, p).wait_recv()
        u = [in_w[p, 8 * i : 8 * i + 8] for i in range(8)]
        part = in_w[p, 64:72]
        power = part if power is None else power + part
        for s in range(16):
            d = [gathered[k, i, s] for i in range(8)]
            re = im = None
            for i in range(4):
                x = u[i] * d[i] + u[i + 4] * d[i + 4]
                y = u[i] * d[i + 4] - u[i + 4] * d[i]
                re = x if re is None else re + x
                im = y if im is None else im + y
            sums[2 * s] = re if k == 0 else sums[2 * s] + re
            sums[2 * s + 1] = im if k == 0 else sums[2 * s + 1] + im
    for s in range(32):
        held[s] = sums[s]
    for half in range(2):
        tile = jnp.concatenate([held[:, 4 * half + f, :] for f in range(4)], 0).T.reshape(4, 4, 8, 128)
        for j in range(4):
            back[:, 2 * j + half] = tile[:, j]
    turned = jnp.concatenate([power, jnp.zeros((120, 128), F32)], 0).T.reshape(4, 4, 8, 128)
    gains = turned[:, 0].reshape(32, 128)
    for j in range(1, 4):
        gains = gains + pltpu.roll(turned[:, j].reshape(32, 128), 8 * j, 1)
    back[:, 8] = gains.reshape(4, 8, 128)

    to_root = lambda p: jnp.logical_and(p == 0, jnp.logical_and(z == 0, far))
    for p in range(4):
        here = jnp.logical_or(q == p, to_root(p))

        @pl.when(jnp.logical_not(here))
        def _():
            back_copy(p, q).start()

    @pl.when(root)
    def _():
        for load in loads[:2]:
            load.wait()
        cl = jnp.concatenate([cl_ref[...]] * 4, 1)
        valid = jnp.concatenate([valid_ref[...]] * 4, 1)
        mark = jnp.where(valid > 0, (cl & 15).astype(F32) + 1.0, 0.0)
        owner = cl >> 4
        row = lax.broadcasted_iota(jnp.int32, (128, 128), 0)
        quarter = lax.broadcasted_iota(jnp.int32, (128, 128), 1) // 32
        base = jnp.where(((row >> 4) & 3) == quarter, ((row & 15) + 1).astype(F32), -1.0)
        for p in range(rows):
            place = jnp.sum(jnp.where(owner == 3 * rows + p, mark, 0.0), 0, keepdims=True)
            hot = jnp.where(base == place, 1.0, 0.0)
            hot = jnp.concatenate(
                [jnp.where(row < 64, hot, 0.0), jnp.where(row < 64, 0.0, hot)], 1
            ).astype(BF16)
            root_data_copy(p).wait_recv()
            left = jnp.concatenate(split(root_data[p].reshape(128, 128), 2), 1)
            both = dot(left, jnp.concatenate([hot, hot], 0))
            for m in range(2):
                root_held[p, m] = both[:, 128 * m : 128 * m + 128].reshape(16, 8, 128)
        sums = [None] * 32
        power = None
        for p in range(rows):
            root_copy(p).wait_recv()
            u, v, part = (root_in[p, 8 * m : 8 * m + 8] for m in range(3))
            power = part if p == 0 else power + part
            for s in range(16):
                x, y = root_held[p, 0, s], root_held[p, 1, s]
                re, im = u * x + v * y, u * y - v * x
                sums[2 * s] = re if p == 0 else sums[2 * s] + re
                sums[2 * s + 1] = im if p == 0 else sums[2 * s + 1] + im
        for s in range(32):
            x = sums[s] + pltpu.roll(sums[s], 64, 1)
            held[s] = x + pltpu.roll(x, 32, 1)
        for half in range(2):
            tile = jnp.concatenate([held[:, 4 * half + f, :] for f in range(4)], 0).T
            for j in range(4):
                home[3, 2 * j + half] = tile[8 * j : 8 * j + 8]
        turned = jnp.concatenate([power, jnp.zeros((120, 128), F32)], 0).T
        gains = turned[0:8]
        for j in range(1, 4):
            gains = gains + pltpu.roll(turned[8 * j : 8 * j + 8], 8 * j, 1)
        home[3, 8] = gains

    home[q] = back[q]
    for k in range(1, 4):
        p = lax.rem(q + k, 4)

        @pl.when(jnp.logical_not(jnp.logical_and(root, p == 3)))
        def _():
            back_copy(p, p).wait_recv()

    @pl.when(odd)
    def _():
        @pl.loop(1, n)
        def _(k):
            p = me ^ k
            slot_copy(p, p, pair).wait_send()
            slot_copy(p, p, core).wait_send()

        slot_copy(me, me, pair).wait_send()

    @pl.loop(1, rows)
    def _(k):
        p = lax.rem(z + k, rows)
        data_copy(p, p).wait_send()
        p_copy(p, p).wait_send()
        w_copy(p, p).wait_send()

    for k in range(1, 4):
        p = lax.rem(q + k, 4)

        @pl.when(jnp.logical_not(to_root(p)))
        def _():
            back_copy(p, p).wait_send()

    @pl.when(far)
    def _():
        root_data_copy(z).wait_send()
        root_copy(z).wait_send()


def finish(home, sym_ref, gain_ref):
    total = (home[0] + home[1]) + (home[2] + home[3])
    for j in range(4):
        for f in range(8):
            tile = total[2 * j + f // 4]
            sym_ref[8 * j : 8 * j + 8, f, :] = tile[:, 32 * (f % 4) : 32 * (f % 4) + 32]
    gains = jnp.concatenate([total[8], jnp.zeros((120, 128), F32)], 0).T
    gain_ref[...] = jnp.concatenate([gains[8 * j : 8 * j + 8, 0:8] for j in range(4)], 1)


def body(n, covariances, clusters, cluster_valid, pilots, received_pilot, received_data):
    vmem = pl.BlockSpec(memory_space=pltpu.VMEM)
    rows = n // 4
    home = pl.pallas_call(
        functools.partial(kernel, n),
        out_shape=pltpu.VMEM((4, 9, 8, 128), F32),
        in_specs=[pl.BlockSpec(memory_space=pltpu.HBM)] * 6,
        out_specs=vmem,
        scratch_shapes=[
            pltpu.VMEM((32, 512), F32),
            pltpu.VMEM((16, 32), jnp.int32),
            pltpu.VMEM((16, 32), jnp.int32),
            pltpu.VMEM((1, 32), jnp.int32),
            pltpu.VMEM((16, 8, 128), F32),
            pltpu.VMEM((16, 8, 128), F32),
            pltpu.VMEM((n, 8, 128), F32),
            pltpu.VMEM((n, 8, 128), F32),
            pltpu.VMEM((n // 16, 4, 32, 128), F32),
            pltpu.VMEM((4, 32, 128), F32),
            pltpu.VMEM((8, 8, 256), F32),
            pltpu.VMEM((16, 8, 128), F32),
            pltpu.VMEM((rows, 16, 8, 128), F32),
            pltpu.VMEM((2, 256, 1024), BF16),
            pltpu.VMEM((rows, 8, 16, 8, 128), F32),
            pltpu.VMEM((32, 8, 128), F32),
            pltpu.VMEM((rows, 8, 128), F32),
            pltpu.VMEM((rows, 8, 128), F32),
            pltpu.VMEM((rows, 72, 128), F32),
            pltpu.VMEM((rows, 72, 128), F32),
            pltpu.VMEM((4, 9, 8, 128), F32),
            pltpu.VMEM((rows, 16, 8, 128), F32),
            pltpu.VMEM((rows, 2, 16, 8, 128), F32),
            pltpu.VMEM((24, 128), F32),
            pltpu.VMEM((rows, 24, 128), F32),
            pltpu.SemaphoreType.DMA((6,)),
            pltpu.SemaphoreType.DMA((2, n)),
            pltpu.SemaphoreType.DMA((n,)),
            pltpu.SemaphoreType.DMA((rows,)),
            pltpu.SemaphoreType.DMA((rows,)),
            pltpu.SemaphoreType.DMA((rows,)),
            pltpu.SemaphoreType.DMA((rows,)),
            pltpu.SemaphoreType.DMA((rows,)),
            pltpu.SemaphoreType.DMA((rows,)),
            pltpu.SemaphoreType.DMA((4,)),
            pltpu.SemaphoreType.DMA((4,)),
            pltpu.SemaphoreType.DMA((2,)),
            pltpu.SemaphoreType.DMA((rows,)),
            pltpu.SemaphoreType.DMA((rows,)),
        ],
        compiler_params=pltpu.CompilerParams(
            collective_id=0, has_side_effects=True, vmem_limit_bytes=65000 * 1024
        ),
    )(covariances, clusters.T, cluster_valid.T, pilots.reshape(1, -1), received_pilot, received_data)
    symbols, gain = pl.pallas_call(
        finish,
        out_shape=(jax.ShapeDtypeStruct((32, 8, 32), F32), jax.ShapeDtypeStruct((8, 32), F32)),
        in_specs=[vmem],
        out_specs=(vmem, vmem),
    )(pltpu.with_memory_space_constraint(home, pltpu.VMEM))
    return symbols, gain.T


def solution(mesh):
    placed = (
        P("ap", None),
        P("ap", None),
        P("ap", None),
        P("ap"),
        P("ap", "sc", None),
        P("ap", "sc", None),
    )
    return jax.shard_map(
        functools.partial(body, mesh.shape["ap"]),
        mesh=mesh,
        in_specs=placed,
        out_specs=(P("ap", "sc", None), P("ap", "sc")),
        check_vma=False,
    )
```

```python
import functools

import jax
import jax.numpy as jnp
from jax import lax
from jax.experimental import pallas as pl
from jax.experimental.pallas import tpu as pltpu
from jax.sharding import PartitionSpec as P

F32 = jnp.float32
BF16 = jnp.bfloat16
MESH = pl.DeviceIdType.MESH
PAIRS = [(0, 1), (0, 2), (0, 3), (1, 2), (1, 3), (2, 3)]
ENTRIES = [(i, i) for i in range(4)] + PAIRS
DIAGONAL = [8, 11, 9, 12]
REAL = dict(zip(PAIRS, [0, 1, 2, 3, 4, 10]))
IMAG = dict(zip(PAIRS, [16, 17, 18, 19, 20, 26]))
CODE = 24


def split(x, parts):
    out = []
    for _ in range(parts - 1):
        head = x.astype(BF16)
        out.append(head)
        x = x - head.astype(F32)
    out.append(x.astype(BF16))
    return out


def dot(a, b, rhs_transposed=False):
    dims = (((1,), (1,)), ((), ())) if rhs_transposed else (((1,), (0,)), ((), ()))
    return lax.dot_general(a, b, dims, preferred_element_type=F32)


def dot_split(a, b, parts, rhs_transposed=False):
    rows = a.shape[0]
    full = dot(jnp.concatenate(split(a, parts), 0), b, rhs_transposed)
    total = full[:rows]
    for p in range(1, parts):
        total = total + full[p * rows : (p + 1) * rows]
    return total


def get(h, i, j):
    if i == j:
        return h[i, i]
    if i < j:
        return h[i, j]
    re, im = h[j, i]
    return re, -im


def hermitian_inverse(h):
    h = dict(h)
    for k in range(4):
        inv = 1.0 / h[k, k][0]
        col = {i: get(h, i, k) for i in range(4) if i != k}
        scaled = {i: (c[0] * inv, c[1] * inv) for i, c in col.items()}
        new = {}
        for i, j in ENTRIES:
            if i == k and j == k:
                new[i, j] = (-inv, None)
            elif i == k:
                re, im = scaled[j]
                new[i, j] = (re, -im)
            elif j == k:
                new[i, j] = scaled[i]
            elif i == j:
                a, s = col[i], scaled[i]
                new[i, j] = (h[i, i][0] - (a[0] * s[0] + a[1] * s[1]), None)
            else:
                a, s = scaled[i], col[j]
                re = h[i, j][0] - (a[0] * s[0] + a[1] * s[1])
                im = h[i, j][1] - (a[1] * s[0] - a[0] * s[1])
                new[i, j] = (re, im)
        h = new
    return {k: (-v[0], None if v[1] is None else -v[1]) for k, v in h.items()}


def from_parts(x):
    h = {(i, i): (x[i], None) for i in range(4)}
    for q, p in enumerate(PAIRS):
        h[p] = (x[4 + 2 * q], x[5 + 2 * q])
    return h


def add_products(acc, a, b):
    re, im = a[0] * b[0], None
    if a[1] is not None and b[1] is not None:
        re = re - a[1] * b[1]
    if b[1] is not None:
        im = a[0] * b[1]
    if a[1] is not None:
        im = a[1] * b[0] if im is None else im + a[1] * b[0]
    if acc is None:
        return re, im
    if im is None:
        im = acc[1]
    elif acc[1] is not None:
        im = acc[1] + im
    return acc[0] + re, im


def block_transpose(x):
    lane_block = lax.broadcasted_iota(jnp.int32, x[0].shape, 1) // 16
    x = list(x)
    for m in (1, 2, 4):
        upper = (lane_block & m) != 0
        new = list(x)
        for p in range(8):
            if p & m:
                continue
            q = p + m
            new[p] = jnp.where(upper, pltpu.roll(x[q], 16 * m, 1), x[p])
            new[q] = jnp.where(upper, x[q], pltpu.roll(x[p], 128 - 16 * m, 1))
        x = new
    return x


def lane_groups(x):
    lane_block = lax.broadcasted_iota(jnp.int32, x[0].shape, 1) // 32
    x = list(x)
    for m in (1, 2):
        upper = (lane_block & m) != 0
        new = list(x)
        for p in range(4):
            if p & m:
                continue
            q = p + m
            new[p] = jnp.where(upper, pltpu.roll(x[q], 32 * m, 1), x[p])
            new[q] = jnp.where(upper, x[q], pltpu.roll(x[p], 128 - 32 * m, 1))
        x = new
    return x


def kernel(
    n, cov_hbm, cl_hbm, valid_hbm, pilot_hbm, rp_hbm, rd_hbm, home,
    cov_ref, cl_ref, valid_ref, pilot_ref, rp_ref, rd_ref,
    send, recv, trans, pinv, obs, data, data_in, ones, gathered, held, out_p, in_p, out_w, in_w, back,
    root_data, root_held, out_r, root_in,
    load_sem, send_sem, recv_sem, data_send_sem, data_recv_sem,
    p_send_sem, p_recv_sem, w_send_sem, w_recv_sem, back_send_sem, back_recv_sem,
    root_send_sem, root_data_sem, root_recv_sem,
):
    me = lax.axis_index("ap")
    core = lax.axis_index("sc")
    rows = n // 4
    sets = n // 16
    groups = 4 * sets
    q, z = lax.div(me, rows), lax.rem(me, rows)

    pairs = [
        (cl_hbm, cl_ref), (valid_hbm, valid_ref), (pilot_hbm, pilot_ref),
        (cov_hbm, cov_ref), (rp_hbm, rp_ref), (rd_hbm, rd_ref),
    ]
    loads = [pltpu.make_async_copy(a, b, load_sem.at[i]) for i, (a, b) in enumerate(pairs)]
    odd = lax.rem(core, 2) == 1
    pair = core ^ 1
    even = jnp.logical_not(odd)
    root = jnp.logical_and(me == 0, even)
    far = jnp.logical_and(q == 3, even)
    barrier = pltpu.get_barrier_semaphore()

    def greet(p, c):
        pl.semaphore_signal(barrier, inc=1, device_id=(p, c), device_id_type=MESH)

    @pl.when(odd)
    def _():
        for load in loads[:4]:
            load.start()

        @pl.loop(1, n)
        def _(d):
            greet(me ^ (n - d), core)

    @pl.when(jnp.logical_not(odd))
    def _():
        @pl.loop(0, n)
        def _(d):
            greet(me ^ (n - 1 - d), pair)

        @pl.loop(1, rows)
        def _(d):
            greet(q * rows + (z ^ d), core)

        for d in range(1, 4):
            greet((q ^ d) * rows + z, core)

    @pl.when(root)
    def _():
        for load in loads[:2]:
            load.start()

        @pl.loop(1, rows)
        def _(c):
            greet(3 * rows + c, core)

    for load in loads[4:]:
        load.start()

    trans[...] = jnp.zeros_like(trans)
    ones[...] = jnp.zeros_like(ones)

    def slot_copy(p, slot, to):
        return pltpu.make_async_remote_copy(
            src_ref=send.at[p, 0:5], dst_ref=recv.at[slot, 0:5],
            send_sem=send_sem.at[lax.rem(to, 2)], recv_sem=recv_sem.at[0],
            device_id=(p, to), device_id_type=MESH,
        )

    def wait_all(ref, sem):
        pltpu.make_async_copy(ref, ref, sem).wait()

    def data_copy(p, slot):
        return pltpu.make_async_remote_copy(
            src_ref=data, dst_ref=data_in.at[slot],
            send_sem=data_send_sem.at[0], recv_sem=data_recv_sem.at[0],
            device_id=(q * rows + p, core), device_id_type=MESH,
        )

    def p_copy(p, slot):
        return pltpu.make_async_remote_copy(
            src_ref=out_p.at[p], dst_ref=in_p.at[slot],
            send_sem=p_send_sem.at[0], recv_sem=p_recv_sem.at[0],
            device_id=(q * rows + p, core), device_id_type=MESH,
        )

    def w_copy(p, slot):
        return pltpu.make_async_remote_copy(
            src_ref=out_w.at[p], dst_ref=in_w.at[slot],
            send_sem=w_send_sem.at[0], recv_sem=w_recv_sem.at[(p ^ z) - 1],
            device_id=(q * rows + p, core), device_id_type=MESH,
        )

    def root_data_copy(slot):
        return pltpu.make_async_remote_copy(
            src_ref=data, dst_ref=root_data.at[slot],
            send_sem=root_send_sem.at[0], recv_sem=root_data_sem.at[0],
            device_id=(0, core), device_id_type=MESH,
        )

    def root_copy(slot):
        return pltpu.make_async_remote_copy(
            src_ref=out_r, dst_ref=root_in.at[slot],
            send_sem=root_send_sem.at[1], recv_sem=root_recv_sem.at[0],
            device_id=(0, core), device_id_type=MESH,
        )

    def back_copy(p, slot):
        return pltpu.make_async_remote_copy(
            src_ref=back.at[p], dst_ref=home.at[slot],
            send_sem=back_send_sem.at[0], recv_sem=back_recv_sem.at[0],
            device_id=(p * rows + z, core), device_id_type=MESH,
        )

    @pl.when(odd)
    def _():
        for load in loads[:4]:
            load.wait()
        wide = lambda x: jnp.concatenate([x] * 4, 1)
        cl = wide(cl_ref[...])
        code = jnp.where(
            wide(valid_ref[...]) > 0, (wide(pilot_ref[...]) * 16 + (cl & 15)).astype(F32) + 1.0, 0.0
        )
        owner = (cl >> 4) - lax.broadcasted_iota(jnp.int32, (16, 128), 1) // 32
        slots = []
        for a in range(4):
            part = cov_ref[:, 128 * a : 128 * a + 128]
            turned = jnp.concatenate([part] * 4, 0).T
            slots += [turned[32 * j : 32 * j + 32] for j in range(4)]
        row8 = lax.broadcasted_iota(jnp.int32, (8, 128), 0)
        for t in range(n // 4):
            tiles = [jnp.zeros((8, 128), F32)] * 4
            mark = jnp.zeros((8, 128), F32)
            for c in range(16):
                mine = jnp.broadcast_to(owner[c : c + 1], (8, 128)) == 4 * t
                tiles = [jnp.where(mine, slots[c][8 * v : 8 * v + 8], tiles[v]) for v in range(4)]
                mark = jnp.where(mine, jnp.broadcast_to(code[c : c + 1], (8, 128)), mark)
            first = jnp.broadcast_to(tiles[0][0:1], (8, 128))
            second = jnp.broadcast_to(tiles[0][5:6], (8, 128))
            tiles[1] = jnp.where(row8 == 1, first, jnp.where(row8 == 6, second, tiles[1]))
            tiles[3] = jnp.where(row8 == 1, mark, tiles[3])
            tiles = [jnp.where(row8 < 3, pltpu.roll(x, 7, 0), pltpu.roll(x, 5, 0)) for x in tiles]
            for j, tile in enumerate(lane_groups(tiles)):
                send[4 * t + j] = tile
        pl.semaphore_wait(barrier, 2 * n - 1)

        @pl.loop(0, n)
        def _(d):
            slot_copy(me ^ (n - 1 - d), me, pair).start()

        @pl.loop(1, n)
        def _(d):
            slot_copy(me ^ (n - d), me, core).start()

        recv[me] = send[me]

    extra = jnp.logical_and(far, z > 0)

    @pl.when(jnp.logical_and(even, extra))
    def _():
        pl.semaphore_wait(barrier, rows + 3)

    @pl.when(jnp.logical_and(even, jnp.logical_not(extra)))
    def _():
        pl.semaphore_wait(barrier, rows + 2)

    for load in loads[4:]:
        load.wait()
    turned = jnp.concatenate([rd_ref[:, f, :] for f in range(8)], 0).T.reshape(16, 8, 128)
    for f, tile in enumerate(block_transpose([turned[:, i, :] for i in range(8)])):
        data[:, f, :] = tile

    @pl.loop(1, rows)
    def _(d):
        data_copy(lax.rem(z + d, rows), z).start()

    @pl.when(far)
    def _():
        root_data_copy(z).start()

    turned = jnp.concatenate([rp_ref[:, f, :] for f in range(8)], 0).T
    for half in range(2):
        tiles = [turned[8 * (8 * half + t) : 8 * (8 * half + t) + 8] for t in range(8)]
        for f, tile in enumerate(block_transpose(tiles)):
            obs[f, :, 128 * half : 128 * half + 128] = tile
    observed = jnp.concatenate([obs[:, i, :] for i in range(8)], 0)
    observed = jnp.concatenate(split(observed, 3), 0)

    @pl.when(odd)
    def _():
        wait_all(recv.at[0 : n - 1, 0:5], recv_sem.at[0])

    @pl.when(even)
    def _():
        wait_all(recv.at[:, 0:5], recv_sem.at[0])

    row32 = lax.broadcasted_iota(jnp.int32, (32, 128), 0)
    codes, matrices = [], []
    for e in range(sets):
        for j in range(4):
            tiles = lane_groups([recv[h * rows + 4 * e + j] for h in range(4)])
            for v, tile in enumerate(tiles):
                trans[e, j, 8 * v : 8 * v + 5] = tile[0:5]
            codes.append(tiles[3][0:1])
            matrices.append(jnp.where(row32 == CODE, 0.0, trans[e, j]))
    codes = jnp.concatenate(codes, 1) - 1.0
    matrices = jnp.concatenate(matrices, 1)
    width = 128 * groups
    bins = lax.broadcasted_iota(jnp.int32, (256, width), 0).astype(F32)
    choose = jnp.where(bins == codes, 1.0, 0.0).astype(BF16)
    places = jnp.where(codes >= 0.0, codes - 16.0 * jnp.floor(codes * 0.0625), -1.0)
    ap_rows = (lax.broadcasted_iota(jnp.int32, (128, width), 0) & 15).astype(F32)
    pick = jnp.where(ap_rows == places, 1.0, 0.0).astype(BF16)
    for g in range(groups):
        out_p[g] = jnp.broadcast_to(places[:, 128 * g : 128 * g + 128], (8, 128))

        @pl.when(z != g)
        def _():
            p_copy(g, z).start()

    if sets == 1:
        rest = jnp.zeros((124, 128), F32)
        column = jnp.concatenate([codes[:, 128 * j : 128 * j + 128] for j in range(4)] + [rest], 0).T
        column_places = jnp.where(column >= 0.0, column - 16.0 * jnp.floor(column * 0.0625), -1.0)

        def alike(x, y):
            blocks = [jnp.where(x[:, j : j + 1] == y, 1.0, 0.0).astype(BF16) for j in range(4)]
            return jnp.concatenate(blocks, 0)

        slot_psi = dot_split(matrices, alike(column, codes), 3)
    else:
        slot_psi = dot_split(dot_split(matrices, choose, 3, True), choose, 3)
    slot_obs = dot(observed, choose)
    slot_obs = slot_obs[0:64] + slot_obs[64:128] + slot_obs[128:192]

    estimates, outers = [], []
    for e in range(sets):
        for j in range(4):
            g = 4 * e + j
            pinv[j] = slot_psi[:, 128 * g : 128 * g + 128]
        psi = {(i, i): (pinv[:, DIAGONAL[i], :] + 1.0, None) for i in range(4)}
        psi.update({p: (pinv[:, REAL[p], :], pinv[:, IMAG[p], :]) for p in PAIRS})
        pi = hermitian_inverse(psi)
        r = {(i, i): (trans[e, :, DIAGONAL[i], :], None) for i in range(4)}
        for p in PAIRS:
            r[p] = (trans[e, :, REAL[p], :], trans[e, :, IMAG[p], :])
        w = {}
        for i in range(4):
            for k in range(4):
                acc = None
                for l in range(4):
                    acc = add_products(acc, get(r, i, l), get(pi, l, k))
                w[i, k] = acc
        err = {}
        for i, k in ENTRIES:
            acc = None
            for l in range(4):
                acc = add_products(acc, w[i, l], get(r, l, k))
            re = r[i, k][0] - acc[0]
            err[i, k] = (re, None) if i == k else (re, r[i, k][1] - acc[1])
        for j in range(4):
            g = 4 * e + j
            cols = slice(128 * g, 128 * g + 128)
            y = [(slot_obs[8 * i : 8 * i + 8, cols], slot_obs[32 + 8 * i : 40 + 8 * i, cols]) for i in range(4)]
            h = []
            for i in range(4):
                acc = None
                for k in range(4):
                    wr, wi = w[i, k]
                    acc = add_products(acc, (wr[j : j + 1], wi[j : j + 1]), y[k])
                h.append(acc)
            estimates.append(h)
            out = []
            for i in range(4):
                out.append(h[i][0] * h[i][0] + h[i][1] * h[i][1] + err[i, i][0][j : j + 1])
            for i, k in PAIRS:
                out.append(h[i][0] * h[k][0] + h[i][1] * h[k][1] + err[i, k][0][j : j + 1])
                out.append(h[i][1] * h[k][0] - h[i][0] * h[k][1] + err[i, k][1][j : j + 1])
            outers.append(jnp.concatenate(out, 0))
    outers = jnp.concatenate(outers, 1)
    if sets == 1:
        slot_sum = dot_split(outers, alike(column_places, places), 3)
    else:
        summed = dot_split(outers, pick, 3, True)
        own_f = lax.broadcasted_iota(jnp.int32, (8, 128), 1) // 16 == lax.broadcasted_iota(jnp.int32, (8, 128), 0)
        comps = [
            jnp.sum(jnp.where(own_f, summed[8 * x : 8 * x + 8], 0.0), 0, keepdims=True) for x in range(16)
        ]
        masked = jnp.concatenate([jnp.where(own_f, c, 0.0) for c in comps], 0)
        slot_sum = dot_split(masked, pick, 3)
    for g in range(groups):
        cols = slice(128 * g, 128 * g + 128)
        h = estimates[g]
        parts = [slot_sum[8 * x : 8 * x + 8, cols] for x in range(16)]
        gs = hermitian_inverse(from_parts([c + 1.0 if x < 4 else c for x, c in enumerate(parts)]))
        power = None
        for i in range(4):
            acc = None
            for k in range(4):
                acc = add_products(acc, get(gs, i, k), h[k])
            out_w[g, 8 * i : 8 * i + 8] = acc[0]
            out_w[g, 32 + 8 * i : 40 + 8 * i] = acc[1]
            term = h[i][0] * acc[0] + h[i][1] * acc[1]
            power = term if power is None else power + term
        out_w[g, 64:72] = power

        if g == 0:
            @pl.when(far)
            def _():
                quarter = lax.broadcasted_iota(jnp.int32, (8, 128), 1) // 32
                for m in range(2):
                    packed = out_w[0, 32 * m : 32 * m + 8]
                    for j in range(1, 4):
                        at = 32 * m + 8 * j
                        packed = jnp.where(quarter == j, pltpu.roll(out_w[0, at : at + 8], 32 * j, 1), packed)
                    out_r[8 * m : 8 * m + 8] = packed
                out_r[16:24] = out_w[0, 64:72]
                root_copy(z).start()

        @pl.when(z != g)
        def _():
            w_copy(g, z).start()

    row16 = lax.broadcasted_iota(jnp.int32, (16, 128), 0).astype(F32)
    in_p[z] = out_p[z]
    in_w[z] = out_w[z]
    for k in range(rows):
        p = z ^ k
        if k == 1:
            wait_all(data_in.at[0 : rows - 1], data_recv_sem.at[0])
            wait_all(in_p.at[0 : rows - 1], p_recv_sem.at[0])
        place = in_p[p]
        hot = jnp.where(row16 == jnp.concatenate([place, place], 0), 1.0, 0.0).astype(BF16)
        for i in range(8):
            for half in range(2):
                at = 128 * half + 16 * i
                ones[k % 2, at : at + 16, 128 * i : 128 * i + 128] = hot
        source = (data[...] if k == 0 else data_in[p]).reshape(128, 128)
        left = jnp.concatenate(split(source, 2), 1)
        for i in range(4):
            cols = slice(256 * i, 256 * i + 256)
            wide_out = dot(left, ones[k % 2, :, cols])
            gathered[k, 2 * i] = wide_out[:, :128].reshape(16, 8, 128)
            gathered[k, 2 * i + 1] = wide_out[:, 128:].reshape(16, 8, 128)

    sums = [None] * 32
    power = None
    for k in range(rows):
        p = z ^ k
        if k > 0:
            w_copy(p, p).wait_recv()
        u = [in_w[p, 8 * i : 8 * i + 8] for i in range(8)]
        part = in_w[p, 64:72]
        power = part if power is None else power + part
        for s in range(16):
            d = [gathered[k, i, s] for i in range(8)]
            re = im = None
            for i in range(4):
                x = u[i] * d[i] + u[i + 4] * d[i + 4]
                y = u[i] * d[i + 4] - u[i + 4] * d[i]
                re = x if re is None else re + x
                im = y if im is None else im + y
            sums[2 * s] = re if k == 0 else sums[2 * s] + re
            sums[2 * s + 1] = im if k == 0 else sums[2 * s + 1] + im
    for s in range(32):
        held[s] = sums[s]
    for half in range(2):
        tile = jnp.concatenate([held[:, 4 * half + f, :] for f in range(4)], 0).T.reshape(4, 4, 8, 128)
        for j in range(4):
            back[:, 2 * j + half] = tile[:, j]
    turned = jnp.concatenate([power, jnp.zeros((120, 128), F32)], 0).T.reshape(4, 4, 8, 128)
    gains = turned[:, 0].reshape(32, 128)
    for j in range(1, 4):
        gains = gains + pltpu.roll(turned[:, j].reshape(32, 128), 8 * j, 1)
    back[:, 8] = gains.reshape(4, 8, 128)

    to_root = lambda p: jnp.logical_and(p == 0, jnp.logical_and(z == 0, far))
    for p in range(4):
        here = jnp.logical_or(q == p, to_root(p))

        @pl.when(jnp.logical_not(here))
        def _():
            back_copy(p, q).start()

    @pl.when(root)
    def _():
        for load in loads[:2]:
            load.wait()
        cl = jnp.concatenate([cl_ref[...]] * 4, 1)
        valid = jnp.concatenate([valid_ref[...]] * 4, 1)
        mark = jnp.where(valid > 0, (cl & 15).astype(F32) + 1.0, 0.0)
        owner = cl >> 4
        row = lax.broadcasted_iota(jnp.int32, (128, 128), 0)
        quarter = lax.broadcasted_iota(jnp.int32, (128, 128), 1) // 32
        base = jnp.where(((row >> 4) & 3) == quarter, ((row & 15) + 1).astype(F32), -1.0)
        for p in range(rows):
            place = jnp.sum(jnp.where(owner == 3 * rows + p, mark, 0.0), 0, keepdims=True)
            hot = jnp.where(base == place, 1.0, 0.0)
            hot = jnp.concatenate(
                [jnp.where(row < 64, hot, 0.0), jnp.where(row < 64, 0.0, hot)], 1
            ).astype(BF16)
            if p == 0:
                wait_all(root_data, root_data_sem.at[0])
            left = jnp.concatenate(split(root_data[p].reshape(128, 128), 2), 1)
            both = dot(left, jnp.concatenate([hot, hot], 0))
            for m in range(2):
                root_held[p, m] = both[:, 128 * m : 128 * m + 128].reshape(16, 8, 128)
        sums = [None] * 32
        power = None
        for p in range(rows):
            if p == 0:
                wait_all(root_in, root_recv_sem.at[0])
            u, v, part = (root_in[p, 8 * m : 8 * m + 8] for m in range(3))
            power = part if p == 0 else power + part
            for s in range(16):
                x, y = root_held[p, 0, s], root_held[p, 1, s]
                re, im = u * x + v * y, u * y - v * x
                sums[2 * s] = re if p == 0 else sums[2 * s] + re
                sums[2 * s + 1] = im if p == 0 else sums[2 * s + 1] + im
        for s in range(32):
            x = sums[s] + pltpu.roll(sums[s], 64, 1)
            held[s] = x + pltpu.roll(x, 32, 1)
        for half in range(2):
            tile = jnp.concatenate([held[:, 4 * half + f, :] for f in range(4)], 0).T
            for j in range(4):
                home[3, 2 * j + half] = tile[8 * j : 8 * j + 8]
        turned = jnp.concatenate([power, jnp.zeros((120, 128), F32)], 0).T
        gains = turned[0:8]
        for j in range(1, 4):
            gains = gains + pltpu.roll(turned[8 * j : 8 * j + 8], 8 * j, 1)
        home[3, 8] = gains

    home[q] = back[q]

    @pl.when(jnp.logical_not(root))
    def _():
        wait_all(home.at[0:3], back_recv_sem.at[0])

    @pl.when(root)
    def _():
        wait_all(home.at[0:2], back_recv_sem.at[0])

    @pl.when(odd)
    def _():
        wait_all(send.at[:, 0:5], send_sem.at[0])
        wait_all(send.at[0 : n - 1, 0:5], send_sem.at[1])

    wait_all(data_in.at[0 : rows - 1], data_send_sem.at[0])
    wait_all(in_p.at[0 : rows - 1], p_send_sem.at[0])
    wait_all(in_w.at[0 : rows - 1], w_send_sem.at[0])

    @pl.when(to_root(0))
    def _():
        wait_all(back.at[0:2], back_send_sem.at[0])

    @pl.when(jnp.logical_not(to_root(0)))
    def _():
        wait_all(back.at[0:3], back_send_sem.at[0])

    @pl.when(far)
    def _():
        root_data_copy(z).wait_send()
        root_copy(z).wait_send()


def finish(home, sym_ref, gain_ref):
    total = (home[0] + home[1]) + (home[2] + home[3])
    for j in range(4):
        for f in range(8):
            tile = total[2 * j + f // 4]
            sym_ref[8 * j : 8 * j + 8, f, :] = tile[:, 32 * (f % 4) : 32 * (f % 4) + 32]
    gains = jnp.concatenate([total[8], jnp.zeros((120, 128), F32)], 0).T
    gain_ref[...] = jnp.concatenate([gains[8 * j : 8 * j + 8, 0:8] for j in range(4)], 1)


def body(n, covariances, clusters, cluster_valid, pilots, received_pilot, received_data):
    vmem = pl.BlockSpec(memory_space=pltpu.VMEM)
    rows = n // 4
    home = pl.pallas_call(
        functools.partial(kernel, n),
        out_shape=pltpu.VMEM((4, 9, 8, 128), F32),
        in_specs=[pl.BlockSpec(memory_space=pltpu.HBM)] * 6,
        out_specs=vmem,
        scratch_shapes=[
            pltpu.VMEM((32, 512), F32),
            pltpu.VMEM((16, 32), jnp.int32),
            pltpu.VMEM((16, 32), jnp.int32),
            pltpu.VMEM((1, 32), jnp.int32),
            pltpu.VMEM((16, 8, 128), F32),
            pltpu.VMEM((16, 8, 128), F32),
            pltpu.VMEM((n, 8, 128), F32),
            pltpu.VMEM((n, 8, 128), F32),
            pltpu.VMEM((n // 16, 4, 32, 128), F32),
            pltpu.VMEM((4, 32, 128), F32),
            pltpu.VMEM((8, 8, 256), F32),
            pltpu.VMEM((16, 8, 128), F32),
            pltpu.VMEM((rows, 16, 8, 128), F32),
            pltpu.VMEM((2, 256, 1024), BF16),
            pltpu.VMEM((rows, 8, 16, 8, 128), F32),
            pltpu.VMEM((32, 8, 128), F32),
            pltpu.VMEM((rows, 8, 128), F32),
            pltpu.VMEM((rows, 8, 128), F32),
            pltpu.VMEM((rows, 72, 128), F32),
            pltpu.VMEM((rows, 72, 128), F32),
            pltpu.VMEM((4, 9, 8, 128), F32),
            pltpu.VMEM((rows, 16, 8, 128), F32),
            pltpu.VMEM((rows, 2, 16, 8, 128), F32),
            pltpu.VMEM((24, 128), F32),
            pltpu.VMEM((rows, 24, 128), F32),
            pltpu.SemaphoreType.DMA((6,)),
            pltpu.SemaphoreType.DMA((2,)),
            pltpu.SemaphoreType.DMA((1,)),
            pltpu.SemaphoreType.DMA((1,)),
            pltpu.SemaphoreType.DMA((1,)),
            pltpu.SemaphoreType.DMA((1,)),
            pltpu.SemaphoreType.DMA((1,)),
            pltpu.SemaphoreType.DMA((1,)),
            pltpu.SemaphoreType.DMA((rows - 1,)),
            pltpu.SemaphoreType.DMA((1,)),
            pltpu.SemaphoreType.DMA((1,)),
            pltpu.SemaphoreType.DMA((2,)),
            pltpu.SemaphoreType.DMA((1,)),
            pltpu.SemaphoreType.DMA((1,)),
        ],
        compiler_params=pltpu.CompilerParams(
            collective_id=0, has_side_effects=True, vmem_limit_bytes=65000 * 1024
        ),
    )(covariances, clusters.T, cluster_valid.T, pilots.reshape(1, -1), received_pilot, received_data)
    symbols, gain = pl.pallas_call(
        finish,
        out_shape=(jax.ShapeDtypeStruct((32, 8, 32), F32), jax.ShapeDtypeStruct((8, 32), F32)),
        in_specs=[vmem],
        out_specs=(vmem, vmem),
    )(pltpu.with_memory_space_constraint(home, pltpu.VMEM))
    return symbols, gain.T


def solution(mesh):
    placed = (
        P("ap", None),
        P("ap", None),
        P("ap", None),
        P("ap"),
        P("ap", "sc", None),
        P("ap", "sc", None),
    )
    return jax.shard_map(
        functools.partial(body, mesh.shape["ap"]),
        mesh=mesh,
        in_specs=placed,
        out_specs=(P("ap", "sc", None), P("ap", "sc")),
        check_vma=False,
    )
```

```python
import functools

import jax
import jax.numpy as jnp
from jax import lax
from jax.experimental import pallas as pl
from jax.experimental.pallas import tpu as pltpu
from jax.sharding import PartitionSpec as P

F32 = jnp.float32
BF16 = jnp.bfloat16
MESH = pl.DeviceIdType.MESH
PAIRS = [(0, 1), (0, 2), (0, 3), (1, 2), (1, 3), (2, 3)]
ENTRIES = [(i, i) for i in range(4)] + PAIRS
DIAGONAL = [8, 11, 9, 12]
REAL = dict(zip(PAIRS, [0, 1, 2, 3, 4, 10]))
IMAG = dict(zip(PAIRS, [16, 17, 18, 19, 20, 26]))
CODE = 24


def split(x, parts):
    out = []
    for _ in range(parts - 1):
        head = x.astype(BF16)
        out.append(head)
        x = x - head.astype(F32)
    out.append(x.astype(BF16))
    return out


def dot(a, b, rhs_transposed=False):
    dims = (((1,), (1,)), ((), ())) if rhs_transposed else (((1,), (0,)), ((), ()))
    return lax.dot_general(a, b, dims, preferred_element_type=F32)


def dot_split(a, b, parts, rhs_transposed=False):
    rows = a.shape[0]
    full = dot(jnp.concatenate(split(a, parts), 0), b, rhs_transposed)
    total = full[:rows]
    for p in range(1, parts):
        total = total + full[p * rows : (p + 1) * rows]
    return total


def get(h, i, j):
    if i == j:
        return h[i, i]
    if i < j:
        return h[i, j]
    re, im = h[j, i]
    return re, -im


def hermitian_inverse(h):
    h = dict(h)
    for k in range(4):
        inv = 1.0 / h[k, k][0]
        col = {i: get(h, i, k) for i in range(4) if i != k}
        scaled = {i: (c[0] * inv, c[1] * inv) for i, c in col.items()}
        new = {}
        for i, j in ENTRIES:
            if i == k and j == k:
                new[i, j] = (-inv, None)
            elif i == k:
                re, im = scaled[j]
                new[i, j] = (re, -im)
            elif j == k:
                new[i, j] = scaled[i]
            elif i == j:
                a, s = col[i], scaled[i]
                new[i, j] = (h[i, i][0] - (a[0] * s[0] + a[1] * s[1]), None)
            else:
                a, s = scaled[i], col[j]
                re = h[i, j][0] - (a[0] * s[0] + a[1] * s[1])
                im = h[i, j][1] - (a[1] * s[0] - a[0] * s[1])
                new[i, j] = (re, im)
        h = new
    return {k: (-v[0], None if v[1] is None else -v[1]) for k, v in h.items()}


def from_parts(x):
    h = {(i, i): (x[i], None) for i in range(4)}
    for q, p in enumerate(PAIRS):
        h[p] = (x[4 + 2 * q], x[5 + 2 * q])
    return h


def add_products(acc, a, b):
    re, im = a[0] * b[0], None
    if a[1] is not None and b[1] is not None:
        re = re - a[1] * b[1]
    if b[1] is not None:
        im = a[0] * b[1]
    if a[1] is not None:
        im = a[1] * b[0] if im is None else im + a[1] * b[0]
    if acc is None:
        return re, im
    if im is None:
        im = acc[1]
    elif acc[1] is not None:
        im = acc[1] + im
    return acc[0] + re, im


def block_transpose(x):
    lane_block = lax.broadcasted_iota(jnp.int32, x[0].shape, 1) // 16
    x = list(x)
    for m in (1, 2, 4):
        upper = (lane_block & m) != 0
        new = list(x)
        for p in range(8):
            if p & m:
                continue
            q = p + m
            new[p] = jnp.where(upper, pltpu.roll(x[q], 16 * m, 1), x[p])
            new[q] = jnp.where(upper, x[q], pltpu.roll(x[p], 128 - 16 * m, 1))
        x = new
    return x


def lane_groups(x):
    lane_block = lax.broadcasted_iota(jnp.int32, x[0].shape, 1) // 32
    x = list(x)
    for m in (1, 2):
        upper = (lane_block & m) != 0
        new = list(x)
        for p in range(4):
            if p & m:
                continue
            q = p + m
            new[p] = jnp.where(upper, pltpu.roll(x[q], 32 * m, 1), x[p])
            new[q] = jnp.where(upper, x[q], pltpu.roll(x[p], 128 - 32 * m, 1))
        x = new
    return x


def kernel(
    n, cov_hbm, cl_hbm, valid_hbm, pilot_hbm, rp_hbm, rd_hbm, home,
    cov_ref, cl_ref, valid_ref, pilot_ref, rp_ref, rd_ref,
    send, recv, trans, pinv, obs, data, data_in, ones, gathered, held, out_p, in_p, out_w, in_w, back,
    root_data, root_held, out_r, root_in,
    load_sem, send_sem, recv_sem, data_send_sem, data_recv_sem,
    p_send_sem, p_recv_sem, w_send_sem, w_recv_sem, back_send_sem, back_recv_sem,
    root_send_sem, root_data_sem, root_recv_sem,
):
    me = lax.axis_index("ap")
    core = lax.axis_index("sc")
    rows = n // 4
    sets = n // 16
    groups = 4 * sets
    q, z = lax.div(me, rows), lax.rem(me, rows)

    pairs = [
        (cl_hbm, cl_ref), (valid_hbm, valid_ref), (pilot_hbm, pilot_ref),
        (cov_hbm, cov_ref), (rp_hbm, rp_ref), (rd_hbm, rd_ref),
    ]
    loads = [pltpu.make_async_copy(a, b, load_sem.at[i]) for i, (a, b) in enumerate(pairs)]
    odd = lax.rem(core, 2) == 1
    pair = core ^ 1
    even = jnp.logical_not(odd)
    root = jnp.logical_and(me == 0, even)
    far = jnp.logical_and(q == 3, even)
    barrier = pltpu.get_barrier_semaphore()

    def greet(p, c):
        pl.semaphore_signal(barrier, inc=1, device_id=(p, c), device_id_type=MESH)

    @pl.when(odd)
    def _():
        for load in loads[:4]:
            load.start()

        @pl.loop(1, n)
        def _(d):
            greet(me ^ (n - d), core)

    @pl.when(jnp.logical_not(odd))
    def _():
        greet(me, pair)

        @pl.loop(1, rows)
        def _(d):
            greet(q * rows + (z ^ d), core)

        for d in range(1, 4):
            greet((q ^ d) * rows + z, core)

    @pl.when(root)
    def _():
        for load in loads[:2]:
            load.start()

        @pl.loop(1, rows)
        def _(c):
            greet(3 * rows + c, core)

    for load in loads[4:]:
        load.start()

    trans[...] = jnp.zeros_like(trans)
    ones[...] = jnp.zeros_like(ones)

    def slot_copy(p, slot, to):
        return pltpu.make_async_remote_copy(
            src_ref=send.at[p, 0:5], dst_ref=recv.at[slot, 0:5],
            send_sem=send_sem.at[lax.rem(to, 2)], recv_sem=recv_sem.at[0],
            device_id=(p, to), device_id_type=MESH,
        )

    def wait_all(ref, sem):
        pltpu.make_async_copy(ref, ref, sem).wait()

    def data_copy(p, slot):
        return pltpu.make_async_remote_copy(
            src_ref=data, dst_ref=data_in.at[slot],
            send_sem=data_send_sem.at[0], recv_sem=data_recv_sem.at[0],
            device_id=(q * rows + p, core), device_id_type=MESH,
        )

    def p_copy(p, slot):
        return pltpu.make_async_remote_copy(
            src_ref=out_p.at[p], dst_ref=in_p.at[slot],
            send_sem=p_send_sem.at[0], recv_sem=p_recv_sem.at[0],
            device_id=(q * rows + p, core), device_id_type=MESH,
        )

    def w_copy(p, slot):
        return pltpu.make_async_remote_copy(
            src_ref=out_w.at[p], dst_ref=in_w.at[slot],
            send_sem=w_send_sem.at[0], recv_sem=w_recv_sem.at[(p ^ z) - 1],
            device_id=(q * rows + p, core), device_id_type=MESH,
        )

    def root_data_copy(slot):
        return pltpu.make_async_remote_copy(
            src_ref=data, dst_ref=root_data.at[slot],
            send_sem=root_send_sem.at[0], recv_sem=root_data_sem.at[0],
            device_id=(0, core), device_id_type=MESH,
        )

    def root_copy(slot):
        return pltpu.make_async_remote_copy(
            src_ref=out_r, dst_ref=root_in.at[slot],
            send_sem=root_send_sem.at[1], recv_sem=root_recv_sem.at[0],
            device_id=(0, core), device_id_type=MESH,
        )

    def back_copy(p, slot):
        return pltpu.make_async_remote_copy(
            src_ref=back.at[p], dst_ref=home.at[slot],
            send_sem=back_send_sem.at[0], recv_sem=back_recv_sem.at[0],
            device_id=(p * rows + z, core), device_id_type=MESH,
        )

    @pl.when(odd)
    def _():
        for load in loads[:4]:
            load.wait()
        wide = lambda x: jnp.concatenate([x] * 4, 1)
        cl = wide(cl_ref[...])
        code = jnp.where(
            wide(valid_ref[...]) > 0, (wide(pilot_ref[...]) * 16 + (cl & 15)).astype(F32) + 1.0, 0.0
        )
        owner = (cl >> 4) - lax.broadcasted_iota(jnp.int32, (16, 128), 1) // 32
        slots = []
        for a in range(4):
            part = cov_ref[:, 128 * a : 128 * a + 128]
            turned = jnp.concatenate([part] * 4, 0).T
            slots += [turned[32 * j : 32 * j + 32] for j in range(4)]
        row8 = lax.broadcasted_iota(jnp.int32, (8, 128), 0)
        for t in range(n // 4):
            tiles = [jnp.zeros((8, 128), F32)] * 4
            mark = jnp.zeros((8, 128), F32)
            for c in range(16):
                mine = jnp.broadcast_to(owner[c : c + 1], (8, 128)) == 4 * t
                tiles = [jnp.where(mine, slots[c][8 * v : 8 * v + 8], tiles[v]) for v in range(4)]
                mark = jnp.where(mine, jnp.broadcast_to(code[c : c + 1], (8, 128)), mark)
            first = jnp.broadcast_to(tiles[0][0:1], (8, 128))
            second = jnp.broadcast_to(tiles[0][5:6], (8, 128))
            tiles[1] = jnp.where(row8 == 1, first, jnp.where(row8 == 6, second, tiles[1]))
            tiles[3] = jnp.where(row8 == 1, mark, tiles[3])
            tiles = [jnp.where(row8 < 3, pltpu.roll(x, 7, 0), pltpu.roll(x, 5, 0)) for x in tiles]
            for j, tile in enumerate(lane_groups(tiles)):
                send[4 * t + j] = tile
        pl.semaphore_wait(barrier, n)

        @pl.loop(1, n)
        def _(d):
            slot_copy(me ^ (n - d), me, core).start()

        recv[me] = send[me]

    extra = jnp.logical_and(far, z > 0)

    @pl.when(jnp.logical_and(even, extra))
    def _():
        pl.semaphore_wait(barrier, rows + 3)

    @pl.when(jnp.logical_and(even, jnp.logical_not(extra)))
    def _():
        pl.semaphore_wait(barrier, rows + 2)

    for load in loads[4:]:
        load.wait()
    turned = jnp.concatenate([rd_ref[:, f, :] for f in range(8)], 0).T.reshape(16, 8, 128)
    for f, tile in enumerate(block_transpose([turned[:, i, :] for i in range(8)])):
        data[:, f, :] = tile

    @pl.loop(1, rows)
    def _(d):
        data_copy(lax.rem(z + d, rows), z).start()

    @pl.when(far)
    def _():
        root_data_copy(z).start()

    turned = jnp.concatenate([rp_ref[:, f, :] for f in range(8)], 0).T
    for half in range(2):
        tiles = [turned[8 * (8 * half + t) : 8 * (8 * half + t) + 8] for t in range(8)]
        for f, tile in enumerate(block_transpose(tiles)):
            obs[f, :, 128 * half : 128 * half + 128] = tile
    observed = jnp.concatenate([obs[:, i, :] for i in range(8)], 0)
    observed = jnp.concatenate(split(observed, 3), 0)

    @pl.when(odd)
    def _():
        wait_all(recv.at[0 : n - 1, 0:5], recv_sem.at[0])
        pltpu.make_async_remote_copy(
            src_ref=recv.at[:, 0:5], dst_ref=recv.at[:, 0:5],
            send_sem=send_sem.at[0], recv_sem=recv_sem.at[0],
            device_id=(me, pair), device_id_type=MESH,
        ).start()

    @pl.when(even)
    def _():
        wait_all(recv.at[:, 0:5], recv_sem.at[0])

    row32 = lax.broadcasted_iota(jnp.int32, (32, 128), 0)
    codes, matrices = [], []
    for e in range(sets):
        for j in range(4):
            tiles = lane_groups([recv[h * rows + 4 * e + j] for h in range(4)])
            for v, tile in enumerate(tiles):
                trans[e, j, 8 * v : 8 * v + 5] = tile[0:5]
            codes.append(tiles[3][0:1])
            matrices.append(jnp.where(row32 == CODE, 0.0, trans[e, j]))
    codes = jnp.concatenate(codes, 1) - 1.0
    matrices = jnp.concatenate(matrices, 1)
    width = 128 * groups
    bins = lax.broadcasted_iota(jnp.int32, (256, width), 0).astype(F32)
    choose = jnp.where(bins == codes, 1.0, 0.0).astype(BF16)
    places = jnp.where(codes >= 0.0, codes - 16.0 * jnp.floor(codes * 0.0625), -1.0)
    ap_rows = (lax.broadcasted_iota(jnp.int32, (128, width), 0) & 15).astype(F32)
    pick = jnp.where(ap_rows == places, 1.0, 0.0).astype(BF16)
    for g in range(groups):
        out_p[g] = jnp.broadcast_to(places[:, 128 * g : 128 * g + 128], (8, 128))

        @pl.when(z != g)
        def _():
            p_copy(g, z).start()

    if sets == 1:
        rest = jnp.zeros((124, 128), F32)
        column = jnp.concatenate([codes[:, 128 * j : 128 * j + 128] for j in range(4)] + [rest], 0).T
        column_places = jnp.where(column >= 0.0, column - 16.0 * jnp.floor(column * 0.0625), -1.0)

        def alike(x, y):
            blocks = [jnp.where(x[:, j : j + 1] == y, 1.0, 0.0).astype(BF16) for j in range(4)]
            return jnp.concatenate(blocks, 0)

        slot_psi = dot_split(matrices, alike(column, codes), 3)
    else:
        slot_psi = dot_split(dot_split(matrices, choose, 3, True), choose, 3)
    slot_obs = dot(observed, choose)
    slot_obs = slot_obs[0:64] + slot_obs[64:128] + slot_obs[128:192]

    estimates, outers = [], []
    for e in range(sets):
        for j in range(4):
            g = 4 * e + j
            pinv[j] = slot_psi[:, 128 * g : 128 * g + 128]
        psi = {(i, i): (pinv[:, DIAGONAL[i], :] + 1.0, None) for i in range(4)}
        psi.update({p: (pinv[:, REAL[p], :], pinv[:, IMAG[p], :]) for p in PAIRS})
        pi = hermitian_inverse(psi)
        r = {(i, i): (trans[e, :, DIAGONAL[i], :], None) for i in range(4)}
        for p in PAIRS:
            r[p] = (trans[e, :, REAL[p], :], trans[e, :, IMAG[p], :])
        w = {}
        for i in range(4):
            for k in range(4):
                acc = None
                for l in range(4):
                    acc = add_products(acc, get(r, i, l), get(pi, l, k))
                w[i, k] = acc
        err = {}
        for i, k in ENTRIES:
            acc = None
            for l in range(4):
                acc = add_products(acc, w[i, l], get(r, l, k))
            re = r[i, k][0] - acc[0]
            err[i, k] = (re, None) if i == k else (re, r[i, k][1] - acc[1])
        for j in range(4):
            g = 4 * e + j
            cols = slice(128 * g, 128 * g + 128)
            y = [(slot_obs[8 * i : 8 * i + 8, cols], slot_obs[32 + 8 * i : 40 + 8 * i, cols]) for i in range(4)]
            h = []
            for i in range(4):
                acc = None
                for k in range(4):
                    wr, wi = w[i, k]
                    acc = add_products(acc, (wr[j : j + 1], wi[j : j + 1]), y[k])
                h.append(acc)
            estimates.append(h)
            out = []
            for i in range(4):
                out.append(h[i][0] * h[i][0] + h[i][1] * h[i][1] + err[i, i][0][j : j + 1])
            for i, k in PAIRS:
                out.append(h[i][0] * h[k][0] + h[i][1] * h[k][1] + err[i, k][0][j : j + 1])
                out.append(h[i][1] * h[k][0] - h[i][0] * h[k][1] + err[i, k][1][j : j + 1])
            outers.append(jnp.concatenate(out, 0))
    outers = jnp.concatenate(outers, 1)
    if sets == 1:
        slot_sum = dot_split(outers, alike(column_places, places), 3)
    else:
        summed = dot_split(outers, pick, 3, True)
        own_f = lax.broadcasted_iota(jnp.int32, (8, 128), 1) // 16 == lax.broadcasted_iota(jnp.int32, (8, 128), 0)
        comps = [
            jnp.sum(jnp.where(own_f, summed[8 * x : 8 * x + 8], 0.0), 0, keepdims=True) for x in range(16)
        ]
        masked = jnp.concatenate([jnp.where(own_f, c, 0.0) for c in comps], 0)
        slot_sum = dot_split(masked, pick, 3)
    for g in range(groups):
        cols = slice(128 * g, 128 * g + 128)
        h = estimates[g]
        parts = [slot_sum[8 * x : 8 * x + 8, cols] for x in range(16)]
        gs = hermitian_inverse(from_parts([c + 1.0 if x < 4 else c for x, c in enumerate(parts)]))
        power = None
        for i in range(4):
            acc = None
            for k in range(4):
                acc = add_products(acc, get(gs, i, k), h[k])
            out_w[g, 8 * i : 8 * i + 8] = acc[0]
            out_w[g, 32 + 8 * i : 40 + 8 * i] = acc[1]
            term = h[i][0] * acc[0] + h[i][1] * acc[1]
            power = term if power is None else power + term
        out_w[g, 64:72] = power

        if g == 0:
            @pl.when(far)
            def _():
                quarter = lax.broadcasted_iota(jnp.int32, (8, 128), 1) // 32
                for m in range(2):
                    packed = out_w[0, 32 * m : 32 * m + 8]
                    for j in range(1, 4):
                        at = 32 * m + 8 * j
                        packed = jnp.where(quarter == j, pltpu.roll(out_w[0, at : at + 8], 32 * j, 1), packed)
                    out_r[8 * m : 8 * m + 8] = packed
                out_r[16:24] = out_w[0, 64:72]
                root_copy(z).start()

        @pl.when(z != g)
        def _():
            w_copy(g, z).start()

    row16 = lax.broadcasted_iota(jnp.int32, (16, 128), 0).astype(F32)
    in_p[z] = out_p[z]
    in_w[z] = out_w[z]
    for k in range(rows):
        p = z ^ k
        if k == 1:
            wait_all(data_in.at[0 : rows - 1], data_recv_sem.at[0])
            wait_all(in_p.at[0 : rows - 1], p_recv_sem.at[0])
        place = in_p[p]
        hot = jnp.where(row16 == jnp.concatenate([place, place], 0), 1.0, 0.0).astype(BF16)
        for i in range(8):
            for half in range(2):
                at = 128 * half + 16 * i
                ones[k % 2, at : at + 16, 128 * i : 128 * i + 128] = hot
        source = (data[...] if k == 0 else data_in[p]).reshape(128, 128)
        left = jnp.concatenate(split(source, 2), 1)
        for i in range(4):
            cols = slice(256 * i, 256 * i + 256)
            wide_out = dot(left, ones[k % 2, :, cols])
            gathered[k, 2 * i] = wide_out[:, :128].reshape(16, 8, 128)
            gathered[k, 2 * i + 1] = wide_out[:, 128:].reshape(16, 8, 128)

    sums = [None] * 32
    power = None
    for k in range(rows):
        p = z ^ k
        if k > 0:
            w_copy(p, p).wait_recv()
        u = [in_w[p, 8 * i : 8 * i + 8] for i in range(8)]
        part = in_w[p, 64:72]
        power = part if power is None else power + part
        for s in range(16):
            d = [gathered[k, i, s] for i in range(8)]
            re = im = None
            for i in range(4):
                x = u[i] * d[i] + u[i + 4] * d[i + 4]
                y = u[i] * d[i + 4] - u[i + 4] * d[i]
                re = x if re is None else re + x
                im = y if im is None else im + y
            sums[2 * s] = re if k == 0 else sums[2 * s] + re
            sums[2 * s + 1] = im if k == 0 else sums[2 * s + 1] + im
    for s in range(32):
        held[s] = sums[s]
    for half in range(2):
        tile = jnp.concatenate([held[:, 4 * half + f, :] for f in range(4)], 0).T.reshape(4, 4, 8, 128)
        for j in range(4):
            back[:, 2 * j + half] = tile[:, j]
    turned = jnp.concatenate([power, jnp.zeros((120, 128), F32)], 0).T.reshape(4, 4, 8, 128)
    gains = turned[:, 0].reshape(32, 128)
    for j in range(1, 4):
        gains = gains + pltpu.roll(turned[:, j].reshape(32, 128), 8 * j, 1)
    back[:, 8] = gains.reshape(4, 8, 128)

    to_root = lambda p: jnp.logical_and(p == 0, jnp.logical_and(z == 0, far))
    for p in range(4):
        here = jnp.logical_or(q == p, to_root(p))

        @pl.when(jnp.logical_not(here))
        def _():
            back_copy(p, q).start()

    @pl.when(root)
    def _():
        for load in loads[:2]:
            load.wait()
        cl = jnp.concatenate([cl_ref[...]] * 4, 1)
        valid = jnp.concatenate([valid_ref[...]] * 4, 1)
        mark = jnp.where(valid > 0, (cl & 15).astype(F32) + 1.0, 0.0)
        owner = cl >> 4
        row = lax.broadcasted_iota(jnp.int32, (128, 128), 0)
        quarter = lax.broadcasted_iota(jnp.int32, (128, 128), 1) // 32
        base = jnp.where(((row >> 4) & 3) == quarter, ((row & 15) + 1).astype(F32), -1.0)
        for p in range(rows):
            place = jnp.sum(jnp.where(owner == 3 * rows + p, mark, 0.0), 0, keepdims=True)
            hot = jnp.where(base == place, 1.0, 0.0)
            hot = jnp.concatenate(
                [jnp.where(row < 64, hot, 0.0), jnp.where(row < 64, 0.0, hot)], 1
            ).astype(BF16)
            if p == 0:
                wait_all(root_data, root_data_sem.at[0])
            left = jnp.concatenate(split(root_data[p].reshape(128, 128), 2), 1)
            both = dot(left, jnp.concatenate([hot, hot], 0))
            for m in range(2):
                root_held[p, m] = both[:, 128 * m : 128 * m + 128].reshape(16, 8, 128)
        sums = [None] * 32
        power = None
        for p in range(rows):
            if p == 0:
                wait_all(root_in, root_recv_sem.at[0])
            u, v, part = (root_in[p, 8 * m : 8 * m + 8] for m in range(3))
            power = part if p == 0 else power + part
            for s in range(16):
                x, y = root_held[p, 0, s], root_held[p, 1, s]
                re, im = u * x + v * y, u * y - v * x
                sums[2 * s] = re if p == 0 else sums[2 * s] + re
                sums[2 * s + 1] = im if p == 0 else sums[2 * s + 1] + im
        for s in range(32):
            x = sums[s] + pltpu.roll(sums[s], 64, 1)
            held[s] = x + pltpu.roll(x, 32, 1)
        for half in range(2):
            tile = jnp.concatenate([held[:, 4 * half + f, :] for f in range(4)], 0).T
            for j in range(4):
                home[3, 2 * j + half] = tile[8 * j : 8 * j + 8]
        turned = jnp.concatenate([power, jnp.zeros((120, 128), F32)], 0).T
        gains = turned[0:8]
        for j in range(1, 4):
            gains = gains + pltpu.roll(turned[8 * j : 8 * j + 8], 8 * j, 1)
        home[3, 8] = gains

    home[q] = back[q]

    @pl.when(jnp.logical_not(root))
    def _():
        wait_all(home.at[0:3], back_recv_sem.at[0])

    @pl.when(root)
    def _():
        wait_all(home.at[0:2], back_recv_sem.at[0])

    @pl.when(odd)
    def _():
        wait_all(send.at[:, 0:5], send_sem.at[0])
        wait_all(send.at[0 : n - 1, 0:5], send_sem.at[1])

    wait_all(data_in.at[0 : rows - 1], data_send_sem.at[0])
    wait_all(in_p.at[0 : rows - 1], p_send_sem.at[0])
    wait_all(in_w.at[0 : rows - 1], w_send_sem.at[0])

    @pl.when(to_root(0))
    def _():
        wait_all(back.at[0:2], back_send_sem.at[0])

    @pl.when(jnp.logical_not(to_root(0)))
    def _():
        wait_all(back.at[0:3], back_send_sem.at[0])

    @pl.when(far)
    def _():
        root_data_copy(z).wait_send()
        root_copy(z).wait_send()


def finish(home, sym_ref, gain_ref):
    total = (home[0] + home[1]) + (home[2] + home[3])
    for j in range(4):
        for f in range(8):
            tile = total[2 * j + f // 4]
            sym_ref[8 * j : 8 * j + 8, f, :] = tile[:, 32 * (f % 4) : 32 * (f % 4) + 32]
    gains = jnp.concatenate([total[8], jnp.zeros((120, 128), F32)], 0).T
    gain_ref[...] = jnp.concatenate([gains[8 * j : 8 * j + 8, 0:8] for j in range(4)], 1)


def body(n, covariances, clusters, cluster_valid, pilots, received_pilot, received_data):
    vmem = pl.BlockSpec(memory_space=pltpu.VMEM)
    rows = n // 4
    home = pl.pallas_call(
        functools.partial(kernel, n),
        out_shape=pltpu.VMEM((4, 9, 8, 128), F32),
        in_specs=[pl.BlockSpec(memory_space=pltpu.HBM)] * 6,
        out_specs=vmem,
        scratch_shapes=[
            pltpu.VMEM((32, 512), F32),
            pltpu.VMEM((16, 32), jnp.int32),
            pltpu.VMEM((16, 32), jnp.int32),
            pltpu.VMEM((1, 32), jnp.int32),
            pltpu.VMEM((16, 8, 128), F32),
            pltpu.VMEM((16, 8, 128), F32),
            pltpu.VMEM((n, 8, 128), F32),
            pltpu.VMEM((n, 8, 128), F32),
            pltpu.VMEM((n // 16, 4, 32, 128), F32),
            pltpu.VMEM((4, 32, 128), F32),
            pltpu.VMEM((8, 8, 256), F32),
            pltpu.VMEM((16, 8, 128), F32),
            pltpu.VMEM((rows, 16, 8, 128), F32),
            pltpu.VMEM((2, 256, 1024), BF16),
            pltpu.VMEM((rows, 8, 16, 8, 128), F32),
            pltpu.VMEM((32, 8, 128), F32),
            pltpu.VMEM((rows, 8, 128), F32),
            pltpu.VMEM((rows, 8, 128), F32),
            pltpu.VMEM((rows, 72, 128), F32),
            pltpu.VMEM((rows, 72, 128), F32),
            pltpu.VMEM((4, 9, 8, 128), F32),
            pltpu.VMEM((rows, 16, 8, 128), F32),
            pltpu.VMEM((rows, 2, 16, 8, 128), F32),
            pltpu.VMEM((24, 128), F32),
            pltpu.VMEM((rows, 24, 128), F32),
            pltpu.SemaphoreType.DMA((6,)),
            pltpu.SemaphoreType.DMA((2,)),
            pltpu.SemaphoreType.DMA((1,)),
            pltpu.SemaphoreType.DMA((1,)),
            pltpu.SemaphoreType.DMA((1,)),
            pltpu.SemaphoreType.DMA((1,)),
            pltpu.SemaphoreType.DMA((1,)),
            pltpu.SemaphoreType.DMA((1,)),
            pltpu.SemaphoreType.DMA((rows - 1,)),
            pltpu.SemaphoreType.DMA((1,)),
            pltpu.SemaphoreType.DMA((1,)),
            pltpu.SemaphoreType.DMA((2,)),
            pltpu.SemaphoreType.DMA((1,)),
            pltpu.SemaphoreType.DMA((1,)),
        ],
        compiler_params=pltpu.CompilerParams(
            collective_id=0, has_side_effects=True, vmem_limit_bytes=65000 * 1024
        ),
    )(covariances, clusters.T, cluster_valid.T, pilots.reshape(1, -1), received_pilot, received_data)
    symbols, gain = pl.pallas_call(
        finish,
        out_shape=(jax.ShapeDtypeStruct((32, 8, 32), F32), jax.ShapeDtypeStruct((8, 32), F32)),
        in_specs=[vmem],
        out_specs=(vmem, vmem),
    )(pltpu.with_memory_space_constraint(home, pltpu.VMEM))
    return symbols, gain.T


def solution(mesh):
    placed = (
        P("ap", None),
        P("ap", None),
        P("ap", None),
        P("ap"),
        P("ap", "sc", None),
        P("ap", "sc", None),
    )
    return jax.shard_map(
        functools.partial(body, mesh.shape["ap"]),
        mesh=mesh,
        in_specs=placed,
        out_specs=(P("ap", "sc", None), P("ap", "sc")),
        check_vma=False,
    )
```

```python
import functools

import jax
import jax.numpy as jnp
from jax import lax
from jax.experimental import pallas as pl
from jax.experimental.pallas import tpu as pltpu
from jax.sharding import PartitionSpec as P

F32 = jnp.float32
BF16 = jnp.bfloat16
MESH = pl.DeviceIdType.MESH
PAIRS = [(0, 1), (0, 2), (0, 3), (1, 2), (1, 3), (2, 3)]
ENTRIES = [(i, i) for i in range(4)] + PAIRS
DIAGONAL = [8, 11, 9, 12]
REAL = dict(zip(PAIRS, [0, 1, 2, 3, 4, 10]))
IMAG = dict(zip(PAIRS, [16, 17, 18, 19, 20, 26]))
CODE = 24
DIRECT = 2


def split(x, parts):
    out = []
    for _ in range(parts - 1):
        head = x.astype(BF16)
        out.append(head)
        x = x - head.astype(F32)
    out.append(x.astype(BF16))
    return out


def dot(a, b, rhs_transposed=False):
    dims = (((1,), (1,)), ((), ())) if rhs_transposed else (((1,), (0,)), ((), ()))
    return lax.dot_general(a, b, dims, preferred_element_type=F32)


def dot_split(a, b, parts, rhs_transposed=False):
    rows = a.shape[0]
    full = dot(jnp.concatenate(split(a, parts), 0), b, rhs_transposed)
    total = full[:rows]
    for p in range(1, parts):
        total = total + full[p * rows : (p + 1) * rows]
    return total


def get(h, i, j):
    if i == j:
        return h[i, i]
    if i < j:
        return h[i, j]
    re, im = h[j, i]
    return re, -im


def hermitian_inverse(h):
    h = dict(h)
    for k in range(4):
        inv = 1.0 / h[k, k][0]
        col = {i: get(h, i, k) for i in range(4) if i != k}
        scaled = {i: (c[0] * inv, c[1] * inv) for i, c in col.items()}
        new = {}
        for i, j in ENTRIES:
            if i == k and j == k:
                new[i, j] = (-inv, None)
            elif i == k:
                re, im = scaled[j]
                new[i, j] = (re, -im)
            elif j == k:
                new[i, j] = scaled[i]
            elif i == j:
                a, s = col[i], scaled[i]
                new[i, j] = (h[i, i][0] - (a[0] * s[0] + a[1] * s[1]), None)
            else:
                a, s = scaled[i], col[j]
                re = h[i, j][0] - (a[0] * s[0] + a[1] * s[1])
                im = h[i, j][1] - (a[1] * s[0] - a[0] * s[1])
                new[i, j] = (re, im)
        h = new
    return {k: (-v[0], None if v[1] is None else -v[1]) for k, v in h.items()}


def from_parts(x):
    h = {(i, i): (x[i], None) for i in range(4)}
    for q, p in enumerate(PAIRS):
        h[p] = (x[4 + 2 * q], x[5 + 2 * q])
    return h


def add_products(acc, a, b):
    re, im = a[0] * b[0], None
    if a[1] is not None and b[1] is not None:
        re = re - a[1] * b[1]
    if b[1] is not None:
        im = a[0] * b[1]
    if a[1] is not None:
        im = a[1] * b[0] if im is None else im + a[1] * b[0]
    if acc is None:
        return re, im
    if im is None:
        im = acc[1]
    elif acc[1] is not None:
        im = acc[1] + im
    return acc[0] + re, im


def block_transpose(x):
    lane_block = lax.broadcasted_iota(jnp.int32, x[0].shape, 1) // 16
    x = list(x)
    for m in (1, 2, 4):
        upper = (lane_block & m) != 0
        new = list(x)
        for p in range(8):
            if p & m:
                continue
            q = p + m
            new[p] = jnp.where(upper, pltpu.roll(x[q], 16 * m, 1), x[p])
            new[q] = jnp.where(upper, x[q], pltpu.roll(x[p], 128 - 16 * m, 1))
        x = new
    return x


def lane_groups(x):
    lane_block = lax.broadcasted_iota(jnp.int32, x[0].shape, 1) // 32
    x = list(x)
    for m in (1, 2):
        upper = (lane_block & m) != 0
        new = list(x)
        for p in range(4):
            if p & m:
                continue
            q = p + m
            new[p] = jnp.where(upper, pltpu.roll(x[q], 32 * m, 1), x[p])
            new[q] = jnp.where(upper, x[q], pltpu.roll(x[p], 128 - 32 * m, 1))
        x = new
    return x


def kernel(
    n, cov_hbm, cl_hbm, valid_hbm, pilot_hbm, rp_hbm, rd_hbm, home,
    cov_ref, cl_ref, valid_ref, pilot_ref, rp_ref, rd_ref,
    send, recv, trans, pinv, obs, data, data_in, ones, gathered, held, out_p, in_p, out_w, in_w, back,
    root_data, root_held, out_r, root_in,
    load_sem, send_sem, recv_sem, data_send_sem, data_recv_sem,
    p_send_sem, p_recv_sem, w_send_sem, w_recv_sem, back_send_sem, back_recv_sem,
    root_send_sem, root_data_sem, root_recv_sem,
):
    me = lax.axis_index("ap")
    core = lax.axis_index("sc")
    rows = n // 4
    sets = n // 16
    groups = 4 * sets
    q, z = lax.div(me, rows), lax.rem(me, rows)

    pairs = [
        (cl_hbm, cl_ref), (valid_hbm, valid_ref), (pilot_hbm, pilot_ref),
        (cov_hbm, cov_ref), (rp_hbm, rp_ref), (rd_hbm, rd_ref),
    ]
    loads = [pltpu.make_async_copy(a, b, load_sem.at[min(i, 4)]) for i, (a, b) in enumerate(pairs)]
    odd = lax.rem(core, 2) == 1
    pair = core ^ 1
    even = jnp.logical_not(odd)
    root = jnp.logical_and(me == 0, even)
    far = jnp.logical_and(q >= DIRECT, even)
    barrier = pltpu.get_barrier_semaphore()

    def greet(p, c):
        pl.semaphore_signal(barrier, inc=1, device_id=(p, c), device_id_type=MESH)

    @pl.when(odd)
    def _():
        for load in loads[:4]:
            load.start()

        @pl.loop(1, n)
        def _(d):
            greet(me ^ (n - d), core)

    @pl.when(jnp.logical_not(odd))
    def _():
        greet(me, pair)

        @pl.loop(1, rows)
        def _(d):
            greet(q * rows + (z ^ d), core)

        for d in range(1, 4):
            greet((q ^ d) * rows + z, core)

    @pl.when(root)
    def _():
        for load in loads[:2]:
            load.start()

        for d in range(DIRECT, 4):
            @pl.loop(1, rows)
            def _(c):
                greet(d * rows + c, core)

    for load in loads[4:]:
        load.start()

    trans[...] = jnp.zeros_like(trans)
    ones[...] = jnp.zeros_like(ones)

    def slot_copy(p, slot, to):
        return pltpu.make_async_remote_copy(
            src_ref=send.at[p, 0:5], dst_ref=recv.at[slot, 0:5],
            send_sem=send_sem.at[lax.rem(to, 2)], recv_sem=recv_sem.at[0],
            device_id=(p, to), device_id_type=MESH,
        )

    def wait_all(ref, sem):
        pltpu.make_async_copy(ref, ref, sem).wait()

    def data_copy(p, slot):
        return pltpu.make_async_remote_copy(
            src_ref=data, dst_ref=data_in.at[slot],
            send_sem=data_send_sem.at[0], recv_sem=data_recv_sem.at[0],
            device_id=(q * rows + p, core), device_id_type=MESH,
        )

    def p_copy(p, slot):
        return pltpu.make_async_remote_copy(
            src_ref=out_p.at[p], dst_ref=in_p.at[slot],
            send_sem=p_send_sem.at[0], recv_sem=p_recv_sem.at[0],
            device_id=(q * rows + p, core), device_id_type=MESH,
        )

    def w_copy(p, slot):
        return pltpu.make_async_remote_copy(
            src_ref=out_w.at[p], dst_ref=in_w.at[slot],
            send_sem=w_send_sem.at[0], recv_sem=w_recv_sem.at[(p ^ z) - 1],
            device_id=(q * rows + p, core), device_id_type=MESH,
        )

    def root_data_copy(slot):
        return pltpu.make_async_remote_copy(
            src_ref=data, dst_ref=root_data.at[slot],
            send_sem=root_send_sem.at[0], recv_sem=root_data_sem.at[0],
            device_id=(0, core), device_id_type=MESH,
        )

    def root_copy(slot):
        return pltpu.make_async_remote_copy(
            src_ref=out_r, dst_ref=root_in.at[slot],
            send_sem=root_send_sem.at[1], recv_sem=root_recv_sem.at[0],
            device_id=(0, core), device_id_type=MESH,
        )

    def back_copy(p, slot):
        return pltpu.make_async_remote_copy(
            src_ref=back.at[p], dst_ref=home.at[slot],
            send_sem=back_send_sem.at[0], recv_sem=back_recv_sem.at[0],
            device_id=(p * rows + z, core), device_id_type=MESH,
        )

    @pl.when(odd)
    def _():
        for load in loads[:4]:
            load.wait()
        wide = lambda x: jnp.concatenate([x] * 4, 1)
        cl = wide(cl_ref[...])
        code = jnp.where(
            wide(valid_ref[...]) > 0, (wide(pilot_ref[...]) * 16 + (cl & 15)).astype(F32) + 1.0, 0.0
        )
        owner = (cl >> 4) - lax.broadcasted_iota(jnp.int32, (16, 128), 1) // 32
        slots = []
        for a in range(4):
            part = cov_ref[:, 128 * a : 128 * a + 128]
            turned = jnp.concatenate([part] * 4, 0).T
            slots += [turned[32 * j : 32 * j + 32] for j in range(4)]
        row8 = lax.broadcasted_iota(jnp.int32, (8, 128), 0)
        for t in range(n // 4):
            tiles = [jnp.zeros((8, 128), F32)] * 4
            mark = jnp.zeros((8, 128), F32)
            for c in range(16):
                mine = jnp.broadcast_to(owner[c : c + 1], (8, 128)) == 4 * t
                tiles = [jnp.where(mine, slots[c][8 * v : 8 * v + 8], tiles[v]) for v in range(4)]
                mark = jnp.where(mine, jnp.broadcast_to(code[c : c + 1], (8, 128)), mark)
            first = jnp.broadcast_to(tiles[0][0:1], (8, 128))
            second = jnp.broadcast_to(tiles[0][5:6], (8, 128))
            tiles[1] = jnp.where(row8 == 1, first, jnp.where(row8 == 6, second, tiles[1]))
            tiles[3] = jnp.where(row8 == 1, mark, tiles[3])
            tiles = [jnp.where(row8 < 3, pltpu.roll(x, 7, 0), pltpu.roll(x, 5, 0)) for x in tiles]
            for j, tile in enumerate(lane_groups(tiles)):
                send[4 * t + j] = tile
        pl.semaphore_wait(barrier, n)

        @pl.loop(1, n)
        def _(d):
            slot_copy(me ^ (n - d), me, core).start()

        recv[me] = send[me]

    extra = jnp.logical_and(far, z > 0)

    @pl.when(jnp.logical_and(even, extra))
    def _():
        pl.semaphore_wait(barrier, rows + 3)

    @pl.when(jnp.logical_and(even, jnp.logical_not(extra)))
    def _():
        pl.semaphore_wait(barrier, rows + 2)

    wait_all(data_in.at[0:2], load_sem.at[4])
    turned = jnp.concatenate([rd_ref[:, f, :] for f in range(8)], 0).T.reshape(16, 8, 128)
    for f, tile in enumerate(block_transpose([turned[:, i, :] for i in range(8)])):
        data[:, f, :] = tile

    @pl.loop(1, rows)
    def _(d):
        data_copy(lax.rem(z + d, rows), z).start()

    @pl.when(far)
    def _():
        root_data_copy(me - DIRECT * rows).start()

    turned = jnp.concatenate([rp_ref[:, f, :] for f in range(8)], 0).T
    for half in range(2):
        tiles = [turned[8 * (8 * half + t) : 8 * (8 * half + t) + 8] for t in range(8)]
        for f, tile in enumerate(block_transpose(tiles)):
            obs[f, :, 128 * half : 128 * half + 128] = tile
    observed = jnp.concatenate([obs[:, i, :] for i in range(8)], 0)
    observed = jnp.concatenate(split(observed, 3), 0)

    @pl.when(odd)
    def _():
        wait_all(recv.at[0 : n - 1, 0:5], recv_sem.at[0])
        pltpu.make_async_remote_copy(
            src_ref=recv.at[:, 0:5], dst_ref=recv.at[:, 0:5],
            send_sem=send_sem.at[0], recv_sem=recv_sem.at[0],
            device_id=(me, pair), device_id_type=MESH,
        ).start()

    @pl.when(even)
    def _():
        wait_all(recv.at[:, 0:5], recv_sem.at[0])

    row32 = lax.broadcasted_iota(jnp.int32, (32, 128), 0)
    codes, matrices = [], []
    for e in range(sets):
        for j in range(4):
            tiles = lane_groups([recv[h * rows + 4 * e + j] for h in range(4)])
            for v, tile in enumerate(tiles):
                trans[e, j, 8 * v : 8 * v + 5] = tile[0:5]
            codes.append(tiles[3][0:1])
            matrices.append(jnp.where(row32 == CODE, 0.0, trans[e, j]))
    codes = jnp.concatenate(codes, 1) - 1.0
    matrices = jnp.concatenate(matrices, 1)
    width = 128 * groups
    bins = lax.broadcasted_iota(jnp.int32, (256, width), 0).astype(F32)
    choose = jnp.where(bins == codes, 1.0, 0.0).astype(BF16)
    places = jnp.where(codes >= 0.0, codes - 16.0 * jnp.floor(codes * 0.0625), -1.0)
    ap_rows = (lax.broadcasted_iota(jnp.int32, (128, width), 0) & 15).astype(F32)
    pick = jnp.where(ap_rows == places, 1.0, 0.0).astype(BF16)
    for g in range(groups):
        out_p[g] = jnp.broadcast_to(places[:, 128 * g : 128 * g + 128], (8, 128))

        @pl.when(z != g)
        def _():
            p_copy(g, z).start()

    if sets == 1:
        rest = jnp.zeros((124, 128), F32)
        column = jnp.concatenate([codes[:, 128 * j : 128 * j + 128] for j in range(4)] + [rest], 0).T
        column_places = jnp.where(column >= 0.0, column - 16.0 * jnp.floor(column * 0.0625), -1.0)

        def alike(x, y):
            blocks = [jnp.where(x[:, j : j + 1] == y, 1.0, 0.0).astype(BF16) for j in range(4)]
            return jnp.concatenate(blocks, 0)

        slot_psi = dot_split(matrices, alike(column, codes), 3)
    else:
        slot_psi = dot_split(dot_split(matrices, choose, 3, True), choose, 3)
    slot_obs = dot(observed, choose)
    slot_obs = slot_obs[0:64] + slot_obs[64:128] + slot_obs[128:192]

    estimates, outers = [], []
    for e in range(sets):
        for j in range(4):
            g = 4 * e + j
            pinv[j] = slot_psi[:, 128 * g : 128 * g + 128]
        psi = {(i, i): (pinv[:, DIAGONAL[i], :] + 1.0, None) for i in range(4)}
        psi.update({p: (pinv[:, REAL[p], :], pinv[:, IMAG[p], :]) for p in PAIRS})
        pi = hermitian_inverse(psi)
        r = {(i, i): (trans[e, :, DIAGONAL[i], :], None) for i in range(4)}
        for p in PAIRS:
            r[p] = (trans[e, :, REAL[p], :], trans[e, :, IMAG[p], :])
        w = {}
        for i in range(4):
            for k in range(4):
                acc = None
                for l in range(4):
                    acc = add_products(acc, get(r, i, l), get(pi, l, k))
                w[i, k] = acc
        err = {}
        for i, k in ENTRIES:
            acc = None
            for l in range(4):
                acc = add_products(acc, w[i, l], get(r, l, k))
            re = r[i, k][0] - acc[0]
            err[i, k] = (re, None) if i == k else (re, r[i, k][1] - acc[1])
        for j in range(4):
            g = 4 * e + j
            cols = slice(128 * g, 128 * g + 128)
            y = [(slot_obs[8 * i : 8 * i + 8, cols], slot_obs[32 + 8 * i : 40 + 8 * i, cols]) for i in range(4)]
            h = []
            for i in range(4):
                acc = None
                for k in range(4):
                    wr, wi = w[i, k]
                    acc = add_products(acc, (wr[j : j + 1], wi[j : j + 1]), y[k])
                h.append(acc)
            estimates.append(h)
            out = []
            for i in range(4):
                out.append(h[i][0] * h[i][0] + h[i][1] * h[i][1] + err[i, i][0][j : j + 1])
            for i, k in PAIRS:
                out.append(h[i][0] * h[k][0] + h[i][1] * h[k][1] + err[i, k][0][j : j + 1])
                out.append(h[i][1] * h[k][0] - h[i][0] * h[k][1] + err[i, k][1][j : j + 1])
            outers.append(jnp.concatenate(out, 0))
    outers = jnp.concatenate(outers, 1)
    if sets == 1:
        slot_sum = dot_split(outers, alike(column_places, places), 3)
    else:
        summed = dot_split(outers, pick, 3, True)
        own_f = lax.broadcasted_iota(jnp.int32, (8, 128), 1) // 16 == lax.broadcasted_iota(jnp.int32, (8, 128), 0)
        comps = [
            jnp.sum(jnp.where(own_f, summed[8 * x : 8 * x + 8], 0.0), 0, keepdims=True) for x in range(16)
        ]
        masked = jnp.concatenate([jnp.where(own_f, c, 0.0) for c in comps], 0)
        slot_sum = dot_split(masked, pick, 3)
    for g in range(groups):
        cols = slice(128 * g, 128 * g + 128)
        h = estimates[g]
        parts = [slot_sum[8 * x : 8 * x + 8, cols] for x in range(16)]
        gs = hermitian_inverse(from_parts([c + 1.0 if x < 4 else c for x, c in enumerate(parts)]))
        power = None
        for i in range(4):
            acc = None
            for k in range(4):
                acc = add_products(acc, get(gs, i, k), h[k])
            out_w[g, 8 * i : 8 * i + 8] = acc[0]
            out_w[g, 32 + 8 * i : 40 + 8 * i] = acc[1]
            term = h[i][0] * acc[0] + h[i][1] * acc[1]
            power = term if power is None else power + term
        out_w[g, 64:72] = power

        if g == 0:
            @pl.when(far)
            def _():
                quarter = lax.broadcasted_iota(jnp.int32, (8, 128), 1) // 32
                for m in range(2):
                    packed = out_w[0, 32 * m : 32 * m + 8]
                    for j in range(1, 4):
                        at = 32 * m + 8 * j
                        packed = jnp.where(quarter == j, pltpu.roll(out_w[0, at : at + 8], 32 * j, 1), packed)
                    out_r[8 * m : 8 * m + 8] = packed
                out_r[16:24] = out_w[0, 64:72]
                root_copy(me - DIRECT * rows).start()

        @pl.when(z != g)
        def _():
            w_copy(g, z).start()

    row16 = lax.broadcasted_iota(jnp.int32, (16, 128), 0).astype(F32)
    in_p[z] = out_p[z]
    in_w[z] = out_w[z]
    for k in range(rows):
        p = z ^ k
        if k == 1:
            wait_all(data_in.at[0 : rows - 1], data_recv_sem.at[0])
            wait_all(in_p.at[0 : rows - 1], p_recv_sem.at[0])
        place = in_p[p]
        hot = jnp.where(row16 == jnp.concatenate([place, place], 0), 1.0, 0.0).astype(BF16)
        for i in range(8):
            for half in range(2):
                at = 128 * half + 16 * i
                ones[k % 2, at : at + 16, 128 * i : 128 * i + 128] = hot
        source = (data[...] if k == 0 else data_in[p]).reshape(128, 128)
        left = jnp.concatenate(split(source, 2), 1)
        for i in range(4):
            cols = slice(256 * i, 256 * i + 256)
            wide_out = dot(left, ones[k % 2, :, cols])
            gathered[k, 2 * i] = wide_out[:, :128].reshape(16, 8, 128)
            gathered[k, 2 * i + 1] = wide_out[:, 128:].reshape(16, 8, 128)

    sums = [None] * 32
    power = None
    for k in range(rows):
        p = z ^ k
        if k > 0:
            w_copy(p, p).wait_recv()
        u = [in_w[p, 8 * i : 8 * i + 8] for i in range(8)]
        part = in_w[p, 64:72]
        power = part if power is None else power + part
        for s in range(16):
            d = [gathered[k, i, s] for i in range(8)]
            re = im = None
            for i in range(4):
                x = u[i] * d[i] + u[i + 4] * d[i + 4]
                y = u[i] * d[i + 4] - u[i + 4] * d[i]
                re = x if re is None else re + x
                im = y if im is None else im + y
            sums[2 * s] = re if k == 0 else sums[2 * s] + re
            sums[2 * s + 1] = im if k == 0 else sums[2 * s + 1] + im
    for s in range(32):
        held[s] = sums[s]
    for half in range(2):
        tile = jnp.concatenate([held[:, 4 * half + f, :] for f in range(4)], 0).T.reshape(4, 4, 8, 128)
        for j in range(4):
            back[:, 2 * j + half] = tile[:, j]
    turned = jnp.concatenate([power, jnp.zeros((120, 128), F32)], 0).T.reshape(4, 4, 8, 128)
    gains = turned[:, 0].reshape(32, 128)
    for j in range(1, 4):
        gains = gains + pltpu.roll(turned[:, j].reshape(32, 128), 8 * j, 1)
    back[:, 8] = gains.reshape(4, 8, 128)

    to_root = lambda p: jnp.logical_and(p == 0, jnp.logical_and(z == 0, far))
    for p in range(4):
        here = jnp.logical_or(q == p, to_root(p))

        @pl.when(jnp.logical_not(here))
        def _():
            back_copy(p, q).start()

    @pl.when(root)
    def _():
        for load in loads[:2]:
            load.wait()
        cl = jnp.concatenate([cl_ref[...]] * 4, 1)
        valid = jnp.concatenate([valid_ref[...]] * 4, 1)
        mark = jnp.where(valid > 0, (cl & 15).astype(F32) + 1.0, 0.0)
        owner = cl >> 4
        row = lax.broadcasted_iota(jnp.int32, (128, 128), 0)
        quarter = lax.broadcasted_iota(jnp.int32, (128, 128), 1) // 32
        base = jnp.where(((row >> 4) & 3) == quarter, ((row & 15) + 1).astype(F32), -1.0)
        for p in range((4 - DIRECT) * rows):
            place = jnp.sum(jnp.where(owner == DIRECT * rows + p, mark, 0.0), 0, keepdims=True)
            hot = jnp.where(base == place, 1.0, 0.0)
            hot = jnp.concatenate(
                [jnp.where(row < 64, hot, 0.0), jnp.where(row < 64, 0.0, hot)], 1
            ).astype(BF16)
            if p == 0:
                wait_all(root_data, root_data_sem.at[0])
            left = jnp.concatenate(split(root_data[p].reshape(128, 128), 2), 1)
            both = dot(left, jnp.concatenate([hot, hot], 0))
            for m in range(2):
                root_held[p, m] = both[:, 128 * m : 128 * m + 128].reshape(16, 8, 128)
        sums = [None] * 32
        power = None
        for p in range((4 - DIRECT) * rows):
            if p == 0:
                wait_all(root_in, root_recv_sem.at[0])
            u, v, part = (root_in[p, 8 * m : 8 * m + 8] for m in range(3))
            power = part if p == 0 else power + part
            for s in range(16):
                x, y = root_held[p, 0, s], root_held[p, 1, s]
                re, im = u * x + v * y, u * y - v * x
                sums[2 * s] = re if p == 0 else sums[2 * s] + re
                sums[2 * s + 1] = im if p == 0 else sums[2 * s + 1] + im
        for s in range(32):
            x = sums[s] + pltpu.roll(sums[s], 64, 1)
            held[s] = x + pltpu.roll(x, 32, 1)
        for half in range(2):
            tile = jnp.concatenate([held[:, 4 * half + f, :] for f in range(4)], 0).T
            for j in range(4):
                home[3, 2 * j + half] = tile[8 * j : 8 * j + 8]
        turned = jnp.concatenate([power, jnp.zeros((120, 128), F32)], 0).T
        gains = turned[0:8]
        for j in range(1, 4):
            gains = gains + pltpu.roll(turned[8 * j : 8 * j + 8], 8 * j, 1)
        home[3, 8] = gains
        for p in range(DIRECT, 3):
            home[p] = jnp.zeros_like(home[p])

    home[q] = back[q]

    @pl.when(jnp.logical_not(root))
    def _():
        wait_all(home.at[0:3], back_recv_sem.at[0])

    @pl.when(root)
    def _():
        wait_all(home.at[0 : DIRECT - 1], back_recv_sem.at[0])

    @pl.when(odd)
    def _():
        wait_all(send.at[:, 0:5], send_sem.at[0])
        wait_all(send.at[0 : n - 1, 0:5], send_sem.at[1])

    wait_all(data_in.at[0 : rows - 1], data_send_sem.at[0])
    wait_all(in_p.at[0 : rows - 1], p_send_sem.at[0])
    wait_all(in_w.at[0 : rows - 1], w_send_sem.at[0])

    @pl.when(to_root(0))
    def _():
        wait_all(back.at[0:2], back_send_sem.at[0])

    @pl.when(jnp.logical_not(to_root(0)))
    def _():
        wait_all(back.at[0:3], back_send_sem.at[0])

    @pl.when(far)
    def _():
        root_data_copy(me - DIRECT * rows).wait_send()
        root_copy(me - DIRECT * rows).wait_send()


def finish(home, sym_ref, gain_ref):
    total = (home[0] + home[1]) + (home[2] + home[3])
    for j in range(4):
        for f in range(8):
            tile = total[2 * j + f // 4]
            sym_ref[8 * j : 8 * j + 8, f, :] = tile[:, 32 * (f % 4) : 32 * (f % 4) + 32]
    gains = jnp.concatenate([total[8], jnp.zeros((120, 128), F32)], 0).T
    gain_ref[...] = jnp.concatenate([gains[8 * j : 8 * j + 8, 0:8] for j in range(4)], 1)


def body(n, covariances, clusters, cluster_valid, pilots, received_pilot, received_data):
    vmem = pl.BlockSpec(memory_space=pltpu.VMEM)
    rows = n // 4
    home = pl.pallas_call(
        functools.partial(kernel, n),
        out_shape=pltpu.VMEM((4, 9, 8, 128), F32),
        in_specs=[pl.BlockSpec(memory_space=pltpu.HBM)] * 6,
        out_specs=vmem,
        scratch_shapes=[
            pltpu.VMEM((32, 512), F32),
            pltpu.VMEM((16, 32), jnp.int32),
            pltpu.VMEM((16, 32), jnp.int32),
            pltpu.VMEM((1, 32), jnp.int32),
            pltpu.VMEM((16, 8, 128), F32),
            pltpu.VMEM((16, 8, 128), F32),
            pltpu.VMEM((n, 8, 128), F32),
            pltpu.VMEM((n, 8, 128), F32),
            pltpu.VMEM((n // 16, 4, 32, 128), F32),
            pltpu.VMEM((4, 32, 128), F32),
            pltpu.VMEM((8, 8, 256), F32),
            pltpu.VMEM((16, 8, 128), F32),
            pltpu.VMEM((rows, 16, 8, 128), F32),
            pltpu.VMEM((2, 256, 1024), BF16),
            pltpu.VMEM((rows, 8, 16, 8, 128), F32),
            pltpu.VMEM((32, 8, 128), F32),
            pltpu.VMEM((rows, 8, 128), F32),
            pltpu.VMEM((rows, 8, 128), F32),
            pltpu.VMEM((rows, 72, 128), F32),
            pltpu.VMEM((rows, 72, 128), F32),
            pltpu.VMEM((4, 9, 8, 128), F32),
            pltpu.VMEM(((4 - DIRECT) * rows, 16, 8, 128), F32),
            pltpu.VMEM(((4 - DIRECT) * rows, 2, 16, 8, 128), F32),
            pltpu.VMEM((24, 128), F32),
            pltpu.VMEM(((4 - DIRECT) * rows, 24, 128), F32),
            pltpu.SemaphoreType.DMA((5,)),
            pltpu.SemaphoreType.DMA((2,)),
            pltpu.SemaphoreType.DMA((1,)),
            pltpu.SemaphoreType.DMA((1,)),
            pltpu.SemaphoreType.DMA((1,)),
            pltpu.SemaphoreType.DMA((1,)),
            pltpu.SemaphoreType.DMA((1,)),
            pltpu.SemaphoreType.DMA((1,)),
            pltpu.SemaphoreType.DMA((rows - 1,)),
            pltpu.SemaphoreType.DMA((1,)),
            pltpu.SemaphoreType.DMA((1,)),
            pltpu.SemaphoreType.DMA((2,)),
            pltpu.SemaphoreType.DMA((1,)),
            pltpu.SemaphoreType.DMA((1,)),
        ],
        compiler_params=pltpu.CompilerParams(
            collective_id=0, has_side_effects=True, vmem_limit_bytes=65000 * 1024
        ),
    )(covariances, clusters.T, cluster_valid.T, pilots.reshape(1, -1), received_pilot, received_data)
    symbols, gain = pl.pallas_call(
        finish,
        out_shape=(jax.ShapeDtypeStruct((32, 8, 32), F32), jax.ShapeDtypeStruct((8, 32), F32)),
        in_specs=[vmem],
        out_specs=(vmem, vmem),
    )(pltpu.with_memory_space_constraint(home, pltpu.VMEM))
    return symbols, gain.T


def solution(mesh):
    placed = (
        P("ap", None),
        P("ap", None),
        P("ap", None),
        P("ap"),
        P("ap", "sc", None),
        P("ap", "sc", None),
    )
    return jax.shard_map(
        functools.partial(body, mesh.shape["ap"]),
        mesh=mesh,
        in_specs=placed,
        out_specs=(P("ap", "sc", None), P("ap", "sc")),
        check_vma=False,
    )
```

```python
import functools

import jax
import jax.numpy as jnp
from jax import lax
from jax.experimental import pallas as pl
from jax.experimental.pallas import tpu as pltpu
from jax.sharding import PartitionSpec as P

F32 = jnp.float32
BF16 = jnp.bfloat16
MESH = pl.DeviceIdType.MESH
PAIRS = [(0, 1), (0, 2), (0, 3), (1, 2), (1, 3), (2, 3)]
ENTRIES = [(i, i) for i in range(4)] + PAIRS
DIAGONAL = [8, 11, 9, 12]
REAL = dict(zip(PAIRS, [0, 1, 2, 3, 4, 10]))
IMAG = dict(zip(PAIRS, [16, 17, 18, 19, 20, 26]))
CODE = 24


def split(x, parts):
    out = []
    for _ in range(parts - 1):
        head = x.astype(BF16)
        out.append(head)
        x = x - head.astype(F32)
    out.append(x.astype(BF16))
    return out


def dot(a, b, rhs_transposed=False):
    dims = (((1,), (1,)), ((), ())) if rhs_transposed else (((1,), (0,)), ((), ()))
    return lax.dot_general(a, b, dims, preferred_element_type=F32)


def dot_split(a, b, parts, rhs_transposed=False):
    rows = a.shape[0]
    full = dot(jnp.concatenate(split(a, parts), 0), b, rhs_transposed)
    total = full[:rows]
    for p in range(1, parts):
        total = total + full[p * rows : (p + 1) * rows]
    return total


def get(h, i, j):
    if i == j:
        return h[i, i]
    if i < j:
        return h[i, j]
    re, im = h[j, i]
    return re, -im


def hermitian_inverse(h):
    h = dict(h)
    for k in range(4):
        inv = 1.0 / h[k, k][0]
        col = {i: get(h, i, k) for i in range(4) if i != k}
        scaled = {i: (c[0] * inv, c[1] * inv) for i, c in col.items()}
        new = {}
        for i, j in ENTRIES:
            if i == k and j == k:
                new[i, j] = (-inv, None)
            elif i == k:
                re, im = scaled[j]
                new[i, j] = (re, -im)
            elif j == k:
                new[i, j] = scaled[i]
            elif i == j:
                a, s = col[i], scaled[i]
                new[i, j] = (h[i, i][0] - (a[0] * s[0] + a[1] * s[1]), None)
            else:
                a, s = scaled[i], col[j]
                re = h[i, j][0] - (a[0] * s[0] + a[1] * s[1])
                im = h[i, j][1] - (a[1] * s[0] - a[0] * s[1])
                new[i, j] = (re, im)
        h = new
    return {k: (-v[0], None if v[1] is None else -v[1]) for k, v in h.items()}


def from_parts(x):
    h = {(i, i): (x[i], None) for i in range(4)}
    for q, p in enumerate(PAIRS):
        h[p] = (x[4 + 2 * q], x[5 + 2 * q])
    return h


def add_products(acc, a, b):
    re, im = a[0] * b[0], None
    if a[1] is not None and b[1] is not None:
        re = re - a[1] * b[1]
    if b[1] is not None:
        im = a[0] * b[1]
    if a[1] is not None:
        im = a[1] * b[0] if im is None else im + a[1] * b[0]
    if acc is None:
        return re, im
    if im is None:
        im = acc[1]
    elif acc[1] is not None:
        im = acc[1] + im
    return acc[0] + re, im


def block_transpose(x):
    lane_block = lax.broadcasted_iota(jnp.int32, x[0].shape, 1) // 16
    x = list(x)
    for m in (1, 2, 4):
        upper = (lane_block & m) != 0
        new = list(x)
        for p in range(8):
            if p & m:
                continue
            q = p + m
            new[p] = jnp.where(upper, pltpu.roll(x[q], 16 * m, 1), x[p])
            new[q] = jnp.where(upper, x[q], pltpu.roll(x[p], 128 - 16 * m, 1))
        x = new
    return x


def lane_groups(x):
    lane_block = lax.broadcasted_iota(jnp.int32, x[0].shape, 1) // 32
    x = list(x)
    for m in (1, 2):
        upper = (lane_block & m) != 0
        new = list(x)
        for p in range(4):
            if p & m:
                continue
            q = p + m
            new[p] = jnp.where(upper, pltpu.roll(x[q], 32 * m, 1), x[p])
            new[q] = jnp.where(upper, x[q], pltpu.roll(x[p], 128 - 32 * m, 1))
        x = new
    return x


def kernel(
    n, cov_hbm, cl_hbm, valid_hbm, pilot_hbm, rp_hbm, rd_hbm, home,
    cov_ref, cl_ref, valid_ref, pilot_ref, rp_ref, rd_ref,
    send, recv, trans, pinv, obs, data, data_in, ones, gathered, held, out_p, in_p, out_w, in_w, back,
    root_data, root_held, out_r, root_in,
    load_sem, send_sem, recv_sem, data_send_sem, data_recv_sem,
    p_send_sem, p_recv_sem, w_send_sem, w_recv_sem, back_send_sem, back_recv_sem,
    root_send_sem, root_data_sem, root_recv_sem,
):
    me = lax.axis_index("ap")
    core = lax.axis_index("sc")
    rows = n // 4
    sets = n // 16
    groups = 4 * sets
    q, z = lax.div(me, rows), lax.rem(me, rows)

    pairs = [
        (cl_hbm, cl_ref), (valid_hbm, valid_ref), (pilot_hbm, pilot_ref),
        (cov_hbm, cov_ref), (rp_hbm, rp_ref), (rd_hbm, rd_ref),
    ]
    loads = [pltpu.make_async_copy(a, b, load_sem.at[min(i, 4)]) for i, (a, b) in enumerate(pairs)]
    odd = lax.rem(core, 2) == 1
    pair = core ^ 1
    even = jnp.logical_not(odd)
    root = jnp.logical_and(me == 0, even)
    far = jnp.logical_and(q == 3, even)
    barrier = pltpu.get_barrier_semaphore()

    def greet(p, c):
        pl.semaphore_signal(barrier, inc=1, device_id=(p, c), device_id_type=MESH)

    @pl.when(odd)
    def _():
        for load in loads[:4]:
            load.start()

        @pl.loop(1, n)
        def _(d):
            greet(me ^ (n - d), core)

    @pl.when(jnp.logical_not(odd))
    def _():
        greet(me, pair)

        @pl.loop(1, rows)
        def _(d):
            greet(q * rows + (z ^ d), core)

        for d in range(1, 4):
            greet((q ^ d) * rows + z, core)

    @pl.when(root)
    def _():
        for load in loads[:2]:
            load.start()

        @pl.loop(1, rows)
        def _(c):
            greet(3 * rows + c, core)

    for load in loads[4:]:
        load.start()

    trans[...] = jnp.zeros_like(trans)
    ones[...] = jnp.zeros_like(ones)

    def slot_copy(p, slot, to):
        return pltpu.make_async_remote_copy(
            src_ref=send.at[p, 0:5], dst_ref=recv.at[slot, 0:5],
            send_sem=send_sem.at[lax.rem(to, 2)], recv_sem=recv_sem.at[0],
            device_id=(p, to), device_id_type=MESH,
        )

    def wait_all(ref, sem):
        pltpu.make_async_copy(ref, ref, sem).wait()

    def data_copy(p, slot):
        return pltpu.make_async_remote_copy(
            src_ref=data, dst_ref=data_in.at[slot],
            send_sem=data_send_sem.at[0], recv_sem=data_recv_sem.at[0],
            device_id=(q * rows + p, core), device_id_type=MESH,
        )

    def p_copy(p, slot):
        return pltpu.make_async_remote_copy(
            src_ref=out_p.at[p], dst_ref=in_p.at[slot],
            send_sem=p_send_sem.at[0], recv_sem=p_recv_sem.at[0],
            device_id=(q * rows + p, core), device_id_type=MESH,
        )

    def w_copy(p, slot):
        return pltpu.make_async_remote_copy(
            src_ref=out_w.at[p], dst_ref=in_w.at[slot],
            send_sem=w_send_sem.at[0], recv_sem=w_recv_sem.at[0],
            device_id=(q * rows + p, core), device_id_type=MESH,
        )

    def root_data_copy(slot):
        return pltpu.make_async_remote_copy(
            src_ref=data, dst_ref=root_data.at[slot],
            send_sem=root_send_sem.at[0], recv_sem=root_data_sem.at[0],
            device_id=(0, core), device_id_type=MESH,
        )

    def root_copy(slot):
        return pltpu.make_async_remote_copy(
            src_ref=out_r, dst_ref=root_in.at[slot],
            send_sem=root_send_sem.at[1], recv_sem=root_recv_sem.at[0],
            device_id=(0, core), device_id_type=MESH,
        )

    def back_copy(p, slot):
        return pltpu.make_async_remote_copy(
            src_ref=back.at[p], dst_ref=home.at[slot],
            send_sem=back_send_sem.at[0], recv_sem=back_recv_sem.at[0],
            device_id=(p * rows + z, core), device_id_type=MESH,
        )

    @pl.when(odd)
    def _():
        for load in loads[:4]:
            load.wait()
        wide = lambda x: jnp.concatenate([x] * 4, 1)
        cl = wide(cl_ref[...])
        code = jnp.where(
            wide(valid_ref[...]) > 0, (wide(pilot_ref[...]) * 16 + (cl & 15)).astype(F32) + 1.0, 0.0
        )
        owner = (cl >> 4) - lax.broadcasted_iota(jnp.int32, (16, 128), 1) // 32
        slots = []
        for a in range(4):
            part = cov_ref[:, 128 * a : 128 * a + 128]
            turned = jnp.concatenate([part] * 4, 0).T
            slots += [turned[32 * j : 32 * j + 32] for j in range(4)]
        row8 = lax.broadcasted_iota(jnp.int32, (8, 128), 0)
        for t in range(n // 4):
            tiles = [jnp.zeros((8, 128), F32)] * 4
            mark = jnp.zeros((8, 128), F32)
            for c in range(16):
                mine = jnp.broadcast_to(owner[c : c + 1], (8, 128)) == 4 * t
                tiles = [jnp.where(mine, slots[c][8 * v : 8 * v + 8], tiles[v]) for v in range(4)]
                mark = jnp.where(mine, jnp.broadcast_to(code[c : c + 1], (8, 128)), mark)
            first = jnp.broadcast_to(tiles[0][0:1], (8, 128))
            second = jnp.broadcast_to(tiles[0][5:6], (8, 128))
            tiles[1] = jnp.where(row8 == 1, first, jnp.where(row8 == 6, second, tiles[1]))
            tiles[3] = jnp.where(row8 == 1, mark, tiles[3])
            tiles = [jnp.where(row8 < 3, pltpu.roll(x, 7, 0), pltpu.roll(x, 5, 0)) for x in tiles]
            for j, tile in enumerate(lane_groups(tiles)):
                send[4 * t + j] = tile
        pl.semaphore_wait(barrier, n)

        @pl.loop(1, n)
        def _(d):
            slot_copy(me ^ (n - d), me, core).start()

        recv[me] = send[me]

    extra = jnp.logical_and(far, z > 0)

    @pl.when(jnp.logical_and(even, extra))
    def _():
        pl.semaphore_wait(barrier, rows + 3)

    @pl.when(jnp.logical_and(even, jnp.logical_not(extra)))
    def _():
        pl.semaphore_wait(barrier, rows + 2)

    wait_all(data_in.at[0:2], load_sem.at[4])
    turned = jnp.concatenate([rd_ref[:, f, :] for f in range(8)], 0).T.reshape(16, 8, 128)
    for f, tile in enumerate(block_transpose([turned[:, i, :] for i in range(8)])):
        data[:, f, :] = tile

    @pl.loop(1, rows)
    def _(d):
        data_copy(lax.rem(z + d, rows), z).start()

    @pl.when(far)
    def _():
        root_data_copy(z).start()

    turned = jnp.concatenate([rp_ref[:, f, :] for f in range(8)], 0).T
    for half in range(2):
        tiles = [turned[8 * (8 * half + t) : 8 * (8 * half + t) + 8] for t in range(8)]
        for f, tile in enumerate(block_transpose(tiles)):
            obs[f, :, 128 * half : 128 * half + 128] = tile
    observed = jnp.concatenate([obs[:, i, :] for i in range(8)], 0)
    observed = jnp.concatenate(split(observed, 3), 0)

    @pl.when(odd)
    def _():
        wait_all(recv.at[0 : n - 1, 0:5], recv_sem.at[0])
        pltpu.make_async_remote_copy(
            src_ref=recv.at[:, 0:5], dst_ref=recv.at[:, 0:5],
            send_sem=send_sem.at[0], recv_sem=recv_sem.at[0],
            device_id=(me, pair), device_id_type=MESH,
        ).start()

    @pl.when(even)
    def _():
        wait_all(recv.at[:, 0:5], recv_sem.at[0])

    row32 = lax.broadcasted_iota(jnp.int32, (32, 128), 0)
    codes, matrices = [], []
    for e in range(sets):
        for j in range(4):
            tiles = lane_groups([recv[h * rows + 4 * e + j] for h in range(4)])
            for v, tile in enumerate(tiles):
                trans[e, j, 8 * v : 8 * v + 5] = tile[0:5]
            codes.append(tiles[3][0:1])
            matrices.append(jnp.where(row32 == CODE, 0.0, trans[e, j]))
    codes = jnp.concatenate(codes, 1) - 1.0
    matrices = jnp.concatenate(matrices, 1)
    width = 128 * groups
    bins = lax.broadcasted_iota(jnp.int32, (256, width), 0).astype(F32)
    choose = jnp.where(bins == codes, 1.0, 0.0).astype(BF16)
    places = jnp.where(codes >= 0.0, codes - 16.0 * jnp.floor(codes * 0.0625), -1.0)
    ap_rows = (lax.broadcasted_iota(jnp.int32, (128, width), 0) & 15).astype(F32)
    pick = jnp.where(ap_rows == places, 1.0, 0.0).astype(BF16)
    for g in range(groups):
        out_p[g] = jnp.broadcast_to(places[:, 128 * g : 128 * g + 128], (8, 128))

        @pl.when(z != g)
        def _():
            p_copy(g, z).start()

    if sets == 1:
        rest = jnp.zeros((124, 128), F32)
        column = jnp.concatenate([codes[:, 128 * j : 128 * j + 128] for j in range(4)] + [rest], 0).T
        column_places = jnp.where(column >= 0.0, column - 16.0 * jnp.floor(column * 0.0625), -1.0)

        def alike(x, y):
            blocks = [jnp.where(x[:, j : j + 1] == y, 1.0, 0.0).astype(BF16) for j in range(4)]
            return jnp.concatenate(blocks, 0)

        slot_psi = dot_split(matrices, alike(column, codes), 3)
    else:
        slot_psi = dot_split(dot_split(matrices, choose, 3, True), choose, 3)
    slot_obs = dot(observed, choose)
    slot_obs = slot_obs[0:64] + slot_obs[64:128] + slot_obs[128:192]

    estimates, outers = [], []
    for e in range(sets):
        for j in range(4):
            g = 4 * e + j
            pinv[j] = slot_psi[:, 128 * g : 128 * g + 128]
        psi = {(i, i): (pinv[:, DIAGONAL[i], :] + 1.0, None) for i in range(4)}
        psi.update({p: (pinv[:, REAL[p], :], pinv[:, IMAG[p], :]) for p in PAIRS})
        pi = hermitian_inverse(psi)
        r = {(i, i): (trans[e, :, DIAGONAL[i], :], None) for i in range(4)}
        for p in PAIRS:
            r[p] = (trans[e, :, REAL[p], :], trans[e, :, IMAG[p], :])
        w = {}
        for i in range(4):
            for k in range(4):
                acc = None
                for l in range(4):
                    acc = add_products(acc, get(r, i, l), get(pi, l, k))
                w[i, k] = acc
        err = {}
        for i, k in ENTRIES:
            acc = None
            for l in range(4):
                acc = add_products(acc, w[i, l], get(r, l, k))
            re = r[i, k][0] - acc[0]
            err[i, k] = (re, None) if i == k else (re, r[i, k][1] - acc[1])
        for j in range(4):
            g = 4 * e + j
            cols = slice(128 * g, 128 * g + 128)
            y = [(slot_obs[8 * i : 8 * i + 8, cols], slot_obs[32 + 8 * i : 40 + 8 * i, cols]) for i in range(4)]
            h = []
            for i in range(4):
                acc = None
                for k in range(4):
                    wr, wi = w[i, k]
                    acc = add_products(acc, (wr[j : j + 1], wi[j : j + 1]), y[k])
                h.append(acc)
            estimates.append(h)
            out = []
            for i in range(4):
                out.append(h[i][0] * h[i][0] + h[i][1] * h[i][1] + err[i, i][0][j : j + 1])
            for i, k in PAIRS:
                out.append(h[i][0] * h[k][0] + h[i][1] * h[k][1] + err[i, k][0][j : j + 1])
                out.append(h[i][1] * h[k][0] - h[i][0] * h[k][1] + err[i, k][1][j : j + 1])
            outers.append(jnp.concatenate(out, 0))
    outers = jnp.concatenate(outers, 1)
    if sets == 1:
        slot_sum = dot_split(outers, alike(column_places, places), 3)
    else:
        summed = dot_split(outers, pick, 3, True)
        own_f = lax.broadcasted_iota(jnp.int32, (8, 128), 1) // 16 == lax.broadcasted_iota(jnp.int32, (8, 128), 0)
        comps = [
            jnp.sum(jnp.where(own_f, summed[8 * x : 8 * x + 8], 0.0), 0, keepdims=True) for x in range(16)
        ]
        masked = jnp.concatenate([jnp.where(own_f, c, 0.0) for c in comps], 0)
        slot_sum = dot_split(masked, pick, 3)
    for g in range(groups):
        cols = slice(128 * g, 128 * g + 128)
        h = estimates[g]
        parts = [slot_sum[8 * x : 8 * x + 8, cols] for x in range(16)]
        gs = hermitian_inverse(from_parts([c + 1.0 if x < 4 else c for x, c in enumerate(parts)]))
        power = None
        for i in range(4):
            acc = None
            for k in range(4):
                acc = add_products(acc, get(gs, i, k), h[k])
            out_w[g, 8 * i : 8 * i + 8] = acc[0]
            out_w[g, 32 + 8 * i : 40 + 8 * i] = acc[1]
            term = h[i][0] * acc[0] + h[i][1] * acc[1]
            power = term if power is None else power + term
        out_w[g, 64:72] = power

        if g == 0:
            @pl.when(far)
            def _():
                quarter = lax.broadcasted_iota(jnp.int32, (8, 128), 1) // 32
                for m in range(2):
                    packed = out_w[0, 32 * m : 32 * m + 8]
                    for j in range(1, 4):
                        at = 32 * m + 8 * j
                        packed = jnp.where(quarter == j, pltpu.roll(out_w[0, at : at + 8], 32 * j, 1), packed)
                    out_r[8 * m : 8 * m + 8] = packed
                out_r[16:24] = out_w[0, 64:72]
                root_copy(z).start()

        @pl.when(z != g)
        def _():
            w_copy(g, z).start()

    row16 = lax.broadcasted_iota(jnp.int32, (16, 128), 0).astype(F32)
    in_p[z] = out_p[z]
    in_w[z] = out_w[z]
    for k in range(rows):
        p = z ^ k
        if k == 1:
            wait_all(data_in.at[0 : rows - 1], data_recv_sem.at[0])
            wait_all(in_p.at[0 : rows - 1], p_recv_sem.at[0])
        place = in_p[p]
        hot = jnp.where(row16 == jnp.concatenate([place, place], 0), 1.0, 0.0).astype(BF16)
        for i in range(8):
            for half in range(2):
                at = 128 * half + 16 * i
                ones[k % 2, at : at + 16, 128 * i : 128 * i + 128] = hot
        source = (data[...] if k == 0 else data_in[p]).reshape(128, 128)
        left = jnp.concatenate(split(source, 2), 1)
        for i in range(4):
            cols = slice(256 * i, 256 * i + 256)
            wide_out = dot(left, ones[k % 2, :, cols])
            gathered[k, 2 * i] = wide_out[:, :128].reshape(16, 8, 128)
            gathered[k, 2 * i + 1] = wide_out[:, 128:].reshape(16, 8, 128)

    sums = [None] * 32
    power = None
    for k in range(rows):
        p = z ^ k
        if k == 1:
            wait_all(in_w.at[0 : rows - 1], w_recv_sem.at[0])
        u = [in_w[p, 8 * i : 8 * i + 8] for i in range(8)]
        part = in_w[p, 64:72]
        power = part if power is None else power + part
        for s in range(16):
            d = [gathered[k, i, s] for i in range(8)]
            re = im = None
            for i in range(4):
                x = u[i] * d[i] + u[i + 4] * d[i + 4]
                y = u[i] * d[i + 4] - u[i + 4] * d[i]
                re = x if re is None else re + x
                im = y if im is None else im + y
            sums[2 * s] = re if k == 0 else sums[2 * s] + re
            sums[2 * s + 1] = im if k == 0 else sums[2 * s + 1] + im
    for s in range(32):
        held[s] = sums[s]
    for half in range(2):
        tile = jnp.concatenate([held[:, 4 * half + f, :] for f in range(4)], 0).T.reshape(4, 4, 8, 128)
        for j in range(4):
            back[:, 2 * j + half] = tile[:, j]
    turned = jnp.concatenate([power, jnp.zeros((120, 128), F32)], 0).T.reshape(4, 4, 8, 128)
    gains = turned[:, 0].reshape(32, 128)
    for j in range(1, 4):
        gains = gains + pltpu.roll(turned[:, j].reshape(32, 128), 8 * j, 1)
    back[:, 8] = gains.reshape(4, 8, 128)

    to_root = lambda p: jnp.logical_and(p == 0, jnp.logical_and(z == 0, far))
    for p in range(4):
        here = jnp.logical_or(q == p, to_root(p))

        @pl.when(jnp.logical_not(here))
        def _():
            back_copy(p, q).start()

    @pl.when(root)
    def _():
        for load in loads[:2]:
            load.wait()
        cl = jnp.concatenate([cl_ref[...]] * 4, 1)
        valid = jnp.concatenate([valid_ref[...]] * 4, 1)
        mark = jnp.where(valid > 0, (cl & 15).astype(F32) + 1.0, 0.0)
        owner = cl >> 4
        row = lax.broadcasted_iota(jnp.int32, (128, 128), 0)
        quarter = lax.broadcasted_iota(jnp.int32, (128, 128), 1) // 32
        base = jnp.where(((row >> 4) & 3) == quarter, ((row & 15) + 1).astype(F32), -1.0)
        for p in range(rows):
            place = jnp.sum(jnp.where(owner == 3 * rows + p, mark, 0.0), 0, keepdims=True)
            hot = jnp.where(base == place, 1.0, 0.0)
            hot = jnp.concatenate(
                [jnp.where(row < 64, hot, 0.0), jnp.where(row < 64, 0.0, hot)], 1
            ).astype(BF16)
            if p == 0:
                wait_all(root_data, root_data_sem.at[0])
            left = jnp.concatenate(split(root_data[p].reshape(128, 128), 2), 1)
            both = dot(left, jnp.concatenate([hot, hot], 0))
            for m in range(2):
                root_held[p, m] = both[:, 128 * m : 128 * m + 128].reshape(16, 8, 128)
        sums = [None] * 32
        power = None
        for p in range(rows):
            if p == 0:
                wait_all(root_in, root_recv_sem.at[0])
            u, v, part = (root_in[p, 8 * m : 8 * m + 8] for m in range(3))
            power = part if p == 0 else power + part
            for s in range(16):
                x, y = root_held[p, 0, s], root_held[p, 1, s]
                re, im = u * x + v * y, u * y - v * x
                sums[2 * s] = re if p == 0 else sums[2 * s] + re
                sums[2 * s + 1] = im if p == 0 else sums[2 * s + 1] + im
        for s in range(32):
            x = sums[s] + pltpu.roll(sums[s], 64, 1)
            held[s] = x + pltpu.roll(x, 32, 1)
        for half in range(2):
            tile = jnp.concatenate([held[:, 4 * half + f, :] for f in range(4)], 0).T
            for j in range(4):
                home[3, 2 * j + half] = tile[8 * j : 8 * j + 8]
        turned = jnp.concatenate([power, jnp.zeros((120, 128), F32)], 0).T
        gains = turned[0:8]
        for j in range(1, 4):
            gains = gains + pltpu.roll(turned[8 * j : 8 * j + 8], 8 * j, 1)
        home[3, 8] = gains

    home[q] = back[q]

    @pl.when(jnp.logical_not(root))
    def _():
        wait_all(home.at[0:3], back_recv_sem.at[0])

    @pl.when(root)
    def _():
        wait_all(home.at[0:2], back_recv_sem.at[0])

    @pl.when(odd)
    def _():
        wait_all(send.at[:, 0:5], send_sem.at[0])
        wait_all(send.at[0 : n - 1, 0:5], send_sem.at[1])

    wait_all(data_in.at[0 : rows - 1], data_send_sem.at[0])
    wait_all(in_p.at[0 : rows - 1], p_send_sem.at[0])
    wait_all(in_w.at[0 : rows - 1], w_send_sem.at[0])

    @pl.when(to_root(0))
    def _():
        wait_all(back.at[0:2], back_send_sem.at[0])

    @pl.when(jnp.logical_not(to_root(0)))
    def _():
        wait_all(back.at[0:3], back_send_sem.at[0])

    @pl.when(far)
    def _():
        root_data_copy(z).wait_send()
        root_copy(z).wait_send()


def finish(home, sym_ref, gain_ref):
    total = (home[0] + home[1]) + (home[2] + home[3])
    for j in range(4):
        for f in range(8):
            tile = total[2 * j + f // 4]
            sym_ref[8 * j : 8 * j + 8, f, :] = tile[:, 32 * (f % 4) : 32 * (f % 4) + 32]
    gains = jnp.concatenate([total[8], jnp.zeros((120, 128), F32)], 0).T
    gain_ref[...] = jnp.concatenate([gains[8 * j : 8 * j + 8, 0:8] for j in range(4)], 1)


def body(n, covariances, clusters, cluster_valid, pilots, received_pilot, received_data):
    vmem = pl.BlockSpec(memory_space=pltpu.VMEM)
    rows = n // 4
    home = pl.pallas_call(
        functools.partial(kernel, n),
        out_shape=pltpu.VMEM((4, 9, 8, 128), F32),
        in_specs=[pl.BlockSpec(memory_space=pltpu.HBM)] * 6,
        out_specs=vmem,
        scratch_shapes=[
            pltpu.VMEM((32, 512), F32),
            pltpu.VMEM((16, 32), jnp.int32),
            pltpu.VMEM((16, 32), jnp.int32),
            pltpu.VMEM((1, 32), jnp.int32),
            pltpu.VMEM((16, 8, 128), F32),
            pltpu.VMEM((16, 8, 128), F32),
            pltpu.VMEM((n, 8, 128), F32),
            pltpu.VMEM((n, 8, 128), F32),
            pltpu.VMEM((n // 16, 4, 32, 128), F32),
            pltpu.VMEM((4, 32, 128), F32),
            pltpu.VMEM((8, 8, 256), F32),
            pltpu.VMEM((16, 8, 128), F32),
            pltpu.VMEM((rows, 16, 8, 128), F32),
            pltpu.VMEM((2, 256, 1024), BF16),
            pltpu.VMEM((rows, 8, 16, 8, 128), F32),
            pltpu.VMEM((32, 8, 128), F32),
            pltpu.VMEM((rows, 8, 128), F32),
            pltpu.VMEM((rows, 8, 128), F32),
            pltpu.VMEM((rows, 72, 128), F32),
            pltpu.VMEM((rows, 72, 128), F32),
            pltpu.VMEM((4, 9, 8, 128), F32),
            pltpu.VMEM((rows, 16, 8, 128), F32),
            pltpu.VMEM((rows, 2, 16, 8, 128), F32),
            pltpu.VMEM((24, 128), F32),
            pltpu.VMEM((rows, 24, 128), F32),
            pltpu.SemaphoreType.DMA((5,)),
            pltpu.SemaphoreType.DMA((2,)),
            pltpu.SemaphoreType.DMA((1,)),
            pltpu.SemaphoreType.DMA((1,)),
            pltpu.SemaphoreType.DMA((1,)),
            pltpu.SemaphoreType.DMA((1,)),
            pltpu.SemaphoreType.DMA((1,)),
            pltpu.SemaphoreType.DMA((1,)),
            pltpu.SemaphoreType.DMA((1,)),
            pltpu.SemaphoreType.DMA((1,)),
            pltpu.SemaphoreType.DMA((1,)),
            pltpu.SemaphoreType.DMA((2,)),
            pltpu.SemaphoreType.DMA((1,)),
            pltpu.SemaphoreType.DMA((1,)),
        ],
        compiler_params=pltpu.CompilerParams(
            collective_id=0, has_side_effects=True, vmem_limit_bytes=65000 * 1024
        ),
    )(covariances, clusters.T, cluster_valid.T, pilots.reshape(1, -1), received_pilot, received_data)
    symbols, gain = pl.pallas_call(
        finish,
        out_shape=(jax.ShapeDtypeStruct((32, 8, 32), F32), jax.ShapeDtypeStruct((8, 32), F32)),
        in_specs=[vmem],
        out_specs=(vmem, vmem),
    )(pltpu.with_memory_space_constraint(home, pltpu.VMEM))
    return symbols, gain.T


def solution(mesh):
    placed = (
        P("ap", None),
        P("ap", None),
        P("ap", None),
        P("ap"),
        P("ap", "sc", None),
        P("ap", "sc", None),
    )
    return jax.shard_map(
        functools.partial(body, mesh.shape["ap"]),
        mesh=mesh,
        in_specs=placed,
        out_specs=(P("ap", "sc", None), P("ap", "sc")),
        check_vma=False,
    )
```
